128 devices in a mesh: ctx: 8 (over z_hi, y), tp: 16 (over x, z_lo, core).
Axes of the slice: x: 4, y: 4, z: 4 (z_hi: 2, z_lo: 2; z = z_hi * 2 + z_lo), core: 2. Of those that a mesh axis runs over, the one named last changes fastest.
Arguments:
- context: bfloat16 [1536, 8192], P('ctx', 'tp'), may hold values from -6 to 6
- out_proj: bfloat16 [8192, 4096], P('tp'), may hold values from -0.0625 to 0.0625
- residual: bfloat16 [1536, 4096], P(('ctx', 'tp')), may hold values from -44 to 44
- norm_gain: float32 [4096], replicated, may hold values from 0.1 to 1.9
- gate_weight: bfloat16 [32, 1536, 4096], P('tp', 'ctx'), may hold values from -0.09375 to 0.09375
- up_weight: bfloat16 [32, 1536, 4096], P('tp', 'ctx'), may hold values from -0.09375 to 0.09375
- down_weight: bfloat16 [32, 1536, 4096], P('tp', 'ctx'), may hold values from -0.15625 to 0.15625
- expert_ids: int32 [1536, 8], P(('ctx', 'tp')), may hold values from 0 to 31, all different within a row; in each aligned block of 12 rows (0 to 11, 12 to 23, ...) at most 4 rows name the same one
- gate_codes: int32 [1536, 8], P(('ctx', 'tp')), may hold values from 1 to 32
- cotangent: bfloat16 [1536, 4096], P(('ctx', 'tp')), may hold values from -6 to 6
Outputs:
- output: bfloat16 [1536, 4096], P(('ctx', 'tp'))
- residual_grad: bfloat16 [1536, 4096], P(('ctx', 'tp'))
- context_grad: bfloat16 [1536, 8192], P('ctx', 'tp')
- gate_weight_grad: bfloat16 [32, 1536, 4096], P('tp', 'ctx')
- up_weight_grad: bfloat16 [32, 1536, 4096], P('tp', 'ctx')
- down_weight_grad: bfloat16 [32, 1536, 4096], P('tp', 'ctx')
The draws below stay inside these ranges and needn't reach their ends.
Inputs may be any that keep to these rules, and one draw needn't show every extreme that they name: `expert_ids`: each token's 8 ids differ. Among the 12 tokens of one device no id occurs more than 4 times, and on some device some id occurs exactly 4 times.
All inputs are finite; a program needn't handle non-finite values.
Results may differ from the reference program's by a relative error of at most 0.025.
Values may be sent and summed in bfloat16 or wider, within the bound.
No kernel may reach another device: no remote copies, remote signals or barrier semaphores. Data moves between devices by JAX's collectives and lax.ppermute only.
A program may use at most 192 MiB of HBM per device.

```python
import math
import jax
import jax.numpy as jnp
import numpy as np
from jax import lax

D = 4096
FF = 1536
AW = 8192
TOPK = 8
TOK_DEV = 12
TOKENS = 1536
EXPERTS = 32
CAP = 4
N_CTX = 8
N_TP = 16


def draw_residual(key, part):
    first_key, second_key, third_key = jax.random.split(key, 3)
    base_values = jnp.clip(jax.random.normal(first_key, (TOKENS, D), jnp.float32), -4.0, 4.0)
    row_scale = jnp.exp(jax.random.uniform(second_key, (TOKENS, 1), jnp.float32, math.log(0.3), math.log(3.3)))
    col_scale = jnp.exp(jax.random.uniform(third_key, (1, D), jnp.float32, math.log(0.3), math.log(3.3)))
    return (base_values * row_scale * col_scale).astype(jnp.bfloat16)


def plant(array, rng, smallest, high):
    longest = array.shape.index(max(array.shape))
    spots = []
    for shift in (0, 1):
        where = [jax.random.randint(jax.random.fold_in(rng, axis), (), 0, length) for axis, length in enumerate(array.shape)]
        where[longest] = (where[longest] + shift) % array.shape[longest]
        spots.append(tuple(where))
    return array.at[spots[0]].set(smallest).at[spots[1]].set(high)


def strengthened(values, stream_key, source, target, shards_of, factor):
    def block_of(dim):
        return (jnp.arange(values.shape[dim]) // (values.shape[dim] // shards_of)).reshape((-1,) + (1,) * (values.ndim - 1 - dim))

    first = jax.random.permutation(stream_key, shards_of)[block_of(target)]
    other_side = (block_of(target) + shards_of // 2) % shards_of
    return jnp.where((block_of(source) == first) | (block_of(source) == other_side), factor * values, values)


def steps_of(rng, extent, cuts, least, largest):
    level = 1.0
    for position, parts in cuts:
        steps = jax.random.uniform(jax.random.fold_in(jax.random.fold_in(rng, 6), position), (parts,), jnp.float32, least / len(cuts), largest / len(cuts))
        level = level * jnp.repeat(jnp.exp(steps), extent[position] // parts).reshape((-1,) + (1,) * (len(extent) - 1 - position))
    return level


def shared_out(rng, own, number, rows, number_of, top, reach, lean):
    order = jax.random.permutation(rng, number_of)
    crowded, usual = shares(number_of, rows * top, reach, lean, True), shares(number_of, rows * top, reach, lean, False)
    places = jnp.arange(number_of)

    def named(sizes, rotation):
        used = int((sizes > 0).sum())
        fixed = max(1, used // 4)
        moved = fixed + (places - fixed + rotation * (used - fixed)) % max(1, number_of - fixed)
        return jnp.zeros((number_of,), jnp.int32).at[order[jnp.where(places < fixed, places, moved)]].set(jnp.asarray(sizes, jnp.int32))

    sizes = jnp.where(number % 4 == 0, named(crowded, number // 4), named(usual, number - number // 4 - 1))
    mixed = jax.random.permutation(jax.random.fold_in(own, 3), number_of)
    donor, taker = mixed[0:number_of // 2 * 2:2], mixed[1:number_of // 2 * 2:2]
    slack = jnp.minimum(sizes[donor] - 1, reach - sizes[taker]) // 2
    slack = jnp.where((donor == order[0]) | (taker == order[0]) | (sizes[taker] == 0), 0, jnp.maximum(slack, 0))
    moved = jax.random.randint(jax.random.fold_in(own, 4), (number_of // 2,), 0, 1 << 20) % (slack + 1)
    sizes = sizes.at[donor].add(-moved).at[taker].add(moved)
    members = jnp.searchsorted(jnp.cumsum(sizes), jnp.arange(rows * top), side="right").astype(jnp.int32)
    table = members.reshape(top, rows).T
    table = table[jax.random.permutation(jax.random.fold_in(own, 1), rows)]
    rotation = jax.random.randint(jax.random.fold_in(own, 2), (rows, 1), 0, top)
    return jnp.take_along_axis(table, (jnp.arange(top)[None, :] + rotation) % top, axis=1)


def shares(amount, total, limit, lean, full):
    loads = [(1 << 20) // math.isqrt(rank ** lean) + 1 for rank in range(1, amount + 1)]
    largest = limit if full else min(limit, max(-(-total // amount), total * loads[0] // sum(loads)))
    least = 1 if total - largest >= amount - 1 else 0
    holding, surplus = [largest] + [least] * (amount - 1), total - largest - least * (amount - 1)
    while surplus > 0:
        free = [i for i in range(1, amount) if holding[i] < largest] or [i for i in range(1, amount) if holding[i] < limit]
        pool, left = sum([loads[i] for i in free]), surplus
        for i in free:
            addition = min(limit - holding[i], max(1, left * loads[i] // pool), surplus)
            holding[i] = holding[i] + addition
            surplus = surplus - addition
    return np.array(holding)


def bell_draw(own_key, shape, deviation, limit, cuts=(), held_as=jnp.bfloat16):
    factor_of = steps_of(own_key, shape, cuts, -0.22, 0.18) if cuts else 1.0
    result = jax.random.normal(own_key, shape, jnp.float32) * deviation * factor_of
    return jnp.minimum(jnp.maximum(result, -limit), limit).astype(held_as)


def noise_with(own_key, dims, width, limit, cuts, heavy, kind=jnp.bfloat16):
    drawn = width * jax.random.normal(own_key, dims, jnp.float32)
    if cuts:
        drawn = drawn * steps_of(own_key, dims, cuts, -0.22, 0.18)
    return jnp.clip(strengthened(drawn, jax.random.fold_in(own_key, 3), *heavy), -limit, limit).astype(kind)


def setup_inputs(seed: int = 0) -> dict:
    keys = jax.random.split(jax.random.key(seed), 11)
    context = noise_with(keys[0], (TOKENS, AW), 1.0, 6.0, ((0, 8), (1, 16)), (1, 0, 16, 2.0))
    out_proj = bell_draw(keys[1], (AW, D), AW ** -0.5, 0.0625, ((0, 16),))
    residual = draw_residual(jax.random.fold_in(keys[10], 71), 0)
    norm_gain = jnp.clip(1.0 + 0.18 * jax.random.normal(keys[3], (D,), jnp.float32), 0.1, 1.9)
    gate_weight = bell_draw(keys[4], (EXPERTS, FF, D), D ** -0.5, 0.09375, ((0, 16), (1, 8)))
    up_weight = bell_draw(keys[5], (EXPERTS, FF, D), D ** -0.5, 0.09375, ((0, 16), (1, 8)))
    down_weight = bell_draw(keys[6], (EXPERTS, FF, D), FF ** -0.5, 0.15625, ((0, 16), (1, 8)))
    expert_ids_keys = jax.random.split(jax.random.fold_in(keys[7], 1), TOKENS // TOK_DEV)
    expert_ids_turns = jax.random.permutation(jax.random.fold_in(keys[7], 3), TOKENS // TOK_DEV)
    expert_ids = jax.vmap(lambda own, number: shared_out(jax.random.fold_in(keys[7], 2), own, number, TOK_DEV, EXPERTS, TOPK, CAP, 2))(expert_ids_keys, expert_ids_turns).reshape((TOKENS, TOPK))
    gate_codes = plant(jax.random.randint(keys[8], (TOKENS, TOPK), 1, 33), jax.random.fold_in(keys[8], 1), 1, 32).astype(jnp.int32)
    cotangent = bell_draw(keys[9], (TOKENS, D), 1.0, 6.0, ((0, 128),))
    return dict(context=context, out_proj=out_proj, residual=residual, norm_gain=norm_gain, gate_weight=gate_weight, up_weight=up_weight, down_weight=down_weight, expert_ids=expert_ids, gate_codes=gate_codes, cotangent=cotangent)


epsilon = 1e-06

def slot_positions(expert_ids):
    devices = N_CTX * N_TP
    blocks = expert_ids.reshape(devices, TOK_DEV * TOPK)
    onehot = (blocks[:, :, None] == jnp.arange(EXPERTS, dtype=jnp.int32)[None, None, :]).astype(jnp.int32)
    ranking = lax.optimization_barrier(jnp.sum(jnp.cumsum(onehot, axis=1) * onehot, axis=2)) - 1
    owners = jnp.arange(devices, dtype=jnp.int32)[:, None] * CAP + ranking
    return owners.reshape(TOKENS, TOPK).astype(jnp.int32)

def expert_pass(packed):
    slot_rows, slot_grads, gate_matrix, up_matrix, down_matrix = packed
    gate_act = jnp.dot(slot_rows, gate_matrix.T, preferred_element_type=jnp.float32)
    up_act = jnp.dot(slot_rows, up_matrix.T, preferred_element_type=jnp.float32)
    sigmoid_gate = jax.nn.sigmoid(gate_act)
    hidden = (gate_act * sigmoid_gate * up_act).astype(jnp.bfloat16)
    hidden_grad = jnp.dot(slot_grads, down_matrix.T, preferred_element_type=jnp.float32)
    up_grad = (hidden_grad * gate_act * sigmoid_gate).astype(jnp.bfloat16)
    gate_grad = (hidden_grad * up_act * sigmoid_gate * (1.0 + gate_act * (1.0 - sigmoid_gate))).astype(jnp.bfloat16)
    slice_width = FF // N_CTX
    out_total = jnp.zeros((slot_rows.shape[0], D), jnp.float32)
    back_total = jnp.zeros((slot_rows.shape[0], D), jnp.float32)
    for slice_index in range(N_CTX):
        low_edge = slice_index * slice_width
        high_edge = low_edge + slice_width
        out_piece = jnp.dot(hidden[:, low_edge:high_edge], down_matrix[low_edge:high_edge], preferred_element_type=jnp.float32)
        out_total = out_total + lax.optimization_barrier(out_piece.astype(jnp.bfloat16)).astype(jnp.float32)
        back_term = jnp.dot(gate_grad[:, low_edge:high_edge], gate_matrix[low_edge:high_edge], preferred_element_type=jnp.float32)
        back_term = back_term + jnp.dot(up_grad[:, low_edge:high_edge], up_matrix[low_edge:high_edge], preferred_element_type=jnp.float32)
        back_total = back_total + lax.optimization_barrier(back_term.astype(jnp.bfloat16)).astype(jnp.float32)
    gate_wgrad = jnp.dot(gate_grad.T, slot_rows, preferred_element_type=jnp.float32).astype(jnp.bfloat16)
    up_wgrad = jnp.dot(up_grad.T, slot_rows, preferred_element_type=jnp.float32).astype(jnp.bfloat16)
    down_wgrad = jnp.dot(hidden.T, slot_grads, preferred_element_type=jnp.float32).astype(jnp.bfloat16)
    return (out_total.astype(jnp.bfloat16), back_total.astype(jnp.bfloat16), gate_wgrad, up_wgrad, down_wgrad)

def reference(context, out_proj, residual, norm_gain, gate_weight, up_weight, down_weight, expert_ids, gate_codes, cotangent):
    attended = jnp.dot(context, out_proj, preferred_element_type=jnp.float32)
    stream = residual.astype(jnp.float32) + attended
    inverse = lax.rsqrt(lax.optimization_barrier(jnp.mean(stream * stream, axis=1, keepdims=True)) + epsilon)
    normed = (stream * inverse * norm_gain).astype(jnp.bfloat16)
    code_values = gate_codes.astype(jnp.float32)
    gate_values = code_values / lax.optimization_barrier(jnp.sum(code_values, axis=1, keepdims=True))
    slot_index = slot_positions(expert_ids)
    slot_total = N_CTX * N_TP * CAP
    flat_expert = expert_ids.reshape(-1).astype(jnp.int32)
    flat_slot = slot_index.reshape(-1).astype(jnp.int32)
    token_of = jnp.repeat(jnp.arange(TOKENS, dtype=jnp.int32), TOPK)
    expert_rows = jnp.zeros((EXPERTS, slot_total, D), jnp.bfloat16).at[flat_expert, flat_slot].set(normed[token_of])
    scaled = (gate_values.reshape(-1)[:, None] * cotangent.astype(jnp.float32)[token_of]).astype(jnp.bfloat16)
    expert_grads = jnp.zeros((EXPERTS, slot_total, D), jnp.bfloat16).at[flat_expert, flat_slot].set(scaled)
    results = lax.map(expert_pass, (expert_rows, expert_grads, gate_weight, up_weight, down_weight))
    expert_out, expert_back, gate_weight_grad, up_weight_grad, down_weight_grad = results
    picked_out = expert_out[flat_expert, flat_slot].astype(jnp.float32).reshape(TOKENS, TOPK, D)
    mixture = lax.optimization_barrier(jnp.sum(picked_out * gate_values[:, :, None], axis=1))
    output = (stream + mixture).astype(jnp.bfloat16)
    normed_grad = lax.optimization_barrier(jnp.sum(expert_back[flat_expert, flat_slot].astype(jnp.float32).reshape(TOKENS, TOPK, D), axis=1))
    scaled_grad = normed_grad * norm_gain
    inner_mean = lax.optimization_barrier(jnp.mean(scaled_grad * stream, axis=1, keepdims=True))
    stream_grad = cotangent.astype(jnp.float32) + inverse * scaled_grad - stream * inverse ** 3 * inner_mean
    residual_grad = stream_grad.astype(jnp.bfloat16)
    context_grad = jnp.dot(residual_grad, out_proj.T, preferred_element_type=jnp.float32).astype(jnp.bfloat16)
    return (output, residual_grad, context_grad, gate_weight_grad, up_weight_grad, down_weight_grad)
```

```python
import functools

import numpy as np
import jax
import jax.numpy as jnp
from jax import lax
from jax.experimental import pallas as pl
from jax.experimental.pallas import tpu as pltpu
from jax.sharding import Mesh, PartitionSpec as P

AXES = ("zh", "y", "x", "zl", "core")
CAP = 4
TOK = 12
EPSILON = 1e-06
BF16 = jnp.bfloat16
F32 = jnp.float32
VMEM_LIMIT = 50 * 1024 * 1024


def flat_index(z, y, x, core):
    return ((((z // 2) * 4 + y) * 4 + x) * 2 + z % 2) * 2 + core


def permutation(move):
    return [
        (flat_index(z, y, x, c), flat_index(*move(z, y, x, c)))
        for z in range(4)
        for y in range(4)
        for x in range(4)
        for c in range(2)
    ]


def shifted(axis, steps):
    def move(z, y, x, c):
        d = steps * (1 - 2 * c)
        if axis == "x":
            return z, y, (x + d) % 4, c
        if axis == "y":
            return z, (y + d) % 4, x, c
        return (z + d) % 4, y, x, c

    return permutation(move)


def tp_shifted(steps, flip):
    return permutation(lambda z, y, x, c: (z ^ flip, y, (x + steps * (1 - 2 * c)) % 4, c))


SWAP = permutation(lambda z, y, x, c: (z, y, x, 1 - c))
ORDERS = (("x", "y", "z"), ("y", "z", "x"), ("z", "x", "y"))


def send(v, pairs):
    return lax.ppermute(v, AXES, pairs)


def gather_part(part, order):
    a, b, c = order
    width = part.shape[-1]

    def around(v, axis):
        return [v] + [send(v, shifted(axis, d)) for d in (1, 2, 3)]

    one = jnp.stack(around(part, a))
    two = jnp.stack(around(one, b), axis=1 if a == "z" else 0)
    cur = two.reshape(128, width)
    planes = [cur]
    for _ in range(3):
        cur = send(cur, shifted(c, 1))
        planes.append(cur)
    return planes


def gather_all(parts):
    out = []
    for part, order in zip(parts, ORDERS):
        own = gather_part(part, order)
        out.append((own, [send(v, SWAP) for v in own]))
    return out


def scatter_all(own, sib):
    width = own.shape[-1]
    arrived = {j: send(sib[j], SWAP) for j in (1, 2, 3, 0)}
    sums = []
    for p, (a, b, c) in enumerate(ORDERS):
        t = None
        for j in (1, 2, 3, 0):
            v = own[j, p].astype(F32) + arrived[j][p].astype(F32)
            if t is not None:
                v = v + send(t, shifted(c, 1)).astype(F32)
            t = v.astype(BF16)

        def direct(t, axis, at):
            v = lax.index_in_dim(t, 0, at, False).astype(F32)
            for d in (1, 2, 3):
                v = v + send(lax.index_in_dim(t, d, at, False), shifted(axis, -d)).astype(F32)
            return v

        t = direct(t.reshape(4, 4, 8, width), b, 1 if a == "z" else 0).astype(BF16)
        sums.append(direct(t, a, 0))
    return sums


def pack(rows):
    half = rows.shape[1] // 2
    tail = rows[8:]
    return [rows[:8, :half], rows[:8, half:], jnp.concatenate([tail[:, :half], tail[:, half:]], axis=0)]


def unpack(parts):
    left, right, tail = parts
    return jnp.concatenate(
        [
            jnp.concatenate([left, right], axis=1),
            jnp.concatenate([tail[:4], tail[4:]], axis=1),
        ],
        axis=0,
    )


def row_sums(products):
    head = jnp.sum(products[0], axis=1, keepdims=True) + jnp.sum(products[1], axis=1, keepdims=True)
    tail = jnp.sum(products[2], axis=1, keepdims=True)
    return head, tail + jnp.concatenate([tail[4:], tail[:4]], axis=0)


def routing(meta, first_expert):
    ids = meta[:, :, :TOK].astype(F32)
    codes = meta[:, :, 16 : 16 + TOK].astype(F32)
    experts = (first_expert + jnp.arange(2)).astype(F32)
    hit = (ids[:, None] == experts[None, :, None, None]).astype(F32)
    has = jnp.sum(hit, axis=2)
    gate = jnp.sum(hit * codes[:, None], axis=2) / jnp.sum(codes, axis=1)[:, None]
    earlier = (np.arange(TOK)[:, None] < np.arange(TOK)[None, :]).astype(np.float32)
    rank = jnp.einsum("bet,tu->beu", has, earlier)
    place = has[:, :, None] * (rank[:, :, None] == jnp.arange(CAP, dtype=F32)[None, None, :, None])
    slot_gate = jnp.sum(place * gate[:, :, None], axis=3)
    place = place.reshape(8, 16, 2, CAP, TOK).transpose(0, 2, 1, 3, 4).reshape(8, 128, TOK)
    slot_gate = slot_gate.transpose(1, 0, 2).reshape(1024, 1)

    slot_block = (np.arange(128) % 64) // CAP
    col = np.arange(128)
    row = col % 8
    yx = col // 8
    xy = (yx % 4) * 4 + yx // 4

    def table(block_of, token_of):
        spread = (np.arange(TOK)[:, None] == token_of[None, :]).astype(np.float32)
        mask = (slot_block[:, None] == block_of[None, :]).astype(np.float32)
        return (jnp.einsum("gst,tc->gsc", place, spread) * mask).astype(BF16)

    head = table(yx, row)
    head_xy = table(xy, row)
    tail_left = table(yx, np.where(row < 4, 8 + row, -1))
    tail_right = table(yx, np.where(row < 4, -1, 4 + row))
    tables = jnp.stack([head, head_xy, tail_left, tail_right])
    return tables, slot_gate


def dot(a, b, ca, cb):
    return lax.dot_general(a, b, (((ca,), (cb,)), ((), ())), preferred_element_type=F32)


def place_rows(tables, planes, out_ref):
    for group in range(8):
        half, g = divmod(group, 4)
        zs, xs, ys = (planes[p * 8 + half * 4 : p * 8 + half * 4 + 4] for p in range(3))
        pick = pl.ds(g * 32, 32)
        tail = jnp.concatenate([ref[pick, :] for ref in ys], axis=0)
        right = jnp.concatenate([ref[pick, :] for ref in xs], axis=0)
        for lr, head in enumerate((zs[g][...], right)):
            rows = dot(tables[lr, group], head, 1, 0) + dot(tables[2 + lr, group], tail, 1, 0)
            rows = rows.astype(BF16)
            out_ref[lr, pl.ds(group * 64, 64), :] = rows[:64]
            out_ref[lr, pl.ds(512 + group * 64, 64), :] = rows[64:]


def grads_kernel(*refs):
    tables, planes = refs[0], refs[1:25]
    down = refs[25:27]
    rows, hidden_grad, total = refs[27:]
    step = pl.program_id(0)

    @pl.when(step == 0)
    def _():
        total[...] = jnp.zeros_like(total)

    place_rows(tables, planes, rows)
    for e in range(2):
        at = pl.ds(e * 512, 512)
        total[at, :] += dot(rows[0, at, :], down[0][e], 1, 1) + dot(rows[1, at, :], down[1][e], 1, 1)

    @pl.when(step == pl.num_programs(0) - 1)
    def _():
        hidden_grad[...] = total[...]


def rows_kernel(*refs):
    tables, planes = refs[0], refs[1:25]
    gate, up = refs[25:27], refs[27:29]
    hidden_grad, slot_gate = refs[29:31]
    rows, hidden, gate_grad, up_grad, gate_total, up_total = refs[31:]
    step = pl.program_id(0)

    @pl.when(step == 0)
    def _():
        gate_total[...] = jnp.zeros_like(gate_total)
        up_total[...] = jnp.zeros_like(up_total)

    place_rows(tables, planes, rows)
    for e in range(2):
        at = pl.ds(e * 512, 512)
        left, right = rows[0, at, :], rows[1, at, :]
        gate_total[at, :] += dot(left, gate[0][e], 1, 1) + dot(right, gate[1][e], 1, 1)
        up_total[at, :] += dot(left, up[0][e], 1, 1) + dot(right, up[1][e], 1, 1)

    @pl.when(step == pl.num_programs(0) - 1)
    def _():
        for i in range(8):
            at = pl.ds(i * 128, 128)
            gate_act, up_act = gate_total[at, :], up_total[at, :]
            scale = slot_gate[at, :]
            back = hidden_grad[at, :] * scale
            s = 1.0 / (1.0 + jnp.exp(-gate_act))
            silu = gate_act * s
            hidden[at, :] = (silu * up_act * scale).astype(BF16)
            up_grad[at, :] = (back * silu).astype(BF16)
            gate_grad[at, :] = (back * up_act * s * (1.0 + gate_act * (1.0 - s))).astype(BF16)


def combine_kernel(terms, *refs):
    tables = refs[0]
    acts = refs[1 : 1 + terms]
    weights = refs[1 + terms : 1 + 3 * terms]
    own, sib, slots = refs[1 + 3 * terms :]
    for lr in range(2):
        for e in range(2):
            at = pl.ds(e * 512, 512)
            value = dot(acts[0][at, :], weights[lr][e], 1, 0)
            for i in range(1, terms):
                value = value + dot(acts[i][at, :], weights[2 * i + lr][e], 1, 0)
            slots[lr, at, :] = value.astype(BF16)
    for group in range(8):
        half, g = divmod(group, 4)
        out = (own, sib)[half]
        left, right = (
            jnp.concatenate(
                [slots[lr, pl.ds(group * 64, 64), :], slots[lr, pl.ds(512 + group * 64, 64), :]], axis=0
            )
            for lr in range(2)
        )
        out[g, 0] = dot(tables[0, group], left, 1, 0).astype(BF16)
        head = dot(tables[1, group], right, 1, 0).astype(BF16)
        tail = (dot(tables[2, group], left, 1, 0) + dot(tables[3, group], right, 1, 0)).astype(BF16)
        for i in range(4):
            out[i, 1, pl.ds(g * 32, 32), :] = head[i * 32 : (i + 1) * 32]
            out[i, 2, pl.ds(g * 32, 32), :] = tail[i * 32 : (i + 1) * 32]


def weight_grads_kernel(rows, grads, hidden, gate_grad, up_grad, gate_out, up_out, down_out):
    for e in range(2):
        at = pl.ds(e * 512, 512)
        x = rows[0, at, :]
        gate_out[e] = dot(gate_grad[at, :], x, 0, 0).astype(BF16)
        up_out[e] = dot(up_grad[at, :], x, 0, 0).astype(BF16)
        down_out[e] = dot(hidden[at, :], grads[0, at, :], 0, 0).astype(BF16)


def whole(shape):
    return pl.BlockSpec(shape, lambda *_: (0,) * len(shape))


def params():
    return pltpu.CompilerParams(vmem_limit_bytes=VMEM_LIMIT)


def chunk_of(half):
    return min(512, half)


def flat_planes(planes):
    return [v for part in planes for half in part for v in half]


def weight_specs(weight, chunk, steps):
    shape = (weight.shape[0], weight.shape[1], chunk)
    return [
        pl.BlockSpec(shape, lambda n: (0, 0, n)),
        pl.BlockSpec(shape, lambda n, steps=steps: (0, 0, n + steps)),
    ]


def dispatch_grads(tables, planes, down):
    width, half = down.shape[1], down.shape[2] // 2
    chunk = chunk_of(half)
    steps = half // chunk
    return pl.pallas_call(
        grads_kernel,
        grid=(steps,),
        in_specs=[whole(tables.shape)]
        + [pl.BlockSpec((128, chunk), lambda n: (0, n))] * 24
        + weight_specs(down, chunk, steps),
        out_specs=[pl.BlockSpec((2, 1024, chunk), lambda n: (0, 0, n)), whole((1024, width))],
        out_shape=[
            jax.ShapeDtypeStruct((2, 1024, half), BF16),
            jax.ShapeDtypeStruct((1024, width), F32),
        ],
        scratch_shapes=[pltpu.VMEM((1024, width), F32)],
        compiler_params=params(),
        cost_estimate=pl.CostEstimate(flops=8 * 10**9, bytes_accessed=30 * 10**6, transcendentals=0),
    )(tables, *flat_planes(planes), down, down)


def dispatch_rows(tables, planes, gate, up, hidden_grad, slot_gate):
    width, half = gate.shape[1], gate.shape[2] // 2
    chunk = chunk_of(half)
    steps = half // chunk
    small = jax.ShapeDtypeStruct((1024, width), BF16)
    return pl.pallas_call(
        rows_kernel,
        grid=(steps,),
        in_specs=[whole(tables.shape)]
        + [pl.BlockSpec((128, chunk), lambda n: (0, n))] * 24
        + weight_specs(gate, chunk, steps)
        + weight_specs(up, chunk, steps)
        + [whole((1024, width)), whole((1024, 1))],
        out_specs=[pl.BlockSpec((2, 1024, chunk), lambda n: (0, 0, n))] + [whole((1024, width))] * 3,
        out_shape=[jax.ShapeDtypeStruct((2, 1024, half), BF16), small, small, small],
        scratch_shapes=[pltpu.VMEM((1024, width), F32)] * 2,
        compiler_params=params(),
        cost_estimate=pl.CostEstimate(flops=10**10, bytes_accessed=30 * 10**6, transcendentals=0),
    )(tables, *flat_planes(planes), gate, gate, up, up, hidden_grad, slot_gate)


def combine(tables_t, acts, weights):
    width, half = weights[0].shape[1], weights[0].shape[2] // 2
    chunk = chunk_of(half)
    steps = half // chunk
    specs, doubled = [], []
    for w in weights:
        specs += weight_specs(w, chunk, steps)
        doubled += [w, w]
    out = jax.ShapeDtypeStruct((4, 3, 128, half), BF16)
    return pl.pallas_call(
        functools.partial(combine_kernel, len(acts)),
        grid=(steps,),
        in_specs=[whole(tables_t.shape)] + [whole((1024, width))] * len(acts) + specs,
        out_specs=[pl.BlockSpec((4, 3, 128, chunk), lambda n: (0, 0, 0, n))] * 2,
        out_shape=[out, out],
        scratch_shapes=[pltpu.VMEM((2, 1024, chunk), BF16)],
        compiler_params=params(),
        cost_estimate=pl.CostEstimate(flops=8 * 10**9, bytes_accessed=30 * 10**6, transcendentals=0),
    )(tables_t, *acts, *doubled)


def weight_grads(rows, grads, hidden, gate_grad, up_grad):
    width, half = hidden.shape[1], rows.shape[2]
    chunk = chunk_of(half)
    steps = half // chunk
    out = jax.ShapeDtypeStruct((2, width, 2 * half), BF16)
    return pl.pallas_call(
        weight_grads_kernel,
        grid=(2, steps),
        in_specs=[pl.BlockSpec((1, 1024, chunk), lambda i, n: (i, 0, n))] * 2 + [whole((1024, width))] * 3,
        out_specs=[pl.BlockSpec((2, width, chunk), lambda i, n: (0, 0, i * steps + n))] * 3,
        out_shape=[out] * 3,
        compiler_params=params(),
        cost_estimate=pl.CostEstimate(flops=8 * 10**9, bytes_accessed=30 * 10**6, transcendentals=0),
    )(rows, grads, hidden, gate_grad, up_grad)


def on_device(
    context, out_proj, residual, norm_gain, gate_weight, up_weight, down_weight, expert_ids, gate_codes, cotangent
):
    width = residual.shape[1]
    half = width // 2
    x, zl, core = lax.axis_index("x"), lax.axis_index("zl"), lax.axis_index("core")
    tp = (x * 2 + zl) * 2 + core

    meta = jnp.concatenate(
        [
            jnp.pad(expert_ids.T.astype(BF16), ((0, 0), (0, 4))),
            jnp.pad(gate_codes.T.astype(BF16), ((0, 0), (0, 128 - 16 - TOK))),
        ],
        axis=1,
    )
    cot = pack(cotangent)
    cot_planes = gather_all([cot[0], cot[1], jnp.concatenate([cot[2], meta], axis=1)])

    order = np.arange(16)
    h, j, k = order // 8, (order // 2) % 4, order % 2
    sign = (1 - 2 * core) * jnp.asarray(1 - 2 * h)
    owner = (((x - j * sign) % 4) * 2 + (zl ^ jnp.asarray(k))) * 2 + (core ^ jnp.asarray(h))
    lane = np.arange(8)
    head_row = (owner[:, None] * TOK + lane[None, :]).reshape(128)
    tail_row = (owner[:, None] * TOK + 8 + (lane % 4)[None, :]).reshape(128)
    token = jnp.arange(16 * TOK)
    picked = (jnp.concatenate([head_row, tail_row])[:, None] == token[None, :]).astype(BF16)
    ordered = jnp.dot(picked, context, preferred_element_type=F32).astype(BF16)
    partial = jnp.dot(ordered, out_proj, preferred_element_type=F32).astype(BF16)
    first = jnp.asarray((np.arange(128) % 8 < 4)[:, None])
    tail = jnp.where(first, partial[128:, :half], partial[128:, half:])
    partial = jnp.concatenate([partial[:128], tail], axis=1).reshape(2, 8, 8, 3 * half)
    summed = (partial[0].astype(F32) + send(partial[1], SWAP).astype(F32)).astype(BF16)
    attended = summed[0].astype(F32)
    for j in range(4):
        for k in range(2):
            if j or k:
                attended = attended + send(summed[2 * j + k], tp_shifted(-j, k)).astype(F32)

    split = lambda v: [v[:, i * half : (i + 1) * half] for i in range(3)]
    stream = [r.astype(F32) + a for r, a in zip(pack(residual), split(attended))]
    inverse = [
        lax.rsqrt(s / width + EPSILON) for s in row_sums([s * s for s in stream])
    ]
    upper = jnp.asarray((np.arange(8) < 4)[:, None])
    gain = [
        norm_gain[None, :half],
        norm_gain[None, half:],
        jnp.where(upper, norm_gain[None, :half], norm_gain[None, half:]),
    ]
    inv = [inverse[0], inverse[0], inverse[1]]
    normed = [(s * i * g).astype(BF16) for s, i, g in zip(stream, inv, gain)]
    row_planes = gather_all(normed)

    meta = jnp.stack(
        [
            jnp.stack([v[:, half:].reshape(4, 4, 8, 128) for v in side], axis=1)
            for side in cot_planes[2]
        ]
    ).reshape(128, 8, 128)
    tables, slot_gate = routing(meta, 2 * tp)
    tables_t = tables.transpose(0, 1, 3, 2)

    grad_rows, hidden_grad = dispatch_grads(tables, cot_planes, down_weight)
    rows, hidden, gate_grad, up_grad = dispatch_rows(
        tables, row_planes, gate_weight, up_weight, hidden_grad, slot_gate
    )
    back = scatter_all(*combine(tables_t, [gate_grad, up_grad], [gate_weight, up_weight]))
    mixture = scatter_all(*combine(tables_t, [hidden], [down_weight]))
    gate_out, up_out, down_out = weight_grads(rows, grad_rows, hidden, gate_grad, up_grad)

    scaled = [b * g for b, g in zip(back, gain)]
    inner = [s / width for s in row_sums([a * b for a, b in zip(scaled, stream)])]
    inner = [inner[0], inner[0], inner[1]]
    grad = [
        (c.astype(F32) + i * s - st * (i * i * i) * m).astype(BF16)
        for c, i, s, st, m in zip(cot, inv, scaled, stream, inner)
    ]
    residual_grad = unpack(grad)
    output = unpack([(s + m).astype(BF16) for s, m in zip(stream, mixture)])

    packed = jnp.concatenate(grad, axis=1)
    own = [packed if not (j or k) else send(packed, tp_shifted(j, k)) for j in range(4) for k in range(2)]
    own = jnp.concatenate(own, axis=0)
    both = jnp.concatenate([own, send(own, SWAP)], axis=0)
    is_head = (token[:, None] == head_row[None, :]).astype(BF16)
    is_tail = (token[:, None] == tail_row[None, :]).astype(BF16)
    upper_cols = jnp.asarray(np.arange(128) % 8 < 4)[None, :]
    heads = jnp.dot(is_head, both[:, : 2 * half], preferred_element_type=F32)
    tails = [
        jnp.dot(jnp.where(pick, is_tail, 0).astype(BF16), both[:, 2 * half :], preferred_element_type=F32)
        for pick in (upper_cols, ~upper_cols)
    ]
    full = (heads + jnp.concatenate(tails, axis=1)).astype(BF16)
    context_grad = jnp.einsum("td,ad->ta", full, out_proj, preferred_element_type=F32).astype(BF16)
    return (output, residual_grad, context_grad, gate_out, up_out, down_out)


def solution(mesh):
    fine = Mesh(np.asarray(mesh.devices).reshape(2, 4, 4, 2, 2), AXES)
    ctx, tp = AXES[:2], AXES[2:]
    rows = P(AXES, None)
    experts = P(tp, ctx, None)
    return jax.shard_map(
        on_device,
        mesh=fine,
        in_specs=(P(ctx, tp), P(tp, None), rows, P(), experts, experts, experts, rows, rows, rows),
        out_specs=(rows, rows, P(ctx, tp), experts, experts, experts),
        check_vma=False,
    )
```

```python
import functools

import numpy as np
import jax
import jax.numpy as jnp
from jax import lax
from jax.experimental import pallas as pl
from jax.experimental.pallas import tpu as pltpu
from jax.sharding import Mesh, PartitionSpec as P

AXES = ("zh", "y", "x", "zl", "core")
CAP = 4
TOK = 12
EPSILON = 1e-06
BF16 = jnp.bfloat16
F32 = jnp.float32
VMEM_LIMIT = 50 * 1024 * 1024


def flat_index(z, y, x, core):
    return ((((z // 2) * 4 + y) * 4 + x) * 2 + z % 2) * 2 + core


def permutation(move):
    return [
        (flat_index(z, y, x, c), flat_index(*move(z, y, x, c)))
        for z in range(4)
        for y in range(4)
        for x in range(4)
        for c in range(2)
    ]


def shifted(axis, steps):
    def move(z, y, x, c):
        d = steps * (1 - 2 * c)
        if axis == "x":
            return z, y, (x + d) % 4, c
        if axis == "y":
            return z, (y + d) % 4, x, c
        return (z + d) % 4, y, x, c

    return permutation(move)


def tp_shifted(steps, flip):
    return permutation(lambda z, y, x, c: (z ^ flip, y, (x + steps * (1 - 2 * c)) % 4, c))


SWAP = permutation(lambda z, y, x, c: (z, y, x, 1 - c))
ORDERS = (("x", "y", "z"), ("y", "z", "x"), ("z", "x", "y"))


def send(v, pairs):
    return lax.ppermute(v, AXES, pairs)


def after(v, first):
    return lax.optimization_barrier((v, first))[0]


def around(v, axis, first=None):
    up = send(v, shifted(axis, 1))
    down = send(v, shifted(axis, -1))
    if first is not None:
        up = after(up, first)
    return [v, up, send(up, shifted(axis, 1)), down]


def around_sum(blocks, axis):
    chain = (blocks[3].astype(F32) + send(blocks[2], shifted(axis, 1)).astype(F32)).astype(BF16)
    direct = send(blocks[1], shifted(axis, -1)).astype(F32)
    return blocks[0].astype(F32) + direct + send(chain, shifted(axis, 1)).astype(F32)


def full_ring(v, axis):
    out = [v]
    for _ in range(3):
        out.append(send(out[-1], shifted(axis, 1)))
    return out


def gather_part(part, order):
    a, b, c = order
    width = part.shape[-1]
    one = jnp.stack(around(part, a))
    two = jnp.stack(around(one, b), axis=0 if a == "x" else 1)
    return full_ring(two.reshape(128, width), c)


def gather_parts(parts):
    out = []
    for part, order in zip(parts, ORDERS):
        own = gather_part(part, order)
        out.append((own, [send(v, SWAP) for v in own]))
    return out


def gather_whole(packed, first):
    planes = jnp.concatenate(around(packed, "z", first), axis=0)
    return lax.all_gather(planes, ("y", "x"), axis=0, tiled=True)


def scatter_parts(own, sib, meanwhile):
    width = own[0].shape[-1]
    arrived = {j: send(sib[j], SWAP) for j in (1, 2, 3, 0)}
    sums = []
    for p, (a, b, c) in enumerate(ORDERS):
        t = None
        for j in (1, 2, 3, 0):
            v = own[j][p].astype(F32) + arrived[j][p].astype(F32)
            if j == 0:
                t = after(t, meanwhile)
            if t is not None:
                v = v + send(t, shifted(c, 1)).astype(F32)
            t = v.astype(BF16)
        at = 0 if a == "x" else 1
        t = t.reshape(4, 4, 8, width)
        t = around_sum([lax.index_in_dim(t, d, at, False) for d in range(4)], b).astype(BF16)
        sums.append(around_sum([t[d] for d in range(4)], a))
    return sums


def add_swapped(own, sib):
    return (own.astype(F32) + send(sib, SWAP).astype(F32)).astype(BF16)


def scatter_whole(t):
    t = lax.psum_scatter(t, ("y", "x"), scatter_dimension=0, tiled=True)
    t = around_sum([t[8 * d : 8 * d + 8] for d in range(4)], "z")
    width = t.shape[1] // 3
    return [t[:, i * width : (i + 1) * width] for i in range(3)]


def pack(rows):
    half = rows.shape[1] // 2
    tail = rows[8:]
    return [rows[:8, :half], rows[:8, half:], jnp.concatenate([tail[:, :half], tail[:, half:]], axis=0)]


def unpack(parts):
    left, right, tail = parts
    return jnp.concatenate(
        [
            jnp.concatenate([left, right], axis=1),
            jnp.concatenate([tail[:4], tail[4:]], axis=1),
        ],
        axis=0,
    )


def row_sums(products):
    head = jnp.sum(products[0], axis=1, keepdims=True) + jnp.sum(products[1], axis=1, keepdims=True)
    tail = jnp.sum(products[2], axis=1, keepdims=True)
    return head, tail + jnp.concatenate([tail[4:], tail[:4]], axis=0)


def dot(a, b, ca, cb):
    return lax.dot_general(a, b, (((ca,), (cb,)), ((), ())), preferred_element_type=F32)


def iota(axis):
    return lax.broadcasted_iota(jnp.int32, (128, 128), axis)


def one_if(condition, dtype=BF16):
    return jnp.where(condition, 1.0, 0.0).astype(dtype)


def routing_kernel(plane_of, info, *refs):
    planes, (tables, slot_gate) = refs[:2], refs[2:]
    slot, col = iota(0), iota(1)
    slot_block = (slot & 63) >> 2
    rank_of = (slot & 3).astype(F32)
    expert = ((slot >> 6) + info[2:3, :]).astype(F32)
    lane, sub = col, col & 7
    before = one_if(slot < col)
    is_token = lane < TOK
    spreads = [
        one_if(slot == sub),
        one_if((sub < 4) & (slot == sub + 8)),
        one_if((sub >= 4) & (slot == sub + 4)),
    ]
    block = col >> 3
    zx = one_if(block == slot_block, F32)
    xz = one_if((((block & 3) << 2) + (block >> 2)) == slot_block, F32)
    for group in range(8):
        half, g = divmod(group, 4)
        mine = info[half : half + 1, :] == slot_block
        meta = planes[half][plane_rows(plane_of, group), :]
        has = code = total = jnp.zeros((128, 128), F32)
        for k in range(8):
            value = dot(one_if(mine & (sub == k)), meta, 1, 0)
            codes = pltpu.roll(value, 128 - 16, 1)
            hit = one_if((value == expert) & is_token, F32)
            has = has + hit
            code = code + hit * codes
            total = total + codes
        rank = dot(has.astype(BF16), before, 1, 0)
        place = jnp.where(rank == rank_of, has, 0.0)
        number = jnp.sum(place * code, axis=1, keepdims=True)
        over = jnp.sum(place * total, axis=1, keepdims=True)
        gate = jnp.where(over > 0.0, number / jnp.maximum(over, 1.0), 0.0)
        slot_gate[pl.ds(group * 64, 64), :] = gate[:64]
        slot_gate[pl.ds(512 + group * 64, 64), :] = gate[64:]
        head, left, right = (dot(place.astype(BF16), s, 1, 0) for s in spreads)
        here = one_if(mine, F32)
        for i, (t, m) in enumerate(
            ((head, zx), (head, xz), (left, zx), (right, zx), (head, here), (left, here), (right, here))
        ):
            tables[i, group] = (t * m).astype(BF16)


def plane_rows(plane_of, group):
    return pl.ds(pl.multiple_of(plane_of[group] * 128, 128), 128)


def place_group(tables, group, heads, tail, out_ref, at):
    for lr in range(2):
        rows = dot(tables[at[lr], group], heads[lr], 1, 0) + dot(tables[at[2 + lr], group], tail, 1, 0)
        rows = rows.astype(BF16)
        out_ref[lr, pl.ds(group * 64, 64), :] = rows[:64]
        out_ref[lr, pl.ds(512 + group * 64, 64), :] = rows[64:]


def grads_kernel(plane_of, tables, *refs):
    planes, down = refs[:6], refs[6:8]
    rows, hidden_grad, total = refs[8:]
    step = pl.program_id(0)

    @pl.when(step == 0)
    def _():
        total[...] = jnp.zeros_like(total)

    for group in range(8):
        at = plane_rows(plane_of, group)
        left, right, tail = (planes[2 * p + group // 4][at, :] for p in range(3))
        place_group(tables, group, (left, right), tail, rows, (4, 4, 5, 6))
    for e in range(2):
        at = pl.ds(e * 512, 512)
        total[at, :] += dot(rows[0, at, :], down[0][e], 1, 1) + dot(rows[1, at, :], down[1][e], 1, 1)

    @pl.when(step == pl.num_programs(0) - 1)
    def _():
        hidden_grad[...] = total[...]


def rows_kernel(*refs):
    tables, planes = refs[0], refs[1:25]
    gate, up = refs[25:27], refs[27:29]
    hidden_grad, slot_gate = refs[29:31]
    rows, hidden, gate_grad, up_grad, gate_total, up_total = refs[31:]
    step = pl.program_id(0)

    @pl.when(step == 0)
    def _():
        gate_total[...] = jnp.zeros_like(gate_total)
        up_total[...] = jnp.zeros_like(up_total)

    for group in range(8):
        half, g = divmod(group, 4)
        zs, xs, ys = (planes[p * 8 + half * 4 : p * 8 + half * 4 + 4] for p in range(3))
        pick = pl.ds(g * 32, 32)
        left = jnp.concatenate([ref[pick, :] for ref in zs], axis=0)
        right = jnp.concatenate([ref[pick, :] for ref in xs], axis=0)
        place_group(tables, group, (left, right), ys[g][...], rows, (0, 1, 2, 3))
    for e in range(2):
        at = pl.ds(e * 512, 512)
        left, right = rows[0, at, :], rows[1, at, :]
        gate_total[at, :] += dot(left, gate[0][e], 1, 1) + dot(right, gate[1][e], 1, 1)
        up_total[at, :] += dot(left, up[0][e], 1, 1) + dot(right, up[1][e], 1, 1)

    @pl.when(step == pl.num_programs(0) - 1)
    def _():
        for i in range(8):
            at = pl.ds(i * 128, 128)
            gate_act, up_act = gate_total[at, :], up_total[at, :]
            scale = slot_gate[at, :]
            back = hidden_grad[at, :] * scale
            s = 1.0 / (1.0 + jnp.exp(-gate_act))
            silu = gate_act * s
            hidden[at, :] = (silu * up_act * scale).astype(BF16)
            up_grad[at, :] = (back * silu).astype(BF16)
            gate_grad[at, :] = (back * up_act * s * (1.0 + gate_act * (1.0 - s))).astype(BF16)


def both_experts(slots, lr, group):
    return jnp.concatenate(
        [slots[lr, pl.ds(group * 64, 64), :], slots[lr, pl.ds(512 + group * 64, 64), :]], axis=0
    )


def back_kernel(tables, gate_grad, up_grad, *refs):
    gate, up, outs, slots = refs[:2], refs[2:4], refs[4:-1], refs[-1]
    for lr in range(2):
        for e in range(2):
            pick = pl.ds(e * 512, 512)
            value = dot(gate_grad[pick, :], gate[lr][e], 1, 0) + dot(up_grad[pick, :], up[lr][e], 1, 0)
            slots[lr, pick, :] = value.astype(BF16)
    for group in range(8):
        half, g = divmod(group, 4)
        out = outs[half * 4 : half * 4 + 4]
        left, right = (both_experts(slots, lr, group) for lr in range(2))
        head_left = dot(tables[0, group], left, 0, 0).astype(BF16)
        head_right = dot(tables[1, group], right, 0, 0).astype(BF16)
        tail = dot(tables[2, group], left, 0, 0) + dot(tables[3, group], right, 0, 0)
        for i in range(4):
            out[i][0, pl.ds(g * 32, 32), :] = head_left[i * 32 : (i + 1) * 32]
            out[i][1, pl.ds(g * 32, 32), :] = head_right[i * 32 : (i + 1) * 32]
        out[g][2] = tail.astype(BF16)


def out_kernel(steps, plane_of, tables, hidden, down, own, sib, slots):
    step = pl.program_id(0)
    outs = (own, sib)

    @pl.when(step < 2 * steps)
    def _():
        for e in range(2):
            pick = pl.ds(e * 512, 512)
            slots[step, pick, :] = dot(hidden[pick, :], down[e], 1, 0).astype(BF16)
        for group in range(8):
            value = dot(tables[4, group], both_experts(slots, step, group), 0, 0)
            outs[group // 4][plane_rows(plane_of, group), :] = value.astype(BF16)

    @pl.when(step >= 2 * steps)
    def _():
        for group in range(8):
            value = dot(tables[5, group], both_experts(slots, step - 2 * steps, group), 0, 0)
            value = value + dot(tables[6, group], both_experts(slots, step - steps, group), 0, 0)
            outs[group // 4][plane_rows(plane_of, group), :] = value.astype(BF16)


def weight_grads_kernel(rows, grads, hidden, gate_grad, up_grad, gate_out, up_out, down_out):
    for e in range(2):
        at = pl.ds(e * 512, 512)
        x = rows[0, at, :]
        gate_out[e] = dot(gate_grad[at, :], x, 0, 0).astype(BF16)
        up_out[e] = dot(up_grad[at, :], x, 0, 0).astype(BF16)
        down_out[e] = dot(hidden[at, :], grads[0, at, :], 0, 0).astype(BF16)


def whole(shape):
    return pl.BlockSpec(shape, lambda *_: (0,) * len(shape))


def params():
    return pltpu.CompilerParams(vmem_limit_bytes=VMEM_LIMIT)


def chunk_of(half):
    return min(512, half)


def flat_planes(planes):
    return [v for part in planes for half in part for v in half]


def weight_specs(weight, chunk, steps):
    shape = (weight.shape[0], weight.shape[1], chunk)
    return [
        pl.BlockSpec(shape, lambda n: (0, 0, n)),
        pl.BlockSpec(shape, lambda n, steps=steps: (0, 0, n + steps)),
    ]


def scalars():
    return pl.BlockSpec(memory_space=pltpu.SMEM)


def routing(plane_of, info, planes, width):
    return pl.pallas_call(
        routing_kernel,
        grid=(1,),
        in_specs=[scalars(), whole((8, 128))]
        + [pl.BlockSpec((512, 128), lambda n: (0, width // 128))] * 2,
        out_specs=[whole((7, 8, 128, 128)), whole((1024, 1))],
        out_shape=[
            jax.ShapeDtypeStruct((7, 8, 128, 128), BF16),
            jax.ShapeDtypeStruct((1024, 1), F32),
        ],
        compiler_params=params(),
        cost_estimate=pl.CostEstimate(flops=10**9, bytes_accessed=10**7, transcendentals=0),
    )(plane_of, info, *planes)


def dispatch_grads(plane_of, tables, planes, down):
    width, half = down.shape[1], down.shape[2] // 2
    chunk = chunk_of(half)
    steps = half // chunk
    specs = []
    for p in range(3):
        specs += [pl.BlockSpec((512, chunk), lambda n, p=p: (0, n + p * steps))] * 2
    return pl.pallas_call(
        grads_kernel,
        grid=(steps,),
        in_specs=[scalars(), whole(tables.shape)] + specs + weight_specs(down, chunk, steps),
        out_specs=[pl.BlockSpec((2, 1024, chunk), lambda n: (0, 0, n)), whole((1024, width))],
        out_shape=[
            jax.ShapeDtypeStruct((2, 1024, half), BF16),
            jax.ShapeDtypeStruct((1024, width), F32),
        ],
        scratch_shapes=[pltpu.VMEM((1024, width), F32)],
        compiler_params=params(),
        cost_estimate=pl.CostEstimate(flops=8 * 10**9, bytes_accessed=30 * 10**6, transcendentals=0),
    )(plane_of, tables, *(planes * 3), down, down)


def dispatch_rows(tables, planes, gate, up, hidden_grad, slot_gate):
    width, half = gate.shape[1], gate.shape[2] // 2
    chunk = chunk_of(half)
    steps = half // chunk
    small = jax.ShapeDtypeStruct((1024, width), BF16)
    return pl.pallas_call(
        rows_kernel,
        grid=(steps,),
        in_specs=[whole(tables.shape)]
        + [pl.BlockSpec((128, chunk), lambda n: (0, n))] * 24
        + weight_specs(gate, chunk, steps)
        + weight_specs(up, chunk, steps)
        + [whole((1024, width)), whole((1024, 1))],
        out_specs=[pl.BlockSpec((2, 1024, chunk), lambda n: (0, 0, n))] + [whole((1024, width))] * 3,
        out_shape=[jax.ShapeDtypeStruct((2, 1024, half), BF16), small, small, small],
        scratch_shapes=[pltpu.VMEM((1024, width), F32)] * 2,
        compiler_params=params(),
        cost_estimate=pl.CostEstimate(flops=10**10, bytes_accessed=30 * 10**6, transcendentals=0),
    )(tables, *flat_planes(planes), gate, gate, up, up, hidden_grad, slot_gate)


def combine_back(tables, gate_grad, up_grad, gate, up):
    width, half = gate.shape[1], gate.shape[2] // 2
    chunk = chunk_of(half)
    steps = half // chunk
    out = jax.ShapeDtypeStruct((3, 128, half), BF16)
    outs = pl.pallas_call(
        back_kernel,
        grid=(steps,),
        in_specs=[whole(tables.shape)]
        + [whole((1024, width))] * 2
        + weight_specs(gate, chunk, steps)
        + weight_specs(up, chunk, steps),
        out_specs=[pl.BlockSpec((3, 128, chunk), lambda n: (0, 0, n))] * 8,
        out_shape=[out] * 8,
        scratch_shapes=[pltpu.VMEM((2, 1024, chunk), BF16)],
        compiler_params=params(),
        cost_estimate=pl.CostEstimate(flops=8 * 10**9, bytes_accessed=30 * 10**6, transcendentals=0),
    )(tables, gate_grad, up_grad, gate, gate, up, up)
    return outs[:4], outs[4:]


def combine_out(plane_of, tables, hidden, down):
    width, half = down.shape[1], down.shape[2] // 2
    chunk = chunk_of(half)
    steps = half // chunk
    out = jax.ShapeDtypeStruct((512, 3 * half), BF16)
    return pl.pallas_call(
        functools.partial(out_kernel, steps),
        grid=(3 * steps,),
        in_specs=[
            scalars(),
            whole(tables.shape),
            whole((1024, width)),
            pl.BlockSpec((2, width, chunk), lambda n: (0, 0, jnp.minimum(n, 2 * steps - 1))),
        ],
        out_specs=[pl.BlockSpec((512, chunk), lambda n: (0, n))] * 2,
        out_shape=[out] * 2,
        scratch_shapes=[pltpu.VMEM((2 * steps, 1024, chunk), BF16)],
        compiler_params=params(),
        cost_estimate=pl.CostEstimate(flops=6 * 10**9, bytes_accessed=30 * 10**6, transcendentals=0),
    )(plane_of, tables, hidden, down)


def weight_grads(rows, grads, hidden, gate_grad, up_grad):
    width, half = hidden.shape[1], rows.shape[2]
    chunk = chunk_of(half)
    steps = half // chunk
    out = jax.ShapeDtypeStruct((2, width, 2 * half), BF16)
    return pl.pallas_call(
        weight_grads_kernel,
        grid=(2, steps),
        in_specs=[pl.BlockSpec((1, 1024, chunk), lambda i, n: (i, 0, n))] * 2 + [whole((1024, width))] * 3,
        out_specs=[pl.BlockSpec((2, width, chunk), lambda i, n: (0, 0, i * steps + n))] * 3,
        out_shape=[out] * 3,
        compiler_params=params(),
        cost_estimate=pl.CostEstimate(flops=8 * 10**9, bytes_accessed=30 * 10**6, transcendentals=0),
    )(rows, grads, hidden, gate_grad, up_grad)


def on_device(
    context, out_proj, residual, norm_gain, gate_weight, up_weight, down_weight, expert_ids, gate_codes, cotangent
):
    width = residual.shape[1]
    half = width // 2
    x, zl, core = lax.axis_index("x"), lax.axis_index("zl"), lax.axis_index("core")
    tp = (x * 2 + zl) * 2 + core

    meta = jnp.concatenate(
        [
            jnp.pad(expert_ids.T.astype(BF16), ((0, 0), (0, 4))),
            jnp.pad(gate_codes.T.astype(BF16), ((0, 0), (0, 128 - 16 - TOK))),
        ],
        axis=1,
    )
    cot = pack(cotangent)
    order = np.arange(16)
    h, j, k = order // 8, (order // 2) % 4, order % 2
    sign = (1 - 2 * core) * jnp.asarray(1 - 2 * h)
    owner = (((x - j * sign) % 4) * 2 + (zl ^ jnp.asarray(k))) * 2 + (core ^ jnp.asarray(h))
    lane = np.arange(8)
    head_row = (owner[:, None] * TOK + lane[None, :]).reshape(128)
    tail_row = (owner[:, None] * TOK + 8 + (lane % 4)[None, :]).reshape(128)
    token = jnp.arange(16 * TOK)
    picked = (jnp.concatenate([head_row, tail_row])[:, None] == token[None, :]).astype(BF16)
    ordered = jnp.dot(picked, context, preferred_element_type=F32).astype(BF16)
    partial = jnp.dot(ordered, out_proj, preferred_element_type=F32).astype(BF16)
    cot_own = gather_whole(jnp.concatenate(cot + [meta], axis=1), partial)
    first = jnp.asarray((np.arange(128) % 8 < 4)[:, None])
    tail = jnp.where(first, partial[128:, :half], partial[128:, half:])
    partial = jnp.concatenate([partial[:128], tail], axis=1).reshape(2, 8, 8, 3 * half)
    summed = (partial[0].astype(F32) + send(partial[1], SWAP).astype(F32)).astype(BF16)
    attended = summed[0].astype(F32)
    for j in range(4):
        for k in range(2):
            if j or k:
                attended = attended + send(summed[2 * j + k], tp_shifted(-j, k)).astype(F32)

    split = lambda v: [v[:, i * half : (i + 1) * half] for i in range(3)]
    stream = [r.astype(F32) + a for r, a in zip(pack(residual), split(attended))]
    inverse = [
        lax.rsqrt(s / width + EPSILON) for s in row_sums([s * s for s in stream])
    ]
    upper = jnp.asarray((np.arange(8) < 4)[:, None])
    gain = [
        norm_gain[None, :half],
        norm_gain[None, half:],
        jnp.where(upper, norm_gain[None, :half], norm_gain[None, half:]),
    ]
    inv = [inverse[0], inverse[0], inverse[1]]
    normed = [(s * i * g).astype(BF16) for s, i, g in zip(stream, inv, gain)]
    row_planes = gather_parts(normed)

    cot_own = after(cot_own, [row_planes[p][0][1] for p in range(3)])
    cot_planes = (cot_own, send(cot_own, SWAP))

    y = lax.axis_index("y")
    block = np.arange(128) // 8
    turn = (1 - 2 * core) * jnp.asarray([[1], [-1]])
    steps_to = (block % 4) * 4 + ((x - block // 4) * turn) % 4
    info = jnp.concatenate([steps_to, jnp.full((6, 128), 2 * tp)], axis=0).astype(jnp.int32)
    plane_of = ((y - jnp.arange(4) * turn) % 4).reshape(8).astype(jnp.int32)
    tables, slot_gate = routing(plane_of, info, cot_planes, 3 * half)

    grad_rows, hidden_grad = dispatch_grads(plane_of, tables, cot_planes, down_weight)
    rows, hidden, gate_grad, up_grad = dispatch_rows(
        tables, row_planes, gate_weight, up_weight, hidden_grad, slot_gate
    )
    back = combine_back(tables, gate_grad, up_grad, gate_weight, up_weight)
    out_sums = add_swapped(*combine_out(plane_of, tables, after(hidden, back[1][1]), down_weight))
    back = scatter_parts(*back, out_sums)
    mixture = scatter_whole(out_sums)
    gate_out, up_out, down_out = weight_grads(rows, grad_rows, hidden, gate_grad, up_grad)

    scaled = [b * g for b, g in zip(back, gain)]
    inner = [s / width for s in row_sums([a * b for a, b in zip(scaled, stream)])]
    inner = [inner[0], inner[0], inner[1]]
    grad = [
        (c.astype(F32) + i * s - st * (i * i * i) * m).astype(BF16)
        for c, i, s, st, m in zip(cot, inv, scaled, stream, inner)
    ]
    residual_grad = unpack(grad)
    output = unpack([(s + m).astype(BF16) for s, m in zip(stream, mixture)])

    packed = jnp.concatenate(grad, axis=1)
    own = [packed if not (j or k) else send(packed, tp_shifted(j, k)) for j in range(4) for k in range(2)]
    own = jnp.concatenate(own, axis=0)
    both = jnp.concatenate([own, send(own, SWAP)], axis=0)
    is_head = (token[:, None] == head_row[None, :]).astype(BF16)
    is_tail = (token[:, None] == tail_row[None, :]).astype(BF16)
    upper_cols = jnp.asarray(np.arange(128) % 8 < 4)[None, :]
    heads = jnp.dot(is_head, both[:, : 2 * half], preferred_element_type=F32)
    tails = [
        jnp.dot(jnp.where(pick, is_tail, 0).astype(BF16), both[:, 2 * half :], preferred_element_type=F32)
        for pick in (upper_cols, ~upper_cols)
    ]
    full = (heads + jnp.concatenate(tails, axis=1)).astype(BF16)
    context_grad = jnp.einsum("td,ad->ta", full, out_proj, preferred_element_type=F32).astype(BF16)
    return (output, residual_grad, context_grad, gate_out, up_out, down_out)


def solution(mesh):
    fine = Mesh(np.asarray(mesh.devices).reshape(2, 4, 4, 2, 2), AXES)
    ctx, tp = AXES[:2], AXES[2:]
    rows = P(AXES, None)
    experts = P(tp, ctx, None)
    return jax.shard_map(
        on_device,
        mesh=fine,
        in_specs=(P(ctx, tp), P(tp, None), rows, P(), experts, experts, experts, rows, rows, rows),
        out_specs=(rows, rows, P(ctx, tp), experts, experts, experts),
        check_vma=False,
    )
```

```python
import functools

import numpy as np
import jax
import jax.numpy as jnp
from jax import lax
from jax.experimental import pallas as pl
from jax.experimental.pallas import tpu as pltpu
from jax.sharding import Mesh, PartitionSpec as P

AXES = ("zh", "y", "x", "zl", "core")
CAP = 4
TOK = 12
EPSILON = 1e-06
BF16 = jnp.bfloat16
F32 = jnp.float32
VMEM_LIMIT = 50 * 1024 * 1024


def flat_index(z, y, x, core):
    return ((((z // 2) * 4 + y) * 4 + x) * 2 + z % 2) * 2 + core


def permutation(move):
    return [
        (flat_index(z, y, x, c), flat_index(*move(z, y, x, c)))
        for z in range(4)
        for y in range(4)
        for x in range(4)
        for c in range(2)
    ]


def shifted(axis, steps):
    def move(z, y, x, c):
        d = steps * (1 - 2 * c)
        if axis == "x":
            return z, y, (x + d) % 4, c
        if axis == "y":
            return z, (y + d) % 4, x, c
        return (z + d) % 4, y, x, c

    return permutation(move)


def tp_shifted(steps, flip):
    return permutation(lambda z, y, x, c: (z ^ flip, y, (x + steps * (1 - 2 * c)) % 4, c))


SWAP = permutation(lambda z, y, x, c: (z, y, x, 1 - c))


def send(v, pairs):
    return lax.ppermute(v, AXES, pairs)


def after(v, first):
    return lax.optimization_barrier((v, first))[0]


def around(v, axis, first=None):
    up = send(v, shifted(axis, 1))
    down = send(v, shifted(axis, -1))
    if first is not None:
        up = after(up, first)
    return [v, up, send(up, shifted(axis, 1)), down]


def around_sum(blocks, axis):
    chain = (blocks[3].astype(F32) + send(blocks[2], shifted(axis, 1)).astype(F32)).astype(BF16)
    direct = send(blocks[1], shifted(axis, -1)).astype(F32)
    return blocks[0].astype(F32) + direct + send(chain, shifted(axis, 1)).astype(F32)


def full_ring(v, axis):
    out = [v]
    for _ in range(3):
        out.append(send(out[-1], shifted(axis, 1)))
    return out


def gather_whole(packed):
    return lax.all_gather(packed, ("y", "x"), axis=0, tiled=True)


def gather_plane(part):
    one = jnp.concatenate(around(part, "x"), axis=0)
    return jnp.concatenate(around(one, "y"), axis=0)


def scatter_whole(t):
    return lax.psum_scatter(t, ("y", "x"), scatter_dimension=0, tiled=True)


def finish_whole(t):
    return around_sum([t[8 * d : 8 * d + 8] for d in range(4)], "z")


def add_swapped(own, sib):
    return (own.astype(F32) + send(sib, SWAP).astype(F32)).astype(BF16)


def scatter_planes(own, sib, beside=(None,) * 4):
    t = None
    arrived = {j: send(sib[j], SWAP) for j in (1, 2, 3, 0)}
    for j, other in zip((1, 2, 3, 0), beside):
        v = own[j].astype(F32) + arrived[j].astype(F32)
        if t is not None:
            v = v + send(t, shifted("z", 1)).astype(F32)
        t = v.astype(BF16)
        if other is not None:
            t = after(t, other)
    return t


def finish_planes(t):
    t = around_sum([t[32 * d : 32 * d + 32] for d in range(4)], "y").astype(BF16)
    return around_sum([t[8 * d : 8 * d + 8] for d in range(4)], "x")


def pack(rows):
    half = rows.shape[1] // 2
    tail = rows[8:]
    return [rows[:8, :half], rows[:8, half:], jnp.concatenate([tail[:, :half], tail[:, half:]], axis=0)]


def unpack(parts):
    left, right, tail = parts
    return jnp.concatenate(
        [
            jnp.concatenate([left, right], axis=1),
            jnp.concatenate([tail[:4], tail[4:]], axis=1),
        ],
        axis=0,
    )


def row_sums(products):
    head = jnp.sum(products[0], axis=1, keepdims=True) + jnp.sum(products[1], axis=1, keepdims=True)
    tail = jnp.sum(products[2], axis=1, keepdims=True)
    return head, tail + jnp.concatenate([tail[4:], tail[:4]], axis=0)


def dot(a, b, ca, cb):
    return lax.dot_general(a, b, (((ca,), (cb,)), ((), ())), preferred_element_type=F32)


def iota(axis):
    return lax.broadcasted_iota(jnp.int32, (128, 128), axis)


def one_if(condition, dtype=BF16):
    return jnp.where(condition, 1.0, 0.0).astype(dtype)


def routing_kernel(plane_of, info, *refs):
    planes, (tables, slot_gate) = refs[:2], refs[2:]
    slot, col = iota(0), iota(1)
    slot_block = (slot & 63) >> 2
    rank_of = (slot & 3).astype(F32)
    expert = ((slot >> 6) + info[2:3, :]).astype(F32)
    lane, sub = col, col & 7
    before = one_if(slot < col)
    is_token = lane < TOK
    spreads = [
        one_if(slot == sub),
        one_if((sub < 4) & (slot == sub + 8)),
        one_if((sub >= 4) & (slot == sub + 4)),
    ]
    block = col >> 3
    steps = one_if(block == slot_block, F32)
    for group in range(8):
        half, g = divmod(group, 4)
        mine = info[half : half + 1, :] == slot_block
        meta = planes[half][plane_rows(plane_of, group), :]
        has = code = total = jnp.zeros((128, 128), F32)
        for k in range(8):
            value = dot(one_if(mine & (sub == k)), meta, 1, 0)
            codes = pltpu.roll(value, 128 - 16, 1)
            hit = one_if((value == expert) & is_token, F32)
            has = has + hit
            code = code + hit * codes
            total = total + codes
        rank = dot(has.astype(BF16), before, 1, 0)
        place = jnp.where(rank == rank_of, has, 0.0)
        number = jnp.sum(place * code, axis=1, keepdims=True)
        over = jnp.sum(place * total, axis=1, keepdims=True)
        gate = jnp.where(over > 0.0, number / jnp.maximum(over, 1.0), 0.0)
        slot_gate[pl.ds(group * 64, 64), :] = gate[:64]
        slot_gate[pl.ds(512 + group * 64, 64), :] = gate[64:]
        head, left, right = (dot(place.astype(BF16), s, 1, 0) for s in spreads)
        here = one_if(mine, F32)
        for i, (t, m) in enumerate(
            ((head, here), (left, here), (right, here), (left, steps), (right, steps))
        ):
            tables[i, group] = (t * m).astype(BF16)


def plane_rows(plane_of, group):
    return pl.ds(pl.multiple_of(plane_of[group] * 128, 128), 128)


def place_group(tables, group, heads, tail, out_ref, at):
    for lr in range(2):
        rows = dot(tables[0, group], heads[lr], 1, 0) + dot(tables[at[lr], group], tail, 1, 0)
        rows = rows.astype(BF16)
        out_ref[lr, pl.ds(group * 64, 64), :] = rows[:64]
        out_ref[lr, pl.ds(512 + group * 64, 64), :] = rows[64:]


def grads_kernel(plane_of, tables, *refs):
    planes, down = refs[:6], refs[6:8]
    rows, hidden_grad, total = refs[8:]
    step = pl.program_id(0)

    @pl.when(step == 0)
    def _():
        total[...] = jnp.zeros_like(total)

    for group in range(8):
        at = plane_rows(plane_of, group)
        left, right, tail = (planes[2 * p + group // 4][at, :] for p in range(3))
        place_group(tables, group, (left, right), tail, rows, (1, 2))
    for e in range(2):
        at = pl.ds(e * 512, 512)
        total[at, :] += dot(rows[0, at, :], down[0][e], 1, 1) + dot(rows[1, at, :], down[1][e], 1, 1)

    @pl.when(step == pl.num_programs(0) - 1)
    def _():
        hidden_grad[...] = total[...]


def rows_kernel(plane_of, tables, *refs):
    wholes, planes = refs[:4], refs[4:12]
    gate, up = refs[12:14], refs[14:16]
    hidden_grad, slot_gate = refs[16:18]
    rows, hidden, gate_grad, up_grad, gate_total, up_total = refs[18:]
    step = pl.program_id(0)

    @pl.when(step == 0)
    def _():
        gate_total[...] = jnp.zeros_like(gate_total)
        up_total[...] = jnp.zeros_like(up_total)

    for group in range(8):
        half, g = divmod(group, 4)
        at = plane_rows(plane_of, group)
        heads = [wholes[2 * lr + half][at, :] for lr in range(2)]
        pick = pl.ds(g * 32, 32)
        tail = jnp.concatenate([ref[pick, :] for ref in planes[half * 4 : half * 4 + 4]], axis=0)
        place_group(tables, group, heads, tail, rows, (3, 4))
    for e in range(2):
        at = pl.ds(e * 512, 512)
        left, right = rows[0, at, :], rows[1, at, :]
        gate_total[at, :] += dot(left, gate[0][e], 1, 1) + dot(right, gate[1][e], 1, 1)
        up_total[at, :] += dot(left, up[0][e], 1, 1) + dot(right, up[1][e], 1, 1)

    @pl.when(step == pl.num_programs(0) - 1)
    def _():
        for i in range(8):
            at = pl.ds(i * 128, 128)
            gate_act, up_act = gate_total[at, :], up_total[at, :]
            scale = slot_gate[at, :]
            back = hidden_grad[at, :] * scale
            s = 1.0 / (1.0 + jnp.exp(-gate_act))
            silu = gate_act * s
            hidden[at, :] = (silu * up_act * scale).astype(BF16)
            up_grad[at, :] = (back * silu).astype(BF16)
            gate_grad[at, :] = (back * up_act * s * (1.0 + gate_act * (1.0 - s))).astype(BF16)


def both_experts(slots, lr, group):
    return jnp.concatenate(
        [slots[lr, pl.ds(group * 64, 64), :], slots[lr, pl.ds(512 + group * 64, 64), :]], axis=0
    )


def combine_kernel(steps, terms, plane_of, tables, *refs):
    acts, weights = refs[:terms], refs[terms : 2 * terms]
    wholes, planes, slots = refs[2 * terms : 2 * terms + 2], refs[2 * terms + 2 : -1], refs[-1]
    step = pl.program_id(0)

    @pl.when(step < 2 * steps)
    def _():
        for e in range(2):
            pick = pl.ds(e * 512, 512)
            value = dot(acts[0][pick, :], weights[0][e], 1, 0)
            for i in range(1, terms):
                value = value + dot(acts[i][pick, :], weights[i][e], 1, 0)
            slots[step, pick, :] = value.astype(BF16)
        for group in range(8):
            value = dot(tables[0, group], both_experts(slots, step, group), 0, 0)
            wholes[group // 4][plane_rows(plane_of, group), :] = value.astype(BF16)

    @pl.when(step >= 2 * steps)
    def _():
        for group in range(8):
            half, g = divmod(group, 4)
            value = dot(tables[3, group], both_experts(slots, step - 2 * steps, group), 0, 0)
            value = value + dot(tables[4, group], both_experts(slots, step - steps, group), 0, 0)
            value = value.astype(BF16)
            for i in range(4):
                planes[half * 4 + i][pl.ds(g * 32, 32), :] = value[i * 32 : (i + 1) * 32]


def weight_grads_kernel(rows, grads, hidden, gate_grad, up_grad, gate_out, up_out, down_out):
    for e in range(2):
        at = pl.ds(e * 512, 512)
        x = rows[0, at, :]
        gate_out[e] = dot(gate_grad[at, :], x, 0, 0).astype(BF16)
        up_out[e] = dot(up_grad[at, :], x, 0, 0).astype(BF16)
        down_out[e] = dot(hidden[at, :], grads[0, at, :], 0, 0).astype(BF16)


def whole(shape):
    return pl.BlockSpec(shape, lambda *_: (0,) * len(shape))


def params():
    return pltpu.CompilerParams(vmem_limit_bytes=VMEM_LIMIT)


def chunk_of(half):
    return min(512, half)


def flat_planes(planes):
    return [v for part in planes for half in part for v in half]


def weight_specs(weight, chunk, steps):
    shape = (weight.shape[0], weight.shape[1], chunk)
    return [
        pl.BlockSpec(shape, lambda n: (0, 0, n)),
        pl.BlockSpec(shape, lambda n, steps=steps: (0, 0, n + steps)),
    ]


def scalars():
    return pl.BlockSpec(memory_space=pltpu.SMEM)


def routing(plane_of, info, planes, width):
    return pl.pallas_call(
        routing_kernel,
        grid=(1,),
        in_specs=[scalars(), whole((8, 128))]
        + [pl.BlockSpec((512, 128), lambda n: (0, width // 128))] * 2,
        out_specs=[whole((5, 8, 128, 128)), whole((1024, 1))],
        out_shape=[
            jax.ShapeDtypeStruct((5, 8, 128, 128), BF16),
            jax.ShapeDtypeStruct((1024, 1), F32),
        ],
        compiler_params=params(),
        cost_estimate=pl.CostEstimate(flops=10**9, bytes_accessed=10**7, transcendentals=0),
    )(plane_of, info, *planes)


def dispatch_grads(plane_of, tables, planes, down):
    width, half = down.shape[1], down.shape[2] // 2
    chunk = chunk_of(half)
    steps = half // chunk
    specs = []
    for p in range(3):
        specs += [pl.BlockSpec((512, chunk), lambda n, p=p: (0, n + p * steps))] * 2
    return pl.pallas_call(
        grads_kernel,
        grid=(steps,),
        in_specs=[scalars(), whole(tables.shape)] + specs + weight_specs(down, chunk, steps),
        out_specs=[pl.BlockSpec((2, 1024, chunk), lambda n: (0, 0, n)), whole((1024, width))],
        out_shape=[
            jax.ShapeDtypeStruct((2, 1024, half), BF16),
            jax.ShapeDtypeStruct((1024, width), F32),
        ],
        scratch_shapes=[pltpu.VMEM((1024, width), F32)],
        compiler_params=params(),
        cost_estimate=pl.CostEstimate(flops=8 * 10**9, bytes_accessed=30 * 10**6, transcendentals=0),
    )(plane_of, tables, *(planes * 3), down, down)


def dispatch_rows(plane_of, tables, wholes, planes, gate, up, hidden_grad, slot_gate):
    width, half = gate.shape[1], gate.shape[2] // 2
    chunk = chunk_of(half)
    steps = half // chunk
    small = jax.ShapeDtypeStruct((1024, width), BF16)
    left = pl.BlockSpec((512, chunk), lambda n: (0, n))
    right = pl.BlockSpec((512, chunk), lambda n: (0, n + steps))
    return pl.pallas_call(
        rows_kernel,
        grid=(steps,),
        in_specs=[scalars(), whole(tables.shape), left, left, right, right]
        + [pl.BlockSpec((128, chunk), lambda n: (0, n))] * 8
        + weight_specs(gate, chunk, steps)
        + weight_specs(up, chunk, steps)
        + [whole((1024, width)), whole((1024, 1))],
        out_specs=[pl.BlockSpec((2, 1024, chunk), lambda n: (0, 0, n))] + [whole((1024, width))] * 3,
        out_shape=[jax.ShapeDtypeStruct((2, 1024, half), BF16), small, small, small],
        scratch_shapes=[pltpu.VMEM((1024, width), F32)] * 2,
        compiler_params=params(),
        cost_estimate=pl.CostEstimate(flops=10**10, bytes_accessed=30 * 10**6, transcendentals=0),
    )(plane_of, tables, *wholes, *wholes, *planes, gate, gate, up, up, hidden_grad, slot_gate)


def combine(plane_of, tables, acts, weights):
    width, half = weights[0].shape[1], weights[0].shape[2] // 2
    chunk = chunk_of(half)
    steps = half // chunk
    heads = lambda n: jnp.minimum(n, 2 * steps - 1)
    tails = lambda n: jnp.maximum(n - 2 * steps, 0)
    outs = pl.pallas_call(
        functools.partial(combine_kernel, steps, len(acts)),
        grid=(3 * steps,),
        in_specs=[scalars(), whole(tables.shape)]
        + [whole((1024, width))] * len(acts)
        + [pl.BlockSpec((2, width, chunk), lambda n: (0, 0, heads(n)))] * len(acts),
        out_specs=[pl.BlockSpec((512, chunk), lambda n: (0, heads(n)))] * 2
        + [pl.BlockSpec((128, chunk), lambda n: (0, tails(n)))] * 8,
        out_shape=[jax.ShapeDtypeStruct((512, 2 * half), BF16)] * 2
        + [jax.ShapeDtypeStruct((128, half), BF16)] * 8,
        scratch_shapes=[pltpu.VMEM((2 * steps, 1024, chunk), BF16)],
        compiler_params=params(),
        cost_estimate=pl.CostEstimate(flops=8 * 10**9, bytes_accessed=30 * 10**6, transcendentals=0),
    )(plane_of, tables, *acts, *weights)
    return outs[:2], outs[2:6], outs[6:]


def weight_grads(rows, grads, hidden, gate_grad, up_grad):
    width, half = hidden.shape[1], rows.shape[2]
    chunk = chunk_of(half)
    steps = half // chunk
    out = jax.ShapeDtypeStruct((2, width, 2 * half), BF16)
    return pl.pallas_call(
        weight_grads_kernel,
        grid=(2, steps),
        in_specs=[pl.BlockSpec((1, 1024, chunk), lambda i, n: (i, 0, n))] * 2 + [whole((1024, width))] * 3,
        out_specs=[pl.BlockSpec((2, width, chunk), lambda i, n: (0, 0, i * steps + n))] * 3,
        out_shape=[out] * 3,
        compiler_params=params(),
        cost_estimate=pl.CostEstimate(flops=8 * 10**9, bytes_accessed=30 * 10**6, transcendentals=0),
    )(rows, grads, hidden, gate_grad, up_grad)


def on_device(
    context, out_proj, residual, norm_gain, gate_weight, up_weight, down_weight, expert_ids, gate_codes, cotangent
):
    width = residual.shape[1]
    half = width // 2
    x, zl, core = lax.axis_index("x"), lax.axis_index("zl"), lax.axis_index("core")
    tp = (x * 2 + zl) * 2 + core

    meta = jnp.concatenate(
        [
            jnp.pad(expert_ids.T.astype(BF16), ((0, 0), (0, 4))),
            jnp.pad(gate_codes.T.astype(BF16), ((0, 0), (0, 128 - 16 - TOK))),
        ],
        axis=1,
    )
    cot = pack(cotangent)
    order = np.arange(16)
    h, j, k = order // 8, (order // 2) % 4, order % 2
    sign = (1 - 2 * core) * jnp.asarray(1 - 2 * h)
    owner = (((x - j * sign) % 4) * 2 + (zl ^ jnp.asarray(k))) * 2 + (core ^ jnp.asarray(h))
    lane = np.arange(8)
    head_row = (owner[:, None] * TOK + lane[None, :]).reshape(128)
    tail_row = (owner[:, None] * TOK + 8 + (lane % 4)[None, :]).reshape(128)
    token = jnp.arange(16 * TOK)
    picked = (jnp.concatenate([head_row, tail_row])[:, None] == token[None, :]).astype(BF16)
    ordered = jnp.dot(picked, context, preferred_element_type=F32).astype(BF16)
    partial = jnp.dot(ordered, out_proj, preferred_element_type=F32).astype(BF16)
    cot_steps = around(jnp.concatenate(cot + [meta], axis=1), "z", partial)
    first = jnp.asarray((np.arange(128) % 8 < 4)[:, None])
    tail = jnp.where(first, partial[128:, :half], partial[128:, half:])
    partial = jnp.concatenate([partial[:128], tail], axis=1).reshape(2, 8, 8, 3 * half)
    summed = (partial[0].astype(F32) + send(partial[1], SWAP).astype(F32)).astype(BF16)
    cot_own = gather_whole(after(jnp.concatenate(cot_steps, axis=0), summed))
    attended = summed[0].astype(F32)
    for j in range(4):
        for k in range(2):
            if j or k:
                attended = attended + send(summed[2 * j + k], tp_shifted(-j, k)).astype(F32)

    split = lambda v: [v[:, i * half : (i + 1) * half] for i in range(3)]
    stream = [r.astype(F32) + a for r, a in zip(pack(residual), split(attended))]
    inverse = [
        lax.rsqrt(s / width + EPSILON) for s in row_sums([s * s for s in stream])
    ]
    upper = jnp.asarray((np.arange(8) < 4)[:, None])
    gain = [
        norm_gain[None, :half],
        norm_gain[None, half:],
        jnp.where(upper, norm_gain[None, :half], norm_gain[None, half:]),
    ]
    inv = [inverse[0], inverse[0], inverse[1]]
    normed = [(s * i * g).astype(BF16) for s, i, g in zip(stream, inv, gain)]
    row_heads = jnp.concatenate(around(jnp.concatenate(normed[:2], axis=1), "z"), axis=0)
    cot_own, row_heads = lax.optimization_barrier((cot_own, row_heads))
    row_own = gather_whole(row_heads)
    row_planes = [gather_plane(normed[2])]
    row_planes.append(send(row_planes[0], shifted("z", 1)))
    cot_own = after(cot_own, row_planes[0])
    cot_planes = (cot_own, send(cot_own, SWAP))
    row_planes[1] = after(row_planes[1], cot_planes[1])
    row_planes.append(send(row_planes[1], shifted("z", 1)))

    y = lax.axis_index("y")
    block = np.arange(128) // 8
    turn = (1 - 2 * core) * jnp.asarray([[1], [-1]])
    steps_to = (block % 4) * 4 + ((x - block // 4) * turn) % 4
    info = jnp.concatenate([steps_to, jnp.full((6, 128), 2 * tp)], axis=0).astype(jnp.int32)
    plane_of = ((y - jnp.arange(4) * turn) % 4).reshape(8).astype(jnp.int32)
    tables, slot_gate = routing(plane_of, info, cot_planes, 3 * half)

    grad_rows, hidden_grad = dispatch_grads(plane_of, tables, cot_planes, down_weight)
    row_planes[2] = after(row_planes[2], tables)
    row_planes.append(after(send(row_planes[2], shifted("z", 1)), hidden_grad))
    row_own = after(row_own, row_planes[3])
    row_planes = row_planes + [send(v, SWAP) for v in row_planes]
    rows, hidden, gate_grad, up_grad = dispatch_rows(
        plane_of, tables, (row_own, send(row_own, SWAP)), row_planes, gate_weight, up_weight, hidden_grad, slot_gate
    )
    back_wholes, back_own, back_sib = combine(
        plane_of, tables, [gate_grad, up_grad], [gate_weight, up_weight]
    )
    back_sum = add_swapped(*back_wholes)
    out_wholes, out_own, out_sib = combine(plane_of, tables, [after(hidden, back_sum)], [down_weight])
    out_sum = add_swapped(*out_wholes)
    gate_out, up_out, down_out = weight_grads(
        rows, grad_rows, after(hidden, out_own[0]), gate_grad, up_grad
    )
    back_heads = scatter_whole(back_sum)
    back_tail = scatter_planes(back_own, back_sib, (None, out_own[0], gate_out, out_sum))
    out_heads = scatter_whole(out_sum)
    out_tail = scatter_planes([after(v, back_tail) for v in out_own], [after(v, back_tail) for v in out_sib])
    back_heads = finish_whole(back_heads)
    back = [back_heads[:, :half], back_heads[:, half:], finish_planes(back_tail)]

    scaled = [b * g for b, g in zip(back, gain)]
    inner = [s / width for s in row_sums([a * b for a, b in zip(scaled, stream)])]
    inner = [inner[0], inner[0], inner[1]]
    grad = [
        (c.astype(F32) + i * s - st * (i * i * i) * m).astype(BF16)
        for c, i, s, st, m in zip(cot, inv, scaled, stream, inner)
    ]
    residual_grad = unpack(grad)

    packed = jnp.concatenate(grad, axis=1)
    own = [packed if not (j or k) else send(packed, tp_shifted(j, k)) for j in range(4) for k in range(2)]
    own = jnp.concatenate(own, axis=0)
    out_tail = finish_planes(after(out_tail, packed))
    out_heads = finish_whole(after(out_heads, own))
    mixture = [out_heads[:, :half], out_heads[:, half:], out_tail]
    output = unpack([(s + m).astype(BF16) for s, m in zip(stream, mixture)])
    both = jnp.concatenate([own, send(own, SWAP)], axis=0)
    is_head = (token[:, None] == head_row[None, :]).astype(BF16)
    is_tail = (token[:, None] == tail_row[None, :]).astype(BF16)
    upper_cols = jnp.asarray(np.arange(128) % 8 < 4)[None, :]
    heads = jnp.dot(is_head, both[:, : 2 * half], preferred_element_type=F32)
    tails = [
        jnp.dot(jnp.where(pick, is_tail, 0).astype(BF16), both[:, 2 * half :], preferred_element_type=F32)
        for pick in (upper_cols, ~upper_cols)
    ]
    full = (heads + jnp.concatenate(tails, axis=1)).astype(BF16)
    context_grad = jnp.einsum("td,ad->ta", full, out_proj, preferred_element_type=F32).astype(BF16)
    return (output, residual_grad, context_grad, gate_out, up_out, down_out)


def solution(mesh):
    fine = Mesh(np.asarray(mesh.devices).reshape(2, 4, 4, 2, 2), AXES)
    ctx, tp = AXES[:2], AXES[2:]
    rows = P(AXES, None)
    experts = P(tp, ctx, None)
    return jax.shard_map(
        on_device,
        mesh=fine,
        in_specs=(P(ctx, tp), P(tp, None), rows, P(), experts, experts, experts, rows, rows, rows),
        out_specs=(rows, rows, P(ctx, tp), experts, experts, experts),
        check_vma=False,
    )
```

```python
import functools

import numpy as np
import jax
import jax.numpy as jnp
from jax import lax
from jax.experimental import pallas as pl
from jax.experimental.pallas import tpu as pltpu
from jax.sharding import Mesh, PartitionSpec as P

AXES = ("zh", "y", "x", "zl", "core")
CAP = 4
TOK = 12
EPSILON = 1e-06
BF16 = jnp.bfloat16
F32 = jnp.float32
VMEM_LIMIT = 50 * 1024 * 1024


def flat_index(z, y, x, core):
    return ((((z // 2) * 4 + y) * 4 + x) * 2 + z % 2) * 2 + core


def permutation(move):
    return [
        (flat_index(z, y, x, c), flat_index(*move(z, y, x, c)))
        for z in range(4)
        for y in range(4)
        for x in range(4)
        for c in range(2)
    ]


def shifted(axis, steps):
    def move(z, y, x, c):
        d = steps * (1 - 2 * c)
        if axis == "x":
            return z, y, (x + d) % 4, c
        if axis == "y":
            return z, (y + d) % 4, x, c
        return (z + d) % 4, y, x, c

    return permutation(move)


def tp_shifted(steps, flip):
    return permutation(lambda z, y, x, c: (z ^ flip, y, (x + steps * (1 - 2 * c)) % 4, c))


SWAP = permutation(lambda z, y, x, c: (z, y, x, 1 - c))
ORDERS = (("x", "y", "z"), ("y", "z", "x"), ("z", "x", "y"))


def send(v, pairs):
    return lax.ppermute(v, AXES, pairs)


def after(v, first):
    return lax.optimization_barrier((v, first))[0]


def around(v, axis):
    up = send(v, shifted(axis, 1))
    down = send(v, shifted(axis, -1))
    return [v, up, send(up, shifted(axis, 1)), down]


def around_sum(blocks, axis):
    chain = (blocks[3].astype(F32) + send(blocks[2], shifted(axis, 1)).astype(F32)).astype(BF16)
    direct = send(blocks[1], shifted(axis, -1)).astype(F32)
    return blocks[0].astype(F32) + direct + send(chain, shifted(axis, 1)).astype(F32)


def full_ring(v, axis):
    out = [v]
    for _ in range(3):
        out.append(send(out[-1], shifted(axis, 1)))
    return out


def gather_plane(part, order):
    a, b, c = order
    width = part.shape[-1]
    one = jnp.stack(full_ring(part, a))
    two = jnp.stack(full_ring(one, b), axis=0 if a == "x" else 1)
    return two.reshape(128, width)


def ring_sum(blocks, axis):
    t = blocks[1]
    for d in (2, 3, 0):
        v = blocks[d].astype(F32) + send(t, shifted(axis, 1)).astype(F32)
        t = v.astype(BF16)
    return v


def scatter_parts(own, sib, beside):
    width = own[0].shape[-1]
    arrived = {j: send(sib[j], SWAP) for j in (1, 2, 3, 0)}
    t = [None] * 3
    for j in (1, 2, 3, 0):
        other = beside[j](t) if j in beside else None
        for p, order in enumerate(ORDERS):
            v = own[j][p].astype(F32) + arrived[j][p].astype(F32)
            if t[p] is not None:
                v = v + send(t[p], shifted(order[2], 1)).astype(F32)
            t[p] = v.astype(BF16)
        if other is not None:
            t = after(t, other)
    sums = []
    for v, (a, b, _) in zip(t, ORDERS):
        at = 0 if a == "x" else 1
        v = v.reshape(4, 4, 8, width)
        v = ring_sum([lax.index_in_dim(v, d, at, False) for d in range(4)], b).astype(BF16)
        sums.append(ring_sum([v[d] for d in range(4)], a))
    return sums


def add_swapped(own, sib):
    return (own.astype(F32) + send(sib, SWAP).astype(F32)).astype(BF16)


def scatter_whole(t):
    t = lax.psum_scatter(t, ("y", "x"), scatter_dimension=0, tiled=True)
    t = around_sum([t[8 * d : 8 * d + 8] for d in range(4)], "z")
    width = t.shape[1] // 3
    return [t[:, i * width : (i + 1) * width] for i in range(3)]


def pack(rows):
    half = rows.shape[1] // 2
    tail = rows[8:]
    return [rows[:8, :half], rows[:8, half:], jnp.concatenate([tail[:, :half], tail[:, half:]], axis=0)]


def unpack(parts):
    left, right, tail = parts
    return jnp.concatenate(
        [
            jnp.concatenate([left, right], axis=1),
            jnp.concatenate([tail[:4], tail[4:]], axis=1),
        ],
        axis=0,
    )


def row_sums(products):
    head = jnp.sum(products[0], axis=1, keepdims=True) + jnp.sum(products[1], axis=1, keepdims=True)
    tail = jnp.sum(products[2], axis=1, keepdims=True)
    return head, tail + jnp.concatenate([tail[4:], tail[:4]], axis=0)


def dot(a, b, ca, cb):
    return lax.dot_general(a, b, (((ca,), (cb,)), ((), ())), preferred_element_type=F32)


def iota(axis):
    return lax.broadcasted_iota(jnp.int32, (128, 128), axis)


def one_if(condition, dtype=BF16):
    return jnp.where(condition, 1.0, 0.0).astype(dtype)


def routing_kernel(plane_of, info, *refs):
    planes, (tables, slot_gate) = refs[:2], refs[2:]
    slot, col = iota(0), iota(1)
    slot_block = (slot & 63) >> 2
    rank_of = (slot & 3).astype(F32)
    expert = ((slot >> 6) + info[2:3, :]).astype(F32)
    lane, sub = col, col & 7
    before = one_if(slot < col)
    is_token = lane < TOK
    spreads = [
        one_if(slot == sub),
        one_if((sub < 4) & (slot == sub + 8)),
        one_if((sub >= 4) & (slot == sub + 4)),
    ]
    block = col >> 3
    zx = one_if(block == slot_block, F32)
    xz = one_if((((block & 3) << 2) + (block >> 2)) == slot_block, F32)
    for group in range(8):
        half, g = divmod(group, 4)
        mine = info[half : half + 1, :] == slot_block
        meta = planes[half][plane_rows(plane_of, group), :]
        has = code = total = jnp.zeros((128, 128), F32)
        for k in range(8):
            value = dot(one_if(mine & (sub == k)), meta, 1, 0)
            codes = pltpu.roll(value, 128 - 16, 1)
            hit = one_if((value == expert) & is_token, F32)
            has = has + hit
            code = code + hit * codes
            total = total + codes
        rank = dot(has.astype(BF16), before, 1, 0)
        place = jnp.where(rank == rank_of, has, 0.0)
        number = jnp.sum(place * code, axis=1, keepdims=True)
        over = jnp.sum(place * total, axis=1, keepdims=True)
        gate = jnp.where(over > 0.0, number / jnp.maximum(over, 1.0), 0.0)
        slot_gate[pl.ds(group * 64, 64), :] = gate[:64]
        slot_gate[pl.ds(512 + group * 64, 64), :] = gate[64:]
        head, left, right = (dot(place.astype(BF16), s, 1, 0) for s in spreads)
        here = one_if(mine, F32)
        for i, (t, m) in enumerate(
            ((head, zx), (head, xz), (left, zx), (right, zx), (head, here), (left, here), (right, here))
        ):
            tables[i, group] = (t * m).astype(BF16)


def plane_rows(plane_of, group):
    return pl.ds(pl.multiple_of(plane_of[group] * 128, 128), 128)


def place_group(tables, group, heads, tail, out_ref, at):
    for lr in range(2):
        rows = dot(tables[at[lr], group], heads[lr], 1, 0) + dot(tables[at[2 + lr], group], tail, 1, 0)
        rows = rows.astype(BF16)
        out_ref[lr, pl.ds(group * 64, 64), :] = rows[:64]
        out_ref[lr, pl.ds(512 + group * 64, 64), :] = rows[64:]


def grads_kernel(plane_of, tables, *refs):
    planes, down = refs[:6], refs[6:8]
    rows, hidden_grad, total = refs[8:]
    step = pl.program_id(0)

    @pl.when(step == 0)
    def _():
        total[...] = jnp.zeros_like(total)

    for group in range(8):
        at = plane_rows(plane_of, group)
        left, right, tail = (planes[2 * p + group // 4][at, :] for p in range(3))
        place_group(tables, group, (left, right), tail, rows, (4, 4, 5, 6))
    for e in range(2):
        at = pl.ds(e * 512, 512)
        total[at, :] += dot(rows[0, at, :], down[0][e], 1, 1) + dot(rows[1, at, :], down[1][e], 1, 1)

    @pl.when(step == pl.num_programs(0) - 1)
    def _():
        hidden_grad[...] = total[...]


def rows_kernel(*refs):
    tables, planes = refs[0], refs[1:25]
    gate, up = refs[25:27], refs[27:29]
    hidden_grad, slot_gate = refs[29:31]
    rows, hidden, gate_grad, up_grad, gate_total, up_total = refs[31:]
    step = pl.program_id(0)

    @pl.when(step == 0)
    def _():
        gate_total[...] = jnp.zeros_like(gate_total)
        up_total[...] = jnp.zeros_like(up_total)

    for group in range(8):
        half, g = divmod(group, 4)
        zs, xs, ys = (planes[p * 8 + half * 4 : p * 8 + half * 4 + 4] for p in range(3))
        pick = pl.ds(g * 32, 32)
        left = jnp.concatenate([ref[pick, :] for ref in zs], axis=0)
        right = jnp.concatenate([ref[pick, :] for ref in xs], axis=0)
        place_group(tables, group, (left, right), ys[g][...], rows, (0, 1, 2, 3))
    for e in range(2):
        at = pl.ds(e * 512, 512)
        left, right = rows[0, at, :], rows[1, at, :]
        gate_total[at, :] += dot(left, gate[0][e], 1, 1) + dot(right, gate[1][e], 1, 1)
        up_total[at, :] += dot(left, up[0][e], 1, 1) + dot(right, up[1][e], 1, 1)

    @pl.when(step == pl.num_programs(0) - 1)
    def _():
        for i in range(8):
            at = pl.ds(i * 128, 128)
            gate_act, up_act = gate_total[at, :], up_total[at, :]
            scale = slot_gate[at, :]
            back = hidden_grad[at, :] * scale
            s = 1.0 / (1.0 + jnp.exp(-gate_act))
            silu = gate_act * s
            hidden[at, :] = (silu * up_act * scale).astype(BF16)
            up_grad[at, :] = (back * silu).astype(BF16)
            gate_grad[at, :] = (back * up_act * s * (1.0 + gate_act * (1.0 - s))).astype(BF16)


def both_experts(slots, lr, group):
    return jnp.concatenate(
        [slots[lr, pl.ds(group * 64, 64), :], slots[lr, pl.ds(512 + group * 64, 64), :]], axis=0
    )


def back_kernel(tables, gate_grad, up_grad, *refs):
    gate, up, outs, slots = refs[:2], refs[2:4], refs[4:-1], refs[-1]
    for lr in range(2):
        for e in range(2):
            pick = pl.ds(e * 512, 512)
            value = dot(gate_grad[pick, :], gate[lr][e], 1, 0) + dot(up_grad[pick, :], up[lr][e], 1, 0)
            slots[lr, pick, :] = value.astype(BF16)
    for group in range(8):
        half, g = divmod(group, 4)
        out = outs[half * 4 : half * 4 + 4]
        left, right = (both_experts(slots, lr, group) for lr in range(2))
        head_left = dot(tables[0, group], left, 0, 0).astype(BF16)
        head_right = dot(tables[1, group], right, 0, 0).astype(BF16)
        tail = dot(tables[2, group], left, 0, 0) + dot(tables[3, group], right, 0, 0)
        for i in range(4):
            out[i][0, pl.ds(g * 32, 32), :] = head_left[i * 32 : (i + 1) * 32]
            out[i][1, pl.ds(g * 32, 32), :] = head_right[i * 32 : (i + 1) * 32]
        out[g][2] = tail.astype(BF16)


def out_kernel(steps, plane_of, tables, hidden, down, own, sib, slots):
    step = pl.program_id(0)
    outs = (own, sib)

    @pl.when(step < 2 * steps)
    def _():
        for e in range(2):
            pick = pl.ds(e * 512, 512)
            slots[step, pick, :] = dot(hidden[pick, :], down[e], 1, 0).astype(BF16)
        for group in range(8):
            value = dot(tables[4, group], both_experts(slots, step, group), 0, 0)
            outs[group // 4][plane_rows(plane_of, group), :] = value.astype(BF16)

    @pl.when(step >= 2 * steps)
    def _():
        for group in range(8):
            value = dot(tables[5, group], both_experts(slots, step - 2 * steps, group), 0, 0)
            value = value + dot(tables[6, group], both_experts(slots, step - steps, group), 0, 0)
            outs[group // 4][plane_rows(plane_of, group), :] = value.astype(BF16)


def weight_grads_kernel(rows, grads, hidden, gate_grad, up_grad, gate_out, up_out, down_out):
    for e in range(2):
        at = pl.ds(e * 512, 512)
        x = rows[0, at, :]
        gate_out[e] = dot(gate_grad[at, :], x, 0, 0).astype(BF16)
        up_out[e] = dot(up_grad[at, :], x, 0, 0).astype(BF16)
        down_out[e] = dot(hidden[at, :], grads[0, at, :], 0, 0).astype(BF16)


def whole(shape):
    return pl.BlockSpec(shape, lambda *_: (0,) * len(shape))


def params():
    return pltpu.CompilerParams(vmem_limit_bytes=VMEM_LIMIT)


def chunk_of(half):
    return min(512, half)


def flat_planes(planes):
    return [v for part in planes for half in part for v in half]


def weight_specs(weight, chunk, steps):
    shape = (weight.shape[0], weight.shape[1], chunk)
    return [
        pl.BlockSpec(shape, lambda n: (0, 0, n)),
        pl.BlockSpec(shape, lambda n, steps=steps: (0, 0, n + steps)),
    ]


def scalars():
    return pl.BlockSpec(memory_space=pltpu.SMEM)


def routing(plane_of, info, planes, width):
    return pl.pallas_call(
        routing_kernel,
        grid=(1,),
        in_specs=[scalars(), whole((8, 128))]
        + [pl.BlockSpec((512, 128), lambda n: (0, width // 128))] * 2,
        out_specs=[whole((7, 8, 128, 128)), whole((1024, 1))],
        out_shape=[
            jax.ShapeDtypeStruct((7, 8, 128, 128), BF16),
            jax.ShapeDtypeStruct((1024, 1), F32),
        ],
        compiler_params=params(),
        cost_estimate=pl.CostEstimate(flops=10**9, bytes_accessed=10**7, transcendentals=0),
    )(plane_of, info, *planes)


def dispatch_grads(plane_of, tables, planes, down):
    width, half = down.shape[1], down.shape[2] // 2
    chunk = chunk_of(half)
    steps = half // chunk
    specs = []
    for p in range(3):
        specs += [pl.BlockSpec((512, chunk), lambda n, p=p: (0, n + p * steps))] * 2
    return pl.pallas_call(
        grads_kernel,
        grid=(steps,),
        in_specs=[scalars(), whole(tables.shape)] + specs + weight_specs(down, chunk, steps),
        out_specs=[pl.BlockSpec((2, 1024, chunk), lambda n: (0, 0, n)), whole((1024, width))],
        out_shape=[
            jax.ShapeDtypeStruct((2, 1024, half), BF16),
            jax.ShapeDtypeStruct((1024, width), F32),
        ],
        scratch_shapes=[pltpu.VMEM((1024, width), F32)],
        compiler_params=params(),
        cost_estimate=pl.CostEstimate(flops=8 * 10**9, bytes_accessed=30 * 10**6, transcendentals=0),
    )(plane_of, tables, *(planes * 3), down, down)


def dispatch_rows(tables, planes, gate, up, hidden_grad, slot_gate):
    width, half = gate.shape[1], gate.shape[2] // 2
    chunk = chunk_of(half)
    steps = half // chunk
    small = jax.ShapeDtypeStruct((1024, width), BF16)
    return pl.pallas_call(
        rows_kernel,
        grid=(steps,),
        in_specs=[whole(tables.shape)]
        + [pl.BlockSpec((128, chunk), lambda n: (0, n))] * 24
        + weight_specs(gate, chunk, steps)
        + weight_specs(up, chunk, steps)
        + [whole((1024, width)), whole((1024, 1))],
        out_specs=[pl.BlockSpec((2, 1024, chunk), lambda n: (0, 0, n))] + [whole((1024, width))] * 3,
        out_shape=[jax.ShapeDtypeStruct((2, 1024, half), BF16), small, small, small],
        scratch_shapes=[pltpu.VMEM((1024, width), F32)] * 2,
        compiler_params=params(),
        cost_estimate=pl.CostEstimate(flops=10**10, bytes_accessed=30 * 10**6, transcendentals=0),
    )(tables, *flat_planes(planes), gate, gate, up, up, hidden_grad, slot_gate)


def combine_back(tables, gate_grad, up_grad, gate, up):
    width, half = gate.shape[1], gate.shape[2] // 2
    chunk = chunk_of(half)
    steps = half // chunk
    out = jax.ShapeDtypeStruct((3, 128, half), BF16)
    outs = pl.pallas_call(
        back_kernel,
        grid=(steps,),
        in_specs=[whole(tables.shape)]
        + [whole((1024, width))] * 2
        + weight_specs(gate, chunk, steps)
        + weight_specs(up, chunk, steps),
        out_specs=[pl.BlockSpec((3, 128, chunk), lambda n: (0, 0, n))] * 8,
        out_shape=[out] * 8,
        scratch_shapes=[pltpu.VMEM((2, 1024, chunk), BF16)],
        compiler_params=params(),
        cost_estimate=pl.CostEstimate(flops=8 * 10**9, bytes_accessed=30 * 10**6, transcendentals=0),
    )(tables, gate_grad, up_grad, gate, gate, up, up)
    return outs[:4], outs[4:]


def combine_out(plane_of, tables, hidden, down):
    width, half = down.shape[1], down.shape[2] // 2
    chunk = chunk_of(half)
    steps = half // chunk
    out = jax.ShapeDtypeStruct((512, 3 * half), BF16)
    return pl.pallas_call(
        functools.partial(out_kernel, steps),
        grid=(3 * steps,),
        in_specs=[
            scalars(),
            whole(tables.shape),
            whole((1024, width)),
            pl.BlockSpec((2, width, chunk), lambda n: (0, 0, jnp.minimum(n, 2 * steps - 1))),
        ],
        out_specs=[pl.BlockSpec((512, chunk), lambda n: (0, n))] * 2,
        out_shape=[out] * 2,
        scratch_shapes=[pltpu.VMEM((2 * steps, 1024, chunk), BF16)],
        compiler_params=params(),
        cost_estimate=pl.CostEstimate(flops=6 * 10**9, bytes_accessed=30 * 10**6, transcendentals=0),
    )(plane_of, tables, hidden, down)


def weight_grads(rows, grads, hidden, gate_grad, up_grad):
    width, half = hidden.shape[1], rows.shape[2]
    chunk = chunk_of(half)
    steps = half // chunk
    out = jax.ShapeDtypeStruct((2, width, 2 * half), BF16)
    return pl.pallas_call(
        weight_grads_kernel,
        grid=(2, steps),
        in_specs=[pl.BlockSpec((1, 1024, chunk), lambda i, n: (i, 0, n))] * 2 + [whole((1024, width))] * 3,
        out_specs=[pl.BlockSpec((2, width, chunk), lambda i, n: (0, 0, i * steps + n))] * 3,
        out_shape=[out] * 3,
        compiler_params=params(),
        cost_estimate=pl.CostEstimate(flops=8 * 10**9, bytes_accessed=30 * 10**6, transcendentals=0),
    )(rows, grads, hidden, gate_grad, up_grad)


def on_device(
    context, out_proj, residual, norm_gain, gate_weight, up_weight, down_weight, expert_ids, gate_codes, cotangent
):
    width = residual.shape[1]
    half = width // 2
    x, zl, core = lax.axis_index("x"), lax.axis_index("zl"), lax.axis_index("core")
    tp = (x * 2 + zl) * 2 + core

    meta = jnp.concatenate(
        [
            jnp.pad(expert_ids.T.astype(BF16), ((0, 0), (0, 4))),
            jnp.pad(gate_codes.T.astype(BF16), ((0, 0), (0, 128 - 16 - TOK))),
        ],
        axis=1,
    )
    cot = pack(cotangent)
    cot_own = jnp.concatenate(around(jnp.concatenate(cot + [meta], axis=1), "z"), axis=0)

    order = np.arange(16)
    h, j, k = order // 8, (order // 2) % 4, order % 2
    sign = (1 - 2 * core) * jnp.asarray(1 - 2 * h)
    owner = (((x - j * sign) % 4) * 2 + (zl ^ jnp.asarray(k))) * 2 + (core ^ jnp.asarray(h))
    lane = np.arange(8)
    head_row = (owner[:, None] * TOK + lane[None, :]).reshape(128)
    tail_row = (owner[:, None] * TOK + 8 + (lane % 4)[None, :]).reshape(128)
    token = jnp.arange(16 * TOK)
    picked = (jnp.concatenate([head_row, tail_row])[:, None] == token[None, :]).astype(BF16)
    ordered = jnp.dot(picked, context, preferred_element_type=F32).astype(BF16)
    partial = jnp.dot(ordered, out_proj, preferred_element_type=F32).astype(BF16)
    cot_own = after(cot_own, partial)
    cot_own = lax.all_gather(cot_own, ("y", "x"), axis=0, tiled=True)
    first = jnp.asarray((np.arange(128) % 8 < 4)[:, None])
    tail = jnp.where(first, partial[128:, :half], partial[128:, half:])
    partial = jnp.concatenate([partial[:128], tail], axis=1).reshape(2, 8, 8, 3 * half)
    summed = (partial[0].astype(F32) + send(partial[1], SWAP).astype(F32)).astype(BF16)
    attended = summed[0].astype(F32)
    for j in range(4):
        for k in range(2):
            if j or k:
                attended = attended + send(summed[2 * j + k], tp_shifted(-j, k)).astype(F32)

    split = lambda v: [v[:, i * half : (i + 1) * half] for i in range(3)]
    stream = [r.astype(F32) + a for r, a in zip(pack(residual), split(attended))]
    inverse = [
        lax.rsqrt(s / width + EPSILON) for s in row_sums([s * s for s in stream])
    ]
    upper = jnp.asarray((np.arange(8) < 4)[:, None])
    gain = [
        norm_gain[None, :half],
        norm_gain[None, half:],
        jnp.where(upper, norm_gain[None, :half], norm_gain[None, half:]),
    ]
    inv = [inverse[0], inverse[0], inverse[1]]
    normed = [(s * i * g).astype(BF16) for s, i, g in zip(stream, inv, gain)]
    planes = [[gather_plane(part, order) for part, order in zip(normed, ORDERS)]]
    ring_step = lambda: planes.append([send(v, shifted(order[2], 1)) for v, order in zip(planes[-1], ORDERS)])
    ring_step()
    cot_own = after(cot_own, planes[1])
    ring_step()
    cot_planes = (cot_own, after(send(cot_own, SWAP), planes[2]))
    ring_step()

    y = lax.axis_index("y")
    block = np.arange(128) // 8
    turn = (1 - 2 * core) * jnp.asarray([[1], [-1]])
    steps_to = (block % 4) * 4 + ((x - block // 4) * turn) % 4
    info = jnp.concatenate([steps_to, jnp.full((6, 128), 2 * tp)], axis=0).astype(jnp.int32)
    plane_of = ((y - jnp.arange(4) * turn) % 4).reshape(8).astype(jnp.int32)
    tables, slot_gate = routing(plane_of, info, cot_planes, 3 * half)

    grad_rows, hidden_grad = dispatch_grads(plane_of, tables, cot_planes, down_weight)
    planes[-1] = after(planes[-1], hidden_grad)
    row_planes = []
    for p in range(3):
        own = [step[p] for step in planes]
        row_planes.append((own, [send(v, SWAP) for v in own]))
    rows, hidden, gate_grad, up_grad = dispatch_rows(
        tables, row_planes, gate_weight, up_weight, hidden_grad, slot_gate
    )
    out_own, out_sib = combine_out(plane_of, tables, hidden, down_weight)
    back_own, back_sib = combine_back(tables, after(gate_grad, out_own), up_grad, gate_weight, up_weight)
    out_sum = add_swapped(out_own, out_sib)
    weights = []

    def weights_beside(sums):
        weights.extend(weight_grads(rows, grad_rows, after(hidden, sums), gate_grad, up_grad))
        return weights[0]

    back = scatter_parts(back_own, back_sib, {2: lambda _: out_sum, 0: weights_beside})
    gate_out, up_out, down_out = weights
    mixture = scatter_whole(out_sum)

    scaled = [b * g for b, g in zip(back, gain)]
    inner = [s / width for s in row_sums([a * b for a, b in zip(scaled, stream)])]
    inner = [inner[0], inner[0], inner[1]]
    grad = [
        (c.astype(F32) + i * s - st * (i * i * i) * m).astype(BF16)
        for c, i, s, st, m in zip(cot, inv, scaled, stream, inner)
    ]
    residual_grad = unpack(grad)
    output = unpack([(s + m).astype(BF16) for s, m in zip(stream, mixture)])

    packed = jnp.concatenate(grad, axis=1)
    own = [packed if not (j or k) else send(packed, tp_shifted(j, k)) for j in range(4) for k in range(2)]
    own = jnp.concatenate(own, axis=0)
    both = jnp.concatenate([own, send(own, SWAP)], axis=0)
    is_head = (token[:, None] == head_row[None, :]).astype(BF16)
    is_tail = (token[:, None] == tail_row[None, :]).astype(BF16)
    upper_cols = jnp.asarray(np.arange(128) % 8 < 4)[None, :]
    heads = jnp.dot(is_head, both[:, : 2 * half], preferred_element_type=F32)
    tails = [
        jnp.dot(jnp.where(pick, is_tail, 0).astype(BF16), both[:, 2 * half :], preferred_element_type=F32)
        for pick in (upper_cols, ~upper_cols)
    ]
    full = (heads + jnp.concatenate(tails, axis=1)).astype(BF16)
    context_grad = jnp.einsum("td,ad->ta", full, out_proj, preferred_element_type=F32).astype(BF16)
    return (output, residual_grad, context_grad, gate_out, up_out, down_out)


def solution(mesh):
    fine = Mesh(np.asarray(mesh.devices).reshape(2, 4, 4, 2, 2), AXES)
    ctx, tp = AXES[:2], AXES[2:]
    rows = P(AXES, None)
    experts = P(tp, ctx, None)
    return jax.shard_map(
        on_device,
        mesh=fine,
        in_specs=(P(ctx, tp), P(tp, None), rows, P(), experts, experts, experts, rows, rows, rows),
        out_specs=(rows, rows, P(ctx, tp), experts, experts, experts),
        check_vma=False,
    )
```

```python
import functools

import numpy as np
import jax
import jax.numpy as jnp
from jax import lax
from jax.experimental import pallas as pl
from jax.experimental.pallas import tpu as pltpu
from jax.sharding import Mesh, PartitionSpec as P

AXES = ("zh", "y", "x", "zl", "core")
CAP = 4
TOK = 12
EPSILON = 1e-06
BF16 = jnp.bfloat16
F32 = jnp.float32
VMEM_LIMIT = 28 * 1024 * 1024


def flat_index(z, y, x, core):
    return ((((z // 2) * 4 + y) * 4 + x) * 2 + z % 2) * 2 + core


def permutation(move):
    return [
        (flat_index(z, y, x, c), flat_index(*move(z, y, x, c)))
        for z in range(4)
        for y in range(4)
        for x in range(4)
        for c in range(2)
    ]


def shifted(axis, steps):
    def move(z, y, x, c):
        d = steps * (1 - 2 * c)
        if axis == "x":
            return z, y, (x + d) % 4, c
        if axis == "y":
            return z, (y + d) % 4, x, c
        return (z + d) % 4, y, x, c

    return permutation(move)


def tp_shifted(steps, flip):
    return permutation(lambda z, y, x, c: (z ^ flip, y, (x + steps * (1 - 2 * c)) % 4, c))


SWAP = permutation(lambda z, y, x, c: (z, y, x, 1 - c))
ORDERS = (("x", "y", "z"), ("y", "z", "x"), ("z", "x", "y"))


def send(v, pairs):
    return lax.ppermute(v, AXES, pairs)


def after(v, first):
    return lax.optimization_barrier((v, first))[0]


def around(v, axis):
    up = send(v, shifted(axis, 1))
    down = send(v, shifted(axis, -1))
    return [v, up, send(up, shifted(axis, 1)), down]


def around_sum(blocks, axis):
    chain = (blocks[3].astype(F32) + send(blocks[2], shifted(axis, 1)).astype(F32)).astype(BF16)
    direct = send(blocks[1], shifted(axis, -1)).astype(F32)
    return blocks[0].astype(F32) + direct + send(chain, shifted(axis, 1)).astype(F32)


def full_ring(v, axis):
    out = [v]
    for _ in range(3):
        out.append(send(out[-1], shifted(axis, 1)))
    return out


def gather_plane(part, order):
    a, b, c = order
    width = part.shape[-1]
    one = jnp.stack(full_ring(part, a))
    two = jnp.stack(full_ring(one, b), axis=0 if a == "x" else 1)
    return two.reshape(128, width)


def ring_sum(blocks, axis):
    t = blocks[1]
    for d in (2, 3, 0):
        v = blocks[d].astype(F32) + send(t, shifted(axis, 1)).astype(F32)
        t = v.astype(BF16)
    return v


def scatter_parts(own, sib, beside):
    width = own[0].shape[-1]
    arrived = {j: send(sib[j], SWAP) for j in (1, 2, 3, 0)}
    t = [None] * 3
    for j in (1, 2, 3, 0):
        other = beside[j](t) if j in beside else None
        for p, order in enumerate(ORDERS):
            v = own[j][p].astype(F32) + arrived[j][p].astype(F32)
            if t[p] is not None:
                v = v + send(t[p], shifted(order[2], 1)).astype(F32)
            t[p] = v.astype(BF16)
        if other is not None:
            t = after(t, other)
    sums = []
    for v, (a, b, _) in zip(t, ORDERS):
        at = 0 if a == "x" else 1
        v = v.reshape(4, 4, 8, width)
        v = ring_sum([lax.index_in_dim(v, d, at, False) for d in range(4)], b).astype(BF16)
        sums.append(ring_sum([v[d] for d in range(4)], a))
    return sums


def add_swapped(own, sib):
    return (own.astype(F32) + send(sib, SWAP).astype(F32)).astype(BF16)


def scatter_whole(t):
    t = lax.psum_scatter(t, ("y", "x"), scatter_dimension=0, tiled=True)
    t = around_sum([t[8 * d : 8 * d + 8] for d in range(4)], "z")
    width = t.shape[1] // 3
    return [t[:, i * width : (i + 1) * width] for i in range(3)]


def pack(rows):
    half = rows.shape[1] // 2
    tail = rows[8:]
    return [rows[:8, :half], rows[:8, half:], jnp.concatenate([tail[:, :half], tail[:, half:]], axis=0)]


def unpack(parts):
    left, right, tail = parts
    return jnp.concatenate(
        [
            jnp.concatenate([left, right], axis=1),
            jnp.concatenate([tail[:4], tail[4:]], axis=1),
        ],
        axis=0,
    )


def row_sums(products):
    head = jnp.sum(products[0], axis=1, keepdims=True) + jnp.sum(products[1], axis=1, keepdims=True)
    tail = jnp.sum(products[2], axis=1, keepdims=True)
    return head, tail + jnp.concatenate([tail[4:], tail[:4]], axis=0)


def dot(a, b, ca, cb):
    return lax.dot_general(a, b, (((ca,), (cb,)), ((), ())), preferred_element_type=F32)


def iota(axis):
    return lax.broadcasted_iota(jnp.int32, (128, 128), axis)


def one_if(condition, dtype=BF16):
    return jnp.where(condition, 1.0, 0.0).astype(dtype)


def routing_kernel(plane_of, info, *refs):
    planes, (tables, slot_gate) = refs[:2], refs[2:]
    slot, col = iota(0), iota(1)
    slot_block = (slot & 63) >> 2
    rank_of = (slot & 3).astype(F32)
    expert = ((slot >> 6) + info[2:3, :]).astype(F32)
    lane, sub = col, col & 7
    before = one_if(slot < col)
    is_token = lane < TOK
    spreads = [
        one_if(slot == sub),
        one_if((sub < 4) & (slot == sub + 8)),
        one_if((sub >= 4) & (slot == sub + 4)),
    ]
    block = col >> 3
    zx = one_if(block == slot_block, F32)
    xz = one_if((((block & 3) << 2) + (block >> 2)) == slot_block, F32)
    for group in range(8):
        half, g = divmod(group, 4)
        mine = info[half : half + 1, :] == slot_block
        meta = planes[half][plane_rows(plane_of, group), :]
        has = code = total = jnp.zeros((128, 128), F32)
        for k in range(8):
            value = dot(one_if(mine & (sub == k)), meta, 1, 0)
            codes = pltpu.roll(value, 128 - 16, 1)
            hit = one_if((value == expert) & is_token, F32)
            has = has + hit
            code = code + hit * codes
            total = total + codes
        rank = dot(has.astype(BF16), before, 1, 0)
        place = jnp.where(rank == rank_of, has, 0.0)
        number = jnp.sum(place * code, axis=1, keepdims=True)
        over = jnp.sum(place * total, axis=1, keepdims=True)
        gate = jnp.where(over > 0.0, number / jnp.maximum(over, 1.0), 0.0)
        slot_gate[pl.ds(group * 64, 64), :] = gate[:64]
        slot_gate[pl.ds(512 + group * 64, 64), :] = gate[64:]
        head, left, right = (dot(place.astype(BF16), s, 1, 0) for s in spreads)
        here = one_if(mine, F32)
        for i, (t, m) in enumerate(
            ((head, zx), (head, xz), (left, zx), (right, zx), (head, here), (left, here), (right, here))
        ):
            tables[i, group] = (t * m).astype(BF16)


def plane_rows(plane_of, group):
    return pl.ds(pl.multiple_of(plane_of[group] * 128, 128), 128)


def place_group(tables, group, heads, tail, out_ref, at):
    for lr in range(2):
        table = jnp.concatenate([tables[at[lr], group], tables[at[2 + lr], group]], axis=1)
        rows = dot(table, jnp.concatenate([heads[lr], tail], axis=0), 1, 0)
        rows = rows.astype(BF16)
        out_ref[lr, pl.ds(group * 64, 64), :] = rows[:64]
        out_ref[lr, pl.ds(512 + group * 64, 64), :] = rows[64:]


def grads_kernel(plane_of, tables, *refs):
    planes, down = refs[:6], refs[6:8]
    rows, hidden_grad, total = refs[8:]
    step = pl.program_id(0)

    @pl.when(step == 0)
    def _():
        total[...] = jnp.zeros_like(total)

    for group in range(8):
        at = plane_rows(plane_of, group)
        left, right, tail = (planes[2 * p + group // 4][at, :] for p in range(3))
        place_group(tables, group, (left, right), tail, rows, (4, 4, 5, 6))
    for e in range(2):
        at = pl.ds(e * 512, 512)
        total[at, :] += dot(rows[0, at, :], down[0][e], 1, 1) + dot(rows[1, at, :], down[1][e], 1, 1)

    @pl.when(step == pl.num_programs(0) - 1)
    def _():
        hidden_grad[...] = total[...]


def rows_kernel(*refs):
    tables, planes = refs[0], refs[1:25]
    gate, up = refs[25:27], refs[27:29]
    hidden_grad, slot_gate = refs[29:31]
    rows, hidden, gate_grad, up_grad, gate_total, up_total = refs[31:]
    step = pl.program_id(0)

    @pl.when(step == 0)
    def _():
        gate_total[...] = jnp.zeros_like(gate_total)
        up_total[...] = jnp.zeros_like(up_total)

    for group in range(8):
        half, g = divmod(group, 4)
        zs, xs, ys = (planes[p * 8 + half * 4 : p * 8 + half * 4 + 4] for p in range(3))
        pick = pl.ds(g * 32, 32)
        left = jnp.concatenate([ref[pick, :] for ref in zs], axis=0)
        right = jnp.concatenate([ref[pick, :] for ref in xs], axis=0)
        place_group(tables, group, (left, right), ys[g][...], rows, (0, 1, 2, 3))
    for e in range(2):
        at = pl.ds(e * 512, 512)
        left, right = rows[0, at, :], rows[1, at, :]
        gate_total[at, :] += dot(left, gate[0][e], 1, 1) + dot(right, gate[1][e], 1, 1)
        up_total[at, :] += dot(left, up[0][e], 1, 1) + dot(right, up[1][e], 1, 1)

    @pl.when(step == pl.num_programs(0) - 1)
    def _():
        for i in range(8):
            at = pl.ds(i * 128, 128)
            gate_act, up_act = gate_total[at, :], up_total[at, :]
            scale = slot_gate[at, :]
            back = hidden_grad[at, :] * scale
            s = 1.0 / (1.0 + jnp.exp(-gate_act))
            silu = gate_act * s
            hidden[at, :] = (silu * up_act * scale).astype(BF16)
            up_grad[at, :] = (back * silu).astype(BF16)
            gate_grad[at, :] = (back * up_act * s * (1.0 + gate_act * (1.0 - s))).astype(BF16)


def both_experts(slots, lr, group):
    return jnp.concatenate(
        [slots[lr, pl.ds(group * 64, 64), :], slots[lr, pl.ds(512 + group * 64, 64), :]], axis=0
    )


def back_kernel(tables, gate_grad, up_grad, *refs):
    gate, up, outs, slots = refs[:2], refs[2:4], refs[4:-1], refs[-1]
    for lr in range(2):
        for e in range(2):
            pick = pl.ds(e * 512, 512)
            value = dot(gate_grad[pick, :], gate[lr][e], 1, 0) + dot(up_grad[pick, :], up[lr][e], 1, 0)
            slots[lr, pick, :] = value.astype(BF16)
    for group in range(8):
        half, g = divmod(group, 4)
        out = outs[half * 4 : half * 4 + 4]
        left, right = (both_experts(slots, lr, group) for lr in range(2))
        head_left = dot(tables[0, group], left, 0, 0).astype(BF16)
        head_right = dot(tables[1, group], right, 0, 0).astype(BF16)
        tail = dot(tables[2, group], left, 0, 0) + dot(tables[3, group], right, 0, 0)
        for i in range(4):
            out[i][0, pl.ds(g * 32, 32), :] = head_left[i * 32 : (i + 1) * 32]
            out[i][1, pl.ds(g * 32, 32), :] = head_right[i * 32 : (i + 1) * 32]
        out[g][2] = tail.astype(BF16)


def out_kernel(steps, plane_of, tables, hidden, down, own, sib, slots):
    step = pl.program_id(0)
    outs = (own, sib)

    @pl.when(step < 2 * steps)
    def _():
        for e in range(2):
            pick = pl.ds(e * 512, 512)
            slots[step, pick, :] = dot(hidden[pick, :], down[e], 1, 0).astype(BF16)
        for group in range(8):
            value = dot(tables[4, group], both_experts(slots, step, group), 0, 0)
            outs[group // 4][plane_rows(plane_of, group), :] = value.astype(BF16)

    @pl.when(step >= 2 * steps)
    def _():
        for group in range(8):
            value = dot(tables[5, group], both_experts(slots, step - 2 * steps, group), 0, 0)
            value = value + dot(tables[6, group], both_experts(slots, step - steps, group), 0, 0)
            outs[group // 4][plane_rows(plane_of, group), :] = value.astype(BF16)


def weight_grads_kernel(rows, grads, hidden, gate_grad, up_grad, gate_out, up_out, down_out):
    for e in range(2):
        at = pl.ds(e * 512, 512)
        x = rows[0, at, :]
        gate_out[e] = dot(gate_grad[at, :], x, 0, 0).astype(BF16)
        up_out[e] = dot(up_grad[at, :], x, 0, 0).astype(BF16)
        down_out[e] = dot(hidden[at, :], grads[0, at, :], 0, 0).astype(BF16)


def whole(shape):
    return pl.BlockSpec(shape, lambda *_: (0,) * len(shape))


def params():
    return pltpu.CompilerParams(vmem_limit_bytes=VMEM_LIMIT)


def chunk_of(half):
    return min(512, half)


def flat_planes(planes):
    return [v for part in planes for half in part for v in half]


def weight_specs(weight, chunk, steps):
    shape = (weight.shape[0], weight.shape[1], chunk)
    return [
        pl.BlockSpec(shape, lambda n: (0, 0, n)),
        pl.BlockSpec(shape, lambda n, steps=steps: (0, 0, n + steps)),
    ]


def scalars():
    return pl.BlockSpec(memory_space=pltpu.SMEM)


def routing(plane_of, info, planes, width):
    return pl.pallas_call(
        routing_kernel,
        grid=(1,),
        in_specs=[scalars(), whole((8, 128))]
        + [pl.BlockSpec((512, 128), lambda n: (0, width // 128))] * 2,
        out_specs=[whole((7, 8, 128, 128)), whole((1024, 1))],
        out_shape=[
            jax.ShapeDtypeStruct((7, 8, 128, 128), BF16),
            jax.ShapeDtypeStruct((1024, 1), F32),
        ],
        compiler_params=params(),
        cost_estimate=pl.CostEstimate(flops=10**9, bytes_accessed=10**7, transcendentals=0),
    )(plane_of, info, *planes)


def dispatch_grads(plane_of, tables, planes, down):
    width, half = down.shape[1], down.shape[2] // 2
    chunk = chunk_of(half)
    steps = half // chunk
    specs = []
    for p in range(3):
        specs += [pl.BlockSpec((512, chunk), lambda n, p=p: (0, n + p * steps))] * 2
    return pl.pallas_call(
        grads_kernel,
        grid=(steps,),
        in_specs=[scalars(), whole(tables.shape)] + specs + weight_specs(down, chunk, steps),
        out_specs=[pl.BlockSpec((2, 1024, chunk), lambda n: (0, 0, n)), whole((1024, width))],
        out_shape=[
            jax.ShapeDtypeStruct((2, 1024, half), BF16),
            jax.ShapeDtypeStruct((1024, width), F32),
        ],
        scratch_shapes=[pltpu.VMEM((1024, width), F32)],
        compiler_params=params(),
        cost_estimate=pl.CostEstimate(flops=8 * 10**9, bytes_accessed=30 * 10**6, transcendentals=0),
    )(plane_of, tables, *(planes * 3), down, down)


def dispatch_rows(tables, planes, gate, up, hidden_grad, slot_gate):
    width, half = gate.shape[1], gate.shape[2] // 2
    chunk = chunk_of(half)
    steps = half // chunk
    small = jax.ShapeDtypeStruct((1024, width), BF16)
    return pl.pallas_call(
        rows_kernel,
        grid=(steps,),
        in_specs=[whole(tables.shape)]
        + [pl.BlockSpec((128, chunk), lambda n: (0, n))] * 24
        + weight_specs(gate, chunk, steps)
        + weight_specs(up, chunk, steps)
        + [whole((1024, width)), whole((1024, 1))],
        out_specs=[pl.BlockSpec((2, 1024, chunk), lambda n: (0, 0, n))] + [whole((1024, width))] * 3,
        out_shape=[jax.ShapeDtypeStruct((2, 1024, half), BF16), small, small, small],
        scratch_shapes=[pltpu.VMEM((1024, width), F32)] * 2,
        compiler_params=params(),
        cost_estimate=pl.CostEstimate(flops=10**10, bytes_accessed=30 * 10**6, transcendentals=0),
    )(tables, *flat_planes(planes), gate, gate, up, up, hidden_grad, slot_gate)


def combine_back(tables, gate_grad, up_grad, gate, up):
    width, half = gate.shape[1], gate.shape[2] // 2
    chunk = chunk_of(half)
    steps = half // chunk
    out = jax.ShapeDtypeStruct((3, 128, half), BF16)
    outs = pl.pallas_call(
        back_kernel,
        grid=(steps,),
        in_specs=[whole(tables.shape)]
        + [whole((1024, width))] * 2
        + weight_specs(gate, chunk, steps)
        + weight_specs(up, chunk, steps),
        out_specs=[pl.BlockSpec((3, 128, chunk), lambda n: (0, 0, n))] * 8,
        out_shape=[out] * 8,
        scratch_shapes=[pltpu.VMEM((2, 1024, chunk), BF16)],
        compiler_params=params(),
        cost_estimate=pl.CostEstimate(flops=8 * 10**9, bytes_accessed=30 * 10**6, transcendentals=0),
    )(tables, gate_grad, up_grad, gate, gate, up, up)
    return outs[:4], outs[4:]


def combine_out(plane_of, tables, hidden, down):
    width, half = down.shape[1], down.shape[2] // 2
    chunk = chunk_of(half)
    steps = half // chunk
    out = jax.ShapeDtypeStruct((512, 3 * half), BF16)
    return pl.pallas_call(
        functools.partial(out_kernel, steps),
        grid=(3 * steps,),
        in_specs=[
            scalars(),
            whole(tables.shape),
            whole((1024, width)),
            pl.BlockSpec((2, width, chunk), lambda n: (0, 0, jnp.minimum(n, 2 * steps - 1))),
        ],
        out_specs=[pl.BlockSpec((512, chunk), lambda n: (0, n))] * 2,
        out_shape=[out] * 2,
        scratch_shapes=[pltpu.VMEM((2 * steps, 1024, chunk), BF16)],
        compiler_params=params(),
        cost_estimate=pl.CostEstimate(flops=6 * 10**9, bytes_accessed=30 * 10**6, transcendentals=0),
    )(plane_of, tables, hidden, down)


def weight_grads(rows, grads, hidden, gate_grad, up_grad):
    width, half = hidden.shape[1], rows.shape[2]
    chunk = chunk_of(half)
    steps = half // chunk
    out = jax.ShapeDtypeStruct((2, width, 2 * half), BF16)
    return pl.pallas_call(
        weight_grads_kernel,
        grid=(2, steps),
        in_specs=[pl.BlockSpec((1, 1024, chunk), lambda i, n: (i, 0, n))] * 2 + [whole((1024, width))] * 3,
        out_specs=[pl.BlockSpec((2, width, chunk), lambda i, n: (0, 0, i * steps + n))] * 3,
        out_shape=[out] * 3,
        compiler_params=params(),
        cost_estimate=pl.CostEstimate(flops=8 * 10**9, bytes_accessed=30 * 10**6, transcendentals=0),
    )(rows, grads, hidden, gate_grad, up_grad)


def on_device(
    context, out_proj, residual, norm_gain, gate_weight, up_weight, down_weight, expert_ids, gate_codes, cotangent
):
    width = residual.shape[1]
    half = width // 2
    x, zl, core = lax.axis_index("x"), lax.axis_index("zl"), lax.axis_index("core")
    tp = (x * 2 + zl) * 2 + core

    meta = jnp.concatenate(
        [
            jnp.pad(expert_ids.T.astype(BF16), ((0, 0), (0, 4))),
            jnp.pad(gate_codes.T.astype(BF16), ((0, 0), (0, 128 - 16 - TOK))),
        ],
        axis=1,
    )
    cot = pack(cotangent)
    cot_own = jnp.concatenate(around(jnp.concatenate(cot + [meta], axis=1), "z"), axis=0)

    order = np.arange(16)
    h, j, k = order // 8, (order // 2) % 4, order % 2
    sign = (1 - 2 * core) * jnp.asarray(1 - 2 * h)
    owner = (((x - j * sign) % 4) * 2 + (zl ^ jnp.asarray(k))) * 2 + (core ^ jnp.asarray(h))
    lane = np.arange(8)
    head_row = (owner[:, None] * TOK + lane[None, :]).reshape(128)
    tail_row = (owner[:, None] * TOK + 8 + (lane % 4)[None, :]).reshape(128)
    token = jnp.arange(16 * TOK)
    picked = (jnp.concatenate([head_row, tail_row])[:, None] == token[None, :]).astype(BF16)
    ordered = jnp.dot(picked, context, preferred_element_type=F32).astype(BF16)
    partial = jnp.dot(ordered, out_proj, preferred_element_type=F32).astype(BF16)
    cot_own = after(cot_own, partial)
    cot_own = lax.all_gather(cot_own, ("y", "x"), axis=0, tiled=True)
    first = jnp.asarray((np.arange(128) % 8 < 4)[:, None])
    tail = jnp.where(first, partial[128:, :half], partial[128:, half:])
    partial = jnp.concatenate([partial[:128], tail], axis=1).reshape(2, 8, 8, 3 * half)
    summed = (partial[0].astype(F32) + send(partial[1], SWAP).astype(F32)).astype(BF16)
    attended = summed[0].astype(F32)
    for j in range(4):
        for k in range(2):
            if j or k:
                attended = attended + send(summed[2 * j + k], tp_shifted(-j, k)).astype(F32)

    split = lambda v: [v[:, i * half : (i + 1) * half] for i in range(3)]
    stream = [r.astype(F32) + a for r, a in zip(pack(residual), split(attended))]
    inverse = [
        lax.rsqrt(s / width + EPSILON) for s in row_sums([s * s for s in stream])
    ]
    upper = jnp.asarray((np.arange(8) < 4)[:, None])
    gain = [
        norm_gain[None, :half],
        norm_gain[None, half:],
        jnp.where(upper, norm_gain[None, :half], norm_gain[None, half:]),
    ]
    inv = [inverse[0], inverse[0], inverse[1]]
    normed = [(s * i * g).astype(BF16) for s, i, g in zip(stream, inv, gain)]
    planes = [[gather_plane(part, order) for part, order in zip(normed, ORDERS)]]
    ring_step = lambda: planes.append([send(v, shifted(order[2], 1)) for v, order in zip(planes[-1], ORDERS)])
    ring_step()
    cot_own = after(cot_own, planes[1])
    ring_step()
    cot_planes = (cot_own, after(send(cot_own, SWAP), planes[2]))
    ring_step()

    y = lax.axis_index("y")
    block = np.arange(128) // 8
    turn = (1 - 2 * core) * jnp.asarray([[1], [-1]])
    steps_to = (block % 4) * 4 + ((x - block // 4) * turn) % 4
    info = jnp.concatenate([steps_to, jnp.full((6, 128), 2 * tp)], axis=0).astype(jnp.int32)
    plane_of = ((y - jnp.arange(4) * turn) % 4).reshape(8).astype(jnp.int32)
    tables, slot_gate = routing(plane_of, info, cot_planes, 3 * half)

    grad_rows, hidden_grad = dispatch_grads(plane_of, tables, cot_planes, down_weight)
    planes[-1] = after(planes[-1], hidden_grad)
    row_planes = []
    for p in range(3):
        own = [step[p] for step in planes]
        row_planes.append((own, [send(v, SWAP) for v in own]))
    rows, hidden, gate_grad, up_grad = dispatch_rows(
        tables, row_planes, gate_weight, up_weight, hidden_grad, slot_gate
    )
    out_own, out_sib = combine_out(plane_of, tables, hidden, down_weight)
    back_own, back_sib = combine_back(tables, after(gate_grad, out_own), up_grad, gate_weight, up_weight)
    out_sum = add_swapped(out_own, out_sib)
    weights = []

    def weights_beside(sums):
        weights.extend(weight_grads(rows, grad_rows, after(hidden, sums), gate_grad, up_grad))
        return weights[0]

    back = scatter_parts(back_own, back_sib, {1: lambda _: out_sum, 0: weights_beside})
    gate_out, up_out, down_out = weights
    mixture = scatter_whole(out_sum)

    scaled = [b * g for b, g in zip(back, gain)]
    inner = [s / width for s in row_sums([a * b for a, b in zip(scaled, stream)])]
    inner = [inner[0], inner[0], inner[1]]
    grad = [
        (c.astype(F32) + i * s - st * (i * i * i) * m).astype(BF16)
        for c, i, s, st, m in zip(cot, inv, scaled, stream, inner)
    ]
    residual_grad = unpack(grad)
    output = unpack([(s + m).astype(BF16) for s, m in zip(stream, mixture)])

    packed = jnp.concatenate(grad, axis=1)
    own = [packed if not (j or k) else send(packed, tp_shifted(j, k)) for j in range(4) for k in range(2)]
    own = jnp.concatenate(own, axis=0)
    both = jnp.concatenate([own, send(own, SWAP)], axis=0)
    is_head = (token[:, None] == head_row[None, :]).astype(BF16)
    is_tail = (token[:, None] == tail_row[None, :]).astype(BF16)
    upper_cols = jnp.asarray(np.arange(128) % 8 < 4)[None, :]
    heads = jnp.dot(is_head, both[:, : 2 * half], preferred_element_type=F32)
    tails = [
        jnp.dot(jnp.where(pick, is_tail, 0).astype(BF16), both[:, 2 * half :], preferred_element_type=F32)
        for pick in (upper_cols, ~upper_cols)
    ]
    full = (heads + jnp.concatenate(tails, axis=1)).astype(BF16)
    context_grad = jnp.einsum("td,ad->ta", full, out_proj, preferred_element_type=F32).astype(BF16)
    return (output, residual_grad, context_grad, gate_out, up_out, down_out)


def solution(mesh):
    fine = Mesh(np.asarray(mesh.devices).reshape(2, 4, 4, 2, 2), AXES)
    ctx, tp = AXES[:2], AXES[2:]
    rows = P(AXES, None)
    experts = P(tp, ctx, None)
    return jax.shard_map(
        on_device,
        mesh=fine,
        in_specs=(P(ctx, tp), P(tp, None), rows, P(), experts, experts, experts, rows, rows, rows),
        out_specs=(rows, rows, P(ctx, tp), experts, experts, experts),
        check_vma=False,
    )
```

```python
import functools

import numpy as np
import jax
import jax.numpy as jnp
from jax import lax
from jax.experimental import pallas as pl
from jax.experimental.pallas import tpu as pltpu
from jax.sharding import Mesh, PartitionSpec as P

AXES = ("zh", "y", "x", "zl", "core")
CAP = 4
TOK = 12
EPSILON = 1e-06
BF16 = jnp.bfloat16
F32 = jnp.float32
VMEM_LIMIT = 28 * 1024 * 1024


def flat_index(z, y, x, core):
    return ((((z // 2) * 4 + y) * 4 + x) * 2 + z % 2) * 2 + core


def permutation(move):
    return [
        (flat_index(z, y, x, c), flat_index(*move(z, y, x, c)))
        for z in range(4)
        for y in range(4)
        for x in range(4)
        for c in range(2)
    ]


def shifted(axis, steps):
    def move(z, y, x, c):
        d = steps * (1 - 2 * c)
        if axis == "x":
            return z, y, (x + d) % 4, c
        if axis == "y":
            return z, (y + d) % 4, x, c
        return (z + d) % 4, y, x, c

    return permutation(move)


def tp_shifted(steps, flip):
    return permutation(lambda z, y, x, c: (z ^ flip, y, (x + steps * (1 - 2 * c)) % 4, c))


SWAP = permutation(lambda z, y, x, c: (z, y, x, 1 - c))
ORDERS = (("x", "y", "z"), ("y", "z", "x"), ("z", "x", "y"))


def send(v, pairs):
    return lax.ppermute(v, AXES, pairs)


def after(v, first):
    return lax.optimization_barrier((v, first))[0]


def around(v, axis):
    up = send(v, shifted(axis, 1))
    down = send(v, shifted(axis, -1))
    return [v, up, send(up, shifted(axis, 1)), down]


def around_sum(blocks, axis):
    chain = (blocks[3].astype(F32) + send(blocks[2], shifted(axis, 1)).astype(F32)).astype(BF16)
    direct = send(blocks[1], shifted(axis, -1)).astype(F32)
    return blocks[0].astype(F32) + direct + send(chain, shifted(axis, 1)).astype(F32)


def full_ring(v, axis):
    out = [v]
    for _ in range(3):
        out.append(send(out[-1], shifted(axis, 1)))
    return out


def gather_plane(part, order):
    a, b, c = order
    width = part.shape[-1]
    one = jnp.stack(full_ring(part, a))
    two = jnp.stack(full_ring(one, b), axis=0 if a == "x" else 1)
    return two.reshape(128, width)


def ring_sum(blocks, axis):
    t = blocks[1]
    for d in (2, 3, 0):
        v = blocks[d].astype(F32) + send(t, shifted(axis, 1)).astype(F32)
        t = v.astype(BF16)
    return v


def scatter_parts(own, sib, beside):
    width = own[0].shape[-1]
    arrived = {j: send(sib[j], SWAP) for j in (1, 2, 3, 0)}
    t = [None] * 3
    for j in (1, 2, 3, 0):
        other = beside[j](t) if j in beside else None
        for p, order in enumerate(ORDERS):
            v = own[j][p].astype(F32) + arrived[j][p].astype(F32)
            if t[p] is not None:
                v = v + send(t[p], shifted(order[2], 1)).astype(F32)
            t[p] = v.astype(BF16)
        if other is not None:
            t = after(t, other)
    sums = []
    for v, (a, b, _) in zip(t, ORDERS):
        at = 0 if a == "x" else 1
        v = v.reshape(4, 4, 8, width)
        v = ring_sum([lax.index_in_dim(v, d, at, False) for d in range(4)], b).astype(BF16)
        sums.append(ring_sum([v[d] for d in range(4)], a))
    return sums


def add_float(a, b):
    return (a.astype(F32) + b.astype(F32)).astype(BF16)


def scatter_whole(t):
    t = lax.psum_scatter(t, ("y", "x"), scatter_dimension=0, tiled=True)
    t = around_sum([t[8 * d : 8 * d + 8] for d in range(4)], "z")
    width = t.shape[1] // 3
    return [t[:, i * width : (i + 1) * width] for i in range(3)]


def pack(rows):
    half = rows.shape[1] // 2
    tail = rows[8:]
    return [rows[:8, :half], rows[:8, half:], jnp.concatenate([tail[:, :half], tail[:, half:]], axis=0)]


def unpack(parts):
    left, right, tail = parts
    return jnp.concatenate(
        [
            jnp.concatenate([left, right], axis=1),
            jnp.concatenate([tail[:4], tail[4:]], axis=1),
        ],
        axis=0,
    )


def row_sums(products):
    head = jnp.sum(products[0], axis=1, keepdims=True) + jnp.sum(products[1], axis=1, keepdims=True)
    tail = jnp.sum(products[2], axis=1, keepdims=True)
    return head, tail + jnp.concatenate([tail[4:], tail[:4]], axis=0)


def dot(a, b, ca, cb):
    return lax.dot_general(a, b, (((ca,), (cb,)), ((), ())), preferred_element_type=F32)


def iota(axis):
    return lax.broadcasted_iota(jnp.int32, (128, 128), axis)


def one_if(condition, dtype=BF16):
    return jnp.where(condition, 1.0, 0.0).astype(dtype)


def routing_kernel(plane_of, info, *refs):
    planes, (tables, slot_gate) = refs[:2], refs[2:]
    slot, col = iota(0), iota(1)
    slot_block = (slot & 63) >> 2
    rank_of = (slot & 3).astype(F32)
    expert = ((slot >> 6) + info[2:3, :]).astype(F32)
    lane, sub = col, col & 7
    before = one_if(slot < col)
    is_token = lane < TOK
    spreads = [
        one_if(slot == sub),
        one_if((sub < 4) & (slot == sub + 8)),
        one_if((sub >= 4) & (slot == sub + 4)),
    ]
    block = col >> 3
    zx = one_if(block == slot_block, F32)
    xz = one_if((((block & 3) << 2) + (block >> 2)) == slot_block, F32)
    for group in range(8):
        half, g = divmod(group, 4)
        mine = info[half : half + 1, :] == slot_block
        meta = planes[half][plane_rows(plane_of, group), :]
        has = code = total = jnp.zeros((128, 128), F32)
        for k in range(8):
            value = dot(one_if(mine & (sub == k)), meta, 1, 0)
            codes = pltpu.roll(value, 128 - 16, 1)
            hit = one_if((value == expert) & is_token, F32)
            has = has + hit
            code = code + hit * codes
            total = total + codes
        rank = dot(has.astype(BF16), before, 1, 0)
        place = jnp.where(rank == rank_of, has, 0.0)
        number = jnp.sum(place * code, axis=1, keepdims=True)
        over = jnp.sum(place * total, axis=1, keepdims=True)
        gate = jnp.where(over > 0.0, number / jnp.maximum(over, 1.0), 0.0)
        slot_gate[pl.ds(group * 64, 64), :] = gate[:64]
        slot_gate[pl.ds(512 + group * 64, 64), :] = gate[64:]
        head, left, right = (dot(place.astype(BF16), s, 1, 0) for s in spreads)
        here = one_if(mine, F32)
        for i, (t, m) in enumerate(
            ((head, zx), (head, xz), (left, zx), (right, zx), (head, here), (left, here), (right, here))
        ):
            tables[i, group] = (t * m).astype(BF16)


def plane_rows(plane_of, group):
    return pl.ds(pl.multiple_of(plane_of[group] * 128, 128), 128)


def place_group(tables, group, heads, tail, out_ref, at):
    for lr in range(2):
        table = jnp.concatenate([tables[at[lr], group], tables[at[2 + lr], group]], axis=1)
        rows = dot(table, jnp.concatenate([heads[lr], tail], axis=0), 1, 0)
        rows = rows.astype(BF16)
        out_ref[lr, pl.ds(group * 64, 64), :] = rows[:64]
        out_ref[lr, pl.ds(512 + group * 64, 64), :] = rows[64:]


def grads_kernel(plane_of, tables, *refs):
    planes, down = refs[:6], refs[6:8]
    rows, hidden_grad, total = refs[8:]
    step = pl.program_id(0)

    @pl.when(step == 0)
    def _():
        total[...] = jnp.zeros_like(total)

    for group in range(8):
        at = plane_rows(plane_of, group)
        left, right, tail = (planes[2 * p + group // 4][at, :] for p in range(3))
        place_group(tables, group, (left, right), tail, rows, (4, 4, 5, 6))
    for e in range(2):
        at = pl.ds(e * 512, 512)
        total[at, :] += dot(rows[0, at, :], down[0][e], 1, 1) + dot(rows[1, at, :], down[1][e], 1, 1)

    @pl.when(step == pl.num_programs(0) - 1)
    def _():
        hidden_grad[...] = total[...]


def rows_kernel(*refs):
    tables, planes = refs[0], refs[1:25]
    gate, up = refs[25:27], refs[27:29]
    hidden_grad, slot_gate = refs[29:31]
    rows, hidden, gate_grad, up_grad, gate_total, up_total = refs[31:]
    step = pl.program_id(0)

    @pl.when(step == 0)
    def _():
        gate_total[...] = jnp.zeros_like(gate_total)
        up_total[...] = jnp.zeros_like(up_total)

    for group in range(8):
        half, g = divmod(group, 4)
        zs, xs, ys = (planes[p * 8 + half * 4 : p * 8 + half * 4 + 4] for p in range(3))
        pick = pl.ds(g * 32, 32)
        left = jnp.concatenate([ref[pick, :] for ref in zs], axis=0)
        right = jnp.concatenate([ref[pick, :] for ref in xs], axis=0)
        place_group(tables, group, (left, right), ys[g][...], rows, (0, 1, 2, 3))
    for e in range(2):
        at = pl.ds(e * 512, 512)
        left, right = rows[0, at, :], rows[1, at, :]
        gate_total[at, :] += dot(left, gate[0][e], 1, 1) + dot(right, gate[1][e], 1, 1)
        up_total[at, :] += dot(left, up[0][e], 1, 1) + dot(right, up[1][e], 1, 1)

    @pl.when(step == pl.num_programs(0) - 1)
    def _():
        for i in range(8):
            at = pl.ds(i * 128, 128)
            gate_act, up_act = gate_total[at, :], up_total[at, :]
            scale = slot_gate[at, :]
            back = hidden_grad[at, :] * scale
            s = 1.0 / (1.0 + jnp.exp(-gate_act))
            silu = gate_act * s
            hidden[at, :] = (silu * up_act * scale).astype(BF16)
            up_grad[at, :] = (back * silu).astype(BF16)
            gate_grad[at, :] = (back * up_act * s * (1.0 + gate_act * (1.0 - s))).astype(BF16)


def both_experts(slots, lr, group):
    return jnp.concatenate(
        [slots[lr, pl.ds(group * 64, 64), :], slots[lr, pl.ds(512 + group * 64, 64), :]], axis=0
    )


def back_kernel(tables, gate_grad, up_grad, *refs):
    gate, up, outs, slots = refs[:2], refs[2:4], refs[4:-1], refs[-1]
    for lr in range(2):
        for e in range(2):
            pick = pl.ds(e * 512, 512)
            value = dot(gate_grad[pick, :], gate[lr][e], 1, 0) + dot(up_grad[pick, :], up[lr][e], 1, 0)
            slots[lr, pick, :] = value.astype(BF16)
    for group in range(8):
        half, g = divmod(group, 4)
        out = outs[half * 4 : half * 4 + 4]
        left, right = (both_experts(slots, lr, group) for lr in range(2))
        head_left = dot(tables[0, group], left, 0, 0).astype(BF16)
        head_right = dot(tables[1, group], right, 0, 0).astype(BF16)
        tail = dot(tables[2, group], left, 0, 0) + dot(tables[3, group], right, 0, 0)
        for i in range(4):
            out[i][0, pl.ds(g * 32, 32), :] = head_left[i * 32 : (i + 1) * 32]
            out[i][1, pl.ds(g * 32, 32), :] = head_right[i * 32 : (i + 1) * 32]
        out[g][2] = tail.astype(BF16)


def out_kernel(steps, plane_of, tables, hidden, down, own, sib, slots):
    step = pl.program_id(0)
    outs = (own, sib)

    @pl.when(step < 2 * steps)
    def _():
        for e in range(2):
            pick = pl.ds(e * 512, 512)
            slots[step, pick, :] = dot(hidden[pick, :], down[e], 1, 0).astype(BF16)
        for group in range(8):
            value = dot(tables[4, group], both_experts(slots, step, group), 0, 0)
            outs[group // 4][plane_rows(plane_of, group), :] = value.astype(BF16)

    @pl.when(step >= 2 * steps)
    def _():
        for group in range(8):
            value = dot(tables[5, group], both_experts(slots, step - 2 * steps, group), 0, 0)
            value = value + dot(tables[6, group], both_experts(slots, step - steps, group), 0, 0)
            outs[group // 4][plane_rows(plane_of, group), :] = value.astype(BF16)


def weight_grads_kernel(rows, grads, hidden, gate_grad, up_grad, gate_out, up_out, down_out):
    for e in range(2):
        at = pl.ds(e * 512, 512)
        x = rows[0, at, :]
        gate_out[e] = dot(gate_grad[at, :], x, 0, 0).astype(BF16)
        up_out[e] = dot(up_grad[at, :], x, 0, 0).astype(BF16)
        down_out[e] = dot(hidden[at, :], grads[0, at, :], 0, 0).astype(BF16)


def whole(shape):
    return pl.BlockSpec(shape, lambda *_: (0,) * len(shape))


def params():
    return pltpu.CompilerParams(vmem_limit_bytes=VMEM_LIMIT)


def chunk_of(half):
    return min(512, half)


def flat_planes(planes):
    return [v for part in planes for half in part for v in half]


def weight_specs(weight, chunk, steps):
    shape = (weight.shape[0], weight.shape[1], chunk)
    return [
        pl.BlockSpec(shape, lambda n: (0, 0, n)),
        pl.BlockSpec(shape, lambda n, steps=steps: (0, 0, n + steps)),
    ]


def scalars():
    return pl.BlockSpec(memory_space=pltpu.SMEM)


def routing(plane_of, info, planes, width):
    return pl.pallas_call(
        routing_kernel,
        grid=(1,),
        in_specs=[scalars(), whole((8, 128))]
        + [pl.BlockSpec((512, 128), lambda n: (0, width // 128))] * 2,
        out_specs=[whole((7, 8, 128, 128)), whole((1024, 1))],
        out_shape=[
            jax.ShapeDtypeStruct((7, 8, 128, 128), BF16),
            jax.ShapeDtypeStruct((1024, 1), F32),
        ],
        compiler_params=params(),
        cost_estimate=pl.CostEstimate(flops=10**9, bytes_accessed=10**7, transcendentals=0),
    )(plane_of, info, *planes)


def dispatch_grads(plane_of, tables, planes, down):
    width, half = down.shape[1], down.shape[2] // 2
    chunk = chunk_of(half)
    steps = half // chunk
    specs = []
    for p in range(3):
        specs += [pl.BlockSpec((512, chunk), lambda n, p=p: (0, n + p * steps))] * 2
    return pl.pallas_call(
        grads_kernel,
        grid=(steps,),
        in_specs=[scalars(), whole(tables.shape)] + specs + weight_specs(down, chunk, steps),
        out_specs=[pl.BlockSpec((2, 1024, chunk), lambda n: (0, 0, n)), whole((1024, width))],
        out_shape=[
            jax.ShapeDtypeStruct((2, 1024, half), BF16),
            jax.ShapeDtypeStruct((1024, width), F32),
        ],
        scratch_shapes=[pltpu.VMEM((1024, width), F32)],
        compiler_params=params(),
        cost_estimate=pl.CostEstimate(flops=8 * 10**9, bytes_accessed=30 * 10**6, transcendentals=0),
    )(plane_of, tables, *(planes * 3), down, down)


def dispatch_rows(tables, planes, gate, up, hidden_grad, slot_gate):
    width, half = gate.shape[1], gate.shape[2] // 2
    chunk = chunk_of(half)
    steps = half // chunk
    small = jax.ShapeDtypeStruct((1024, width), BF16)
    return pl.pallas_call(
        rows_kernel,
        grid=(steps,),
        in_specs=[whole(tables.shape)]
        + [pl.BlockSpec((128, chunk), lambda n: (0, n))] * 24
        + weight_specs(gate, chunk, steps)
        + weight_specs(up, chunk, steps)
        + [whole((1024, width)), whole((1024, 1))],
        out_specs=[pl.BlockSpec((2, 1024, chunk), lambda n: (0, 0, n))] + [whole((1024, width))] * 3,
        out_shape=[jax.ShapeDtypeStruct((2, 1024, half), BF16), small, small, small],
        scratch_shapes=[pltpu.VMEM((1024, width), F32)] * 2,
        compiler_params=params(),
        cost_estimate=pl.CostEstimate(flops=10**10, bytes_accessed=30 * 10**6, transcendentals=0),
    )(tables, *flat_planes(planes), gate, gate, up, up, hidden_grad, slot_gate)


def combine_back(tables, gate_grad, up_grad, gate, up):
    width, half = gate.shape[1], gate.shape[2] // 2
    chunk = chunk_of(half)
    steps = half // chunk
    out = jax.ShapeDtypeStruct((3, 128, half), BF16)
    outs = pl.pallas_call(
        back_kernel,
        grid=(steps,),
        in_specs=[whole(tables.shape)]
        + [whole((1024, width))] * 2
        + weight_specs(gate, chunk, steps)
        + weight_specs(up, chunk, steps),
        out_specs=[pl.BlockSpec((3, 128, chunk), lambda n: (0, 0, n))] * 8,
        out_shape=[out] * 8,
        scratch_shapes=[pltpu.VMEM((2, 1024, chunk), BF16)],
        compiler_params=params(),
        cost_estimate=pl.CostEstimate(flops=8 * 10**9, bytes_accessed=30 * 10**6, transcendentals=0),
    )(tables, gate_grad, up_grad, gate, gate, up, up)
    return outs[:4], outs[4:]


def combine_out(plane_of, tables, hidden, down):
    width, half = down.shape[1], down.shape[2] // 2
    chunk = chunk_of(half)
    steps = half // chunk
    out = jax.ShapeDtypeStruct((512, 3 * half), BF16)
    return pl.pallas_call(
        functools.partial(out_kernel, steps),
        grid=(3 * steps,),
        in_specs=[
            scalars(),
            whole(tables.shape),
            whole((1024, width)),
            pl.BlockSpec((2, width, chunk), lambda n: (0, 0, jnp.minimum(n, 2 * steps - 1))),
        ],
        out_specs=[pl.BlockSpec((512, chunk), lambda n: (0, n))] * 2,
        out_shape=[out] * 2,
        scratch_shapes=[pltpu.VMEM((2 * steps, 1024, chunk), BF16)],
        compiler_params=params(),
        cost_estimate=pl.CostEstimate(flops=6 * 10**9, bytes_accessed=30 * 10**6, transcendentals=0),
    )(plane_of, tables, hidden, down)


def weight_grads(rows, grads, hidden, gate_grad, up_grad):
    width, half = hidden.shape[1], rows.shape[2]
    chunk = chunk_of(half)
    steps = half // chunk
    out = jax.ShapeDtypeStruct((2, width, 2 * half), BF16)
    return pl.pallas_call(
        weight_grads_kernel,
        grid=(2, steps),
        in_specs=[pl.BlockSpec((1, 1024, chunk), lambda i, n: (i, 0, n))] * 2 + [whole((1024, width))] * 3,
        out_specs=[pl.BlockSpec((2, width, chunk), lambda i, n: (0, 0, i * steps + n))] * 3,
        out_shape=[out] * 3,
        compiler_params=params(),
        cost_estimate=pl.CostEstimate(flops=8 * 10**9, bytes_accessed=30 * 10**6, transcendentals=0),
    )(rows, grads, hidden, gate_grad, up_grad)


def context_kernel(picks, *refs):
    (own_l, own_r, own_t, sib_l, sib_r, sib_t), (left, right), (out, total) = refs[:6], refs[6:8], refs[8:]
    step = pl.program_id(0)

    @pl.when(step == 0)
    def _():
        total[...] = jnp.zeros_like(total)

    tail = jnp.concatenate([own_t[...], sib_t[...]], axis=0)
    for i, (own, sib, weight) in enumerate(((own_l, sib_l, left), (own_r, sib_r, right))):
        head = jnp.concatenate([own[...], sib[...]], axis=0)
        rows = dot(picks[0], head, 1, 0) + dot(picks[1 + i], tail, 1, 0)
        total[...] += dot(rows.astype(BF16), weight[...], 1, 1)

    @pl.when(step == pl.num_programs(0) - 1)
    def _():
        out[...] = total[...].astype(BF16)


def context_gradient(picks, own, sib, out_proj):
    features, half = out_proj.shape[0], out_proj.shape[1] // 2
    chunk = chunk_of(half)
    steps = half // chunk
    packed = [pl.BlockSpec((64, chunk), lambda n, p=p: (0, n + p * steps)) for p in range(3)]
    tokens = picks.shape[1]
    return pl.pallas_call(
        context_kernel,
        grid=(steps,),
        in_specs=[whole(picks.shape)]
        + packed * 2
        + [pl.BlockSpec((features, chunk), lambda n, p=p: (0, n + p * steps)) for p in range(2)],
        out_specs=whole((tokens, features)),
        out_shape=jax.ShapeDtypeStruct((tokens, features), BF16),
        scratch_shapes=[pltpu.VMEM((tokens, features), F32)],
        compiler_params=params(),
        cost_estimate=pl.CostEstimate(flops=10**9, bytes_accessed=6 * 10**6, transcendentals=0),
    )(picks, own, own, own, sib, sib, sib, out_proj, out_proj)


def on_device(
    context, out_proj, residual, norm_gain, gate_weight, up_weight, down_weight, expert_ids, gate_codes, cotangent
):
    width = residual.shape[1]
    half = width // 2
    x, zl, core = lax.axis_index("x"), lax.axis_index("zl"), lax.axis_index("core")
    tp = (x * 2 + zl) * 2 + core

    meta = jnp.concatenate(
        [
            jnp.pad(expert_ids.T.astype(BF16), ((0, 0), (0, 4))),
            jnp.pad(gate_codes.T.astype(BF16), ((0, 0), (0, 128 - 16 - TOK))),
        ],
        axis=1,
    )
    cot = pack(cotangent)
    cot_own = jnp.concatenate(around(jnp.concatenate(cot + [meta], axis=1), "z"), axis=0)

    order = np.arange(16)
    h, j, k = order // 8, (order // 2) % 4, order % 2
    sign = (1 - 2 * core) * jnp.asarray(1 - 2 * h)
    owner = (((x - j * sign) % 4) * 2 + (zl ^ jnp.asarray(k))) * 2 + (core ^ jnp.asarray(h))
    lane = np.arange(8)
    head_row = (owner[:, None] * TOK + lane[None, :]).reshape(128)
    tail_row = (owner[:, None] * TOK + 8 + (lane % 4)[None, :]).reshape(128)
    token = jnp.arange(16 * TOK)
    picked = (jnp.concatenate([head_row, tail_row])[:, None] == token[None, :]).astype(BF16)
    ordered = jnp.dot(picked, context, preferred_element_type=F32).astype(BF16)
    partial = jnp.dot(ordered, out_proj, preferred_element_type=F32).astype(BF16)
    cot_own = after(cot_own, partial)
    cot_own = lax.all_gather(cot_own, ("y", "x"), axis=0, tiled=True)
    first = jnp.asarray((np.arange(128) % 8 < 4)[:, None])
    tail = jnp.where(first, partial[128:, :half], partial[128:, half:])
    partial = jnp.concatenate([partial[:128], tail], axis=1).reshape(2, 8, 8, 3 * half)
    summed = (partial[0].astype(F32) + send(partial[1], SWAP).astype(F32)).astype(BF16)
    attended = summed[0].astype(F32)
    for j in range(4):
        for k in range(2):
            if j or k:
                attended = attended + send(summed[2 * j + k], tp_shifted(-j, k)).astype(F32)

    split = lambda v: [v[:, i * half : (i + 1) * half] for i in range(3)]
    stream = [r.astype(F32) + a for r, a in zip(pack(residual), split(attended))]
    inverse = [
        lax.rsqrt(s / width + EPSILON) for s in row_sums([s * s for s in stream])
    ]
    upper = jnp.asarray((np.arange(8) < 4)[:, None])
    gain = [
        norm_gain[None, :half],
        norm_gain[None, half:],
        jnp.where(upper, norm_gain[None, :half], norm_gain[None, half:]),
    ]
    inv = [inverse[0], inverse[0], inverse[1]]
    normed = [(s * i * g).astype(BF16) for s, i, g in zip(stream, inv, gain)]
    planes = [[gather_plane(part, order) for part, order in zip(normed, ORDERS)]]
    ring_step = lambda: planes.append([send(v, shifted(order[2], 1)) for v, order in zip(planes[-1], ORDERS)])
    ring_step()
    cot_own = after(cot_own, planes[1])
    ring_step()
    cot_planes = (cot_own, after(send(cot_own, SWAP), planes[2]))
    ring_step()

    y = lax.axis_index("y")
    block = np.arange(128) // 8
    turn = (1 - 2 * core) * jnp.asarray([[1], [-1]])
    steps_to = (block % 4) * 4 + ((x - block // 4) * turn) % 4
    info = jnp.concatenate([steps_to, jnp.full((6, 128), 2 * tp)], axis=0).astype(jnp.int32)
    plane_of = ((y - jnp.arange(4) * turn) % 4).reshape(8).astype(jnp.int32)
    tables, slot_gate = routing(plane_of, info, cot_planes, 3 * half)

    grad_rows, hidden_grad = dispatch_grads(plane_of, tables, cot_planes, down_weight)
    row_planes = []
    for p in range(3):
        own = [step[p] for step in planes]
        early = [after(v, planes[2]) for v in own[:2]]
        row_planes.append((own, [send(v, SWAP) for v in early + own[2:]]))
    rows, hidden, gate_grad, up_grad = dispatch_rows(
        tables, row_planes, gate_weight, up_weight, hidden_grad, slot_gate
    )
    out_own, out_sib = combine_out(plane_of, tables, hidden, down_weight)
    back_own, back_sib = combine_back(tables, after(gate_grad, out_own), up_grad, gate_weight, up_weight)
    out_arrived = send(out_sib, SWAP)
    out_sum = add_float(out_own, out_arrived)
    weights = []

    def weights_beside(sums):
        weights.extend(weight_grads(rows, grad_rows, after(hidden, sums), gate_grad, up_grad))
        return weights[0]

    back = scatter_parts(back_own, back_sib, {1: lambda _: out_arrived, 2: lambda _: out_sum, 0: weights_beside})
    gate_out, up_out, down_out = weights
    mixture = scatter_whole(out_sum)

    scaled = [b * g for b, g in zip(back, gain)]
    inner = [s / width for s in row_sums([a * b for a, b in zip(scaled, stream)])]
    inner = [inner[0], inner[0], inner[1]]
    grad = [
        (c.astype(F32) + i * s - st * (i * i * i) * m).astype(BF16)
        for c, i, s, st, m in zip(cot, inv, scaled, stream, inner)
    ]
    residual_grad = unpack(grad)
    output = unpack([(s + m).astype(BF16) for s, m in zip(stream, mixture)])

    packed = jnp.concatenate(grad, axis=1)
    own = [packed if not (j or k) else send(packed, tp_shifted(j, k)) for j in range(4) for k in range(2)]
    own = jnp.concatenate(own, axis=0)
    is_head = token[:, None] == head_row[None, :]
    is_tail = token[:, None] == tail_row[None, :]
    upper_cols = jnp.asarray(np.arange(128) % 8 < 4)[None, :]
    picks = jnp.stack([is_head, is_tail & upper_cols, is_tail & ~upper_cols]).astype(BF16)
    context_grad = context_gradient(picks, own, send(own, SWAP), out_proj)
    return (output, residual_grad, context_grad, gate_out, up_out, down_out)


def solution(mesh):
    fine = Mesh(np.asarray(mesh.devices).reshape(2, 4, 4, 2, 2), AXES)
    ctx, tp = AXES[:2], AXES[2:]
    rows = P(AXES, None)
    experts = P(tp, ctx, None)
    return jax.shard_map(
        on_device,
        mesh=fine,
        in_specs=(P(ctx, tp), P(tp, None), rows, P(), experts, experts, experts, rows, rows, rows),
        out_specs=(rows, rows, P(ctx, tp), experts, experts, experts),
        check_vma=False,
    )
```

```python
import functools

import numpy as np
import jax
import jax.numpy as jnp
from jax import lax
from jax.experimental import pallas as pl
from jax.experimental.pallas import tpu as pltpu
from jax.sharding import Mesh, PartitionSpec as P

AXES = ("zh", "y", "x", "zl", "core")
CAP = 4
TOK = 12
EPSILON = 1e-06
BF16 = jnp.bfloat16
F32 = jnp.float32
VMEM_LIMIT = 28 * 1024 * 1024


def flat_index(z, y, x, core):
    return ((((z // 2) * 4 + y) * 4 + x) * 2 + z % 2) * 2 + core


def permutation(move):
    return [
        (flat_index(z, y, x, c), flat_index(*move(z, y, x, c)))
        for z in range(4)
        for y in range(4)
        for x in range(4)
        for c in range(2)
    ]


def shifted(axis, steps):
    def move(z, y, x, c):
        d = steps * (1 - 2 * c)
        if axis == "x":
            return z, y, (x + d) % 4, c
        if axis == "y":
            return z, (y + d) % 4, x, c
        return (z + d) % 4, y, x, c

    return permutation(move)


def tp_shifted(steps, flip):
    return permutation(lambda z, y, x, c: (z ^ flip, y, (x + steps * (1 - 2 * c)) % 4, c))


SWAP = permutation(lambda z, y, x, c: (z, y, x, 1 - c))
ORDERS = (("x", "y", "z"), ("y", "z", "x"), ("z", "x", "y"))


def send(v, pairs):
    return lax.ppermute(v, AXES, pairs)


def after(v, first):
    return lax.optimization_barrier((v, first))[0]


def around(v, axis):
    up = send(v, shifted(axis, 1))
    down = send(v, shifted(axis, -1))
    return [v, up, send(up, shifted(axis, 1)), down]


def around_sum(blocks, axis):
    chain = (blocks[3].astype(F32) + send(blocks[2], shifted(axis, 1)).astype(F32)).astype(BF16)
    direct = send(blocks[1], shifted(axis, -1)).astype(F32)
    return blocks[0].astype(F32) + direct + send(chain, shifted(axis, 1)).astype(F32)


def gather_plane(part, order):
    a, b, c = order
    width = part.shape[-1]
    one = jnp.stack(around(part, a))
    two = jnp.stack(around(one, b), axis=0 if a == "x" else 1)
    return two.reshape(128, width)


def scatter_parts(own, sib, beside):
    width = own[0].shape[-1]
    arrived = {j: send(sib[j], SWAP) for j in (1, 2, 3, 0)}
    t = [None] * 3
    for j in (1, 2, 3, 0):
        other = beside[j](t) if j in beside else None
        for p, order in enumerate(ORDERS):
            v = own[j][p].astype(F32) + arrived[j][p].astype(F32)
            if t[p] is not None:
                v = v + send(t[p], shifted(order[2], 1)).astype(F32)
            t[p] = v.astype(BF16)
        if other is not None:
            t = after(t, other)
    sums = []
    for v, (a, b, _) in zip(t, ORDERS):
        at = 0 if a == "x" else 1
        v = v.reshape(4, 4, 8, width)
        v = around_sum([lax.index_in_dim(v, d, at, False) for d in range(4)], b).astype(BF16)
        sums.append(around_sum([v[d] for d in range(4)], a))
    return sums


def add_float(a, b):
    return (a.astype(F32) + b.astype(F32)).astype(BF16)


def scatter_whole(t):
    t = lax.psum_scatter(t, ("y", "x"), scatter_dimension=0, tiled=True)
    t = around_sum([t[8 * d : 8 * d + 8] for d in range(4)], "z")
    width = t.shape[1] // 3
    return [t[:, i * width : (i + 1) * width] for i in range(3)]


def pack(rows):
    half = rows.shape[1] // 2
    tail = rows[8:]
    return [rows[:8, :half], rows[:8, half:], jnp.concatenate([tail[:, :half], tail[:, half:]], axis=0)]


def unpack(parts):
    left, right, tail = parts
    return jnp.concatenate(
        [
            jnp.concatenate([left, right], axis=1),
            jnp.concatenate([tail[:4], tail[4:]], axis=1),
        ],
        axis=0,
    )


def row_sums(products):
    head = jnp.sum(products[0], axis=1, keepdims=True) + jnp.sum(products[1], axis=1, keepdims=True)
    tail = jnp.sum(products[2], axis=1, keepdims=True)
    return head, tail + jnp.concatenate([tail[4:], tail[:4]], axis=0)


def dot(a, b, ca, cb):
    return lax.dot_general(a, b, (((ca,), (cb,)), ((), ())), preferred_element_type=F32)


def iota(axis):
    return lax.broadcasted_iota(jnp.int32, (128, 128), axis)


def one_if(condition, dtype=BF16):
    return jnp.where(condition, 1.0, 0.0).astype(dtype)


def routing_kernel(plane_of, info, *refs):
    planes, (tables, slot_gate) = refs[:2], refs[2:]
    slot, col = iota(0), iota(1)
    slot_block = (slot & 63) >> 2
    rank_of = (slot & 3).astype(F32)
    expert = ((slot >> 6) + info[2:3, :]).astype(F32)
    lane, sub = col, col & 7
    before = one_if(slot < col)
    is_token = lane < TOK
    spreads = [
        one_if(slot == sub),
        one_if((sub < 4) & (slot == sub + 8)),
        one_if((sub >= 4) & (slot == sub + 4)),
    ]
    block = col >> 3
    zx = one_if(block == slot_block, F32)
    xz = one_if((((block & 3) << 2) + (block >> 2)) == slot_block, F32)
    for group in range(8):
        half, g = divmod(group, 4)
        mine = info[half : half + 1, :] == slot_block
        meta = planes[half][plane_rows(plane_of, group), :]
        has = code = total = jnp.zeros((128, 128), F32)
        for k in range(8):
            value = dot(one_if(mine & (sub == k)), meta, 1, 0)
            codes = pltpu.roll(value, 128 - 16, 1)
            hit = one_if((value == expert) & is_token, F32)
            has = has + hit
            code = code + hit * codes
            total = total + codes
        rank = dot(has.astype(BF16), before, 1, 0)
        place = jnp.where(rank == rank_of, has, 0.0)
        number = jnp.sum(place * code, axis=1, keepdims=True)
        over = jnp.sum(place * total, axis=1, keepdims=True)
        gate = jnp.where(over > 0.0, number / jnp.maximum(over, 1.0), 0.0)
        slot_gate[pl.ds(group * 64, 64), :] = gate[:64]
        slot_gate[pl.ds(512 + group * 64, 64), :] = gate[64:]
        head, left, right = (dot(place.astype(BF16), s, 1, 0) for s in spreads)
        here = one_if(mine, F32)
        for i, (t, m) in enumerate(
            ((head, zx), (head, xz), (left, zx), (right, zx), (head, here), (left, here), (right, here))
        ):
            tables[i, group] = (t * m).astype(BF16)


def plane_rows(plane_of, group):
    return pl.ds(pl.multiple_of(plane_of[group] * 128, 128), 128)


def place_group(tables, group, heads, tail, out_ref, at):
    for lr in range(2):
        table = jnp.concatenate([tables[at[lr], group], tables[at[2 + lr], group]], axis=1)
        rows = dot(table, jnp.concatenate([heads[lr], tail], axis=0), 1, 0)
        rows = rows.astype(BF16)
        out_ref[lr, pl.ds(group * 64, 64), :] = rows[:64]
        out_ref[lr, pl.ds(512 + group * 64, 64), :] = rows[64:]


def grads_kernel(plane_of, tables, *refs):
    planes, down = refs[:6], refs[6:8]
    rows, hidden_grad, total = refs[8:]
    step = pl.program_id(0)

    @pl.when(step == 0)
    def _():
        total[...] = jnp.zeros_like(total)

    for group in range(8):
        at = plane_rows(plane_of, group)
        left, right, tail = (planes[2 * p + group // 4][at, :] for p in range(3))
        place_group(tables, group, (left, right), tail, rows, (4, 4, 5, 6))
    for e in range(2):
        at = pl.ds(e * 512, 512)
        total[at, :] += dot(rows[0, at, :], down[0][e], 1, 1) + dot(rows[1, at, :], down[1][e], 1, 1)

    @pl.when(step == pl.num_programs(0) - 1)
    def _():
        hidden_grad[...] = total[...]


def rows_kernel(*refs):
    tables, planes = refs[0], refs[1:25]
    gate, up = refs[25:27], refs[27:29]
    hidden_grad, slot_gate = refs[29:31]
    rows, hidden, gate_grad, up_grad, gate_total, up_total = refs[31:]
    step = pl.program_id(0)

    @pl.when(step == 0)
    def _():
        gate_total[...] = jnp.zeros_like(gate_total)
        up_total[...] = jnp.zeros_like(up_total)

    for group in range(8):
        half, g = divmod(group, 4)
        zs, xs, ys = (planes[p * 8 + half * 4 : p * 8 + half * 4 + 4] for p in range(3))
        pick = pl.ds(g * 32, 32)
        left = jnp.concatenate([ref[pick, :] for ref in zs], axis=0)
        right = jnp.concatenate([ref[pick, :] for ref in xs], axis=0)
        place_group(tables, group, (left, right), ys[g][...], rows, (0, 1, 2, 3))
    for e in range(2):
        at = pl.ds(e * 512, 512)
        left, right = rows[0, at, :], rows[1, at, :]
        gate_total[at, :] += dot(left, gate[0][e], 1, 1) + dot(right, gate[1][e], 1, 1)
        up_total[at, :] += dot(left, up[0][e], 1, 1) + dot(right, up[1][e], 1, 1)

    @pl.when(step == pl.num_programs(0) - 1)
    def _():
        for i in range(8):
            at = pl.ds(i * 128, 128)
            gate_act, up_act = gate_total[at, :], up_total[at, :]
            scale = slot_gate[at, :]
            back = hidden_grad[at, :] * scale
            s = 1.0 / (1.0 + jnp.exp(-gate_act))
            silu = gate_act * s
            hidden[at, :] = (silu * up_act * scale).astype(BF16)
            up_grad[at, :] = (back * silu).astype(BF16)
            gate_grad[at, :] = (back * up_act * s * (1.0 + gate_act * (1.0 - s))).astype(BF16)


def both_experts(slots, lr, group):
    return jnp.concatenate(
        [slots[lr, pl.ds(group * 64, 64), :], slots[lr, pl.ds(512 + group * 64, 64), :]], axis=0
    )


def back_kernel(tables, gate_grad, up_grad, *refs):
    gate, up, outs, slots = refs[:2], refs[2:4], refs[4:-1], refs[-1]
    for lr in range(2):
        for e in range(2):
            pick = pl.ds(e * 512, 512)
            value = dot(gate_grad[pick, :], gate[lr][e], 1, 0) + dot(up_grad[pick, :], up[lr][e], 1, 0)
            slots[lr, pick, :] = value.astype(BF16)
    for group in range(8):
        half, g = divmod(group, 4)
        out = outs[half * 4 : half * 4 + 4]
        left, right = (both_experts(slots, lr, group) for lr in range(2))
        head_left = dot(tables[0, group], left, 0, 0).astype(BF16)
        head_right = dot(tables[1, group], right, 0, 0).astype(BF16)
        tail = dot(tables[2, group], left, 0, 0) + dot(tables[3, group], right, 0, 0)
        for i in range(4):
            out[i][0, pl.ds(g * 32, 32), :] = head_left[i * 32 : (i + 1) * 32]
            out[i][1, pl.ds(g * 32, 32), :] = head_right[i * 32 : (i + 1) * 32]
        out[g][2] = tail.astype(BF16)


def out_kernel(steps, plane_of, tables, hidden, down, own, sib, slots):
    step = pl.program_id(0)
    outs = (own, sib)

    @pl.when(step < 2 * steps)
    def _():
        for e in range(2):
            pick = pl.ds(e * 512, 512)
            slots[step, pick, :] = dot(hidden[pick, :], down[e], 1, 0).astype(BF16)
        for group in range(8):
            value = dot(tables[4, group], both_experts(slots, step, group), 0, 0)
            outs[group // 4][plane_rows(plane_of, group), :] = value.astype(BF16)

    @pl.when(step >= 2 * steps)
    def _():
        for group in range(8):
            value = dot(tables[5, group], both_experts(slots, step - 2 * steps, group), 0, 0)
            value = value + dot(tables[6, group], both_experts(slots, step - steps, group), 0, 0)
            outs[group // 4][plane_rows(plane_of, group), :] = value.astype(BF16)


def weight_grads_kernel(terms, rows, *refs):
    for act, out in zip(refs[:terms], refs[terms:]):
        for e in range(2):
            at = pl.ds(e * 512, 512)
            out[e] = dot(act[at, :], rows[0, at, :], 0, 0).astype(BF16)


def whole(shape):
    return pl.BlockSpec(shape, lambda *_: (0,) * len(shape))


def params():
    return pltpu.CompilerParams(vmem_limit_bytes=VMEM_LIMIT)


def chunk_of(half):
    return min(512, half)


def flat_planes(planes):
    return [v for part in planes for half in part for v in half]


def weight_specs(weight, chunk, steps):
    shape = (weight.shape[0], weight.shape[1], chunk)
    return [
        pl.BlockSpec(shape, lambda n: (0, 0, n)),
        pl.BlockSpec(shape, lambda n, steps=steps: (0, 0, n + steps)),
    ]


def scalars():
    return pl.BlockSpec(memory_space=pltpu.SMEM)


def routing(plane_of, info, planes, width):
    return pl.pallas_call(
        routing_kernel,
        grid=(1,),
        in_specs=[scalars(), whole((8, 128))]
        + [pl.BlockSpec((512, 128), lambda n: (0, width // 128))] * 2,
        out_specs=[whole((7, 8, 128, 128)), whole((1024, 1))],
        out_shape=[
            jax.ShapeDtypeStruct((7, 8, 128, 128), BF16),
            jax.ShapeDtypeStruct((1024, 1), F32),
        ],
        compiler_params=params(),
        cost_estimate=pl.CostEstimate(flops=10**9, bytes_accessed=10**7, transcendentals=0),
    )(plane_of, info, *planes)


def dispatch_grads(plane_of, tables, planes, down):
    width, half = down.shape[1], down.shape[2] // 2
    chunk = chunk_of(half)
    steps = half // chunk
    specs = []
    for p in range(3):
        specs += [pl.BlockSpec((512, chunk), lambda n, p=p: (0, n + p * steps))] * 2
    return pl.pallas_call(
        grads_kernel,
        grid=(steps,),
        in_specs=[scalars(), whole(tables.shape)] + specs + weight_specs(down, chunk, steps),
        out_specs=[pl.BlockSpec((2, 1024, chunk), lambda n: (0, 0, n)), whole((1024, width))],
        out_shape=[
            jax.ShapeDtypeStruct((2, 1024, half), BF16),
            jax.ShapeDtypeStruct((1024, width), F32),
        ],
        scratch_shapes=[pltpu.VMEM((1024, width), F32)],
        compiler_params=params(),
        cost_estimate=pl.CostEstimate(flops=8 * 10**9, bytes_accessed=30 * 10**6, transcendentals=0),
    )(plane_of, tables, *(planes * 3), down, down)


def dispatch_rows(tables, planes, gate, up, hidden_grad, slot_gate):
    width, half = gate.shape[1], gate.shape[2] // 2
    chunk = chunk_of(half)
    steps = half // chunk
    small = jax.ShapeDtypeStruct((1024, width), BF16)
    return pl.pallas_call(
        rows_kernel,
        grid=(steps,),
        in_specs=[whole(tables.shape)]
        + [pl.BlockSpec((128, chunk), lambda n: (0, n))] * 24
        + weight_specs(gate, chunk, steps)
        + weight_specs(up, chunk, steps)
        + [whole((1024, width)), whole((1024, 1))],
        out_specs=[pl.BlockSpec((2, 1024, chunk), lambda n: (0, 0, n))] + [whole((1024, width))] * 3,
        out_shape=[jax.ShapeDtypeStruct((2, 1024, half), BF16), small, small, small],
        scratch_shapes=[pltpu.VMEM((1024, width), F32)] * 2,
        compiler_params=params(),
        cost_estimate=pl.CostEstimate(flops=10**10, bytes_accessed=30 * 10**6, transcendentals=0),
    )(tables, *flat_planes(planes), gate, gate, up, up, hidden_grad, slot_gate)


def combine_back(tables, gate_grad, up_grad, gate, up):
    width, half = gate.shape[1], gate.shape[2] // 2
    chunk = chunk_of(half)
    steps = half // chunk
    out = jax.ShapeDtypeStruct((3, 128, half), BF16)
    outs = pl.pallas_call(
        back_kernel,
        grid=(steps,),
        in_specs=[whole(tables.shape)]
        + [whole((1024, width))] * 2
        + weight_specs(gate, chunk, steps)
        + weight_specs(up, chunk, steps),
        out_specs=[pl.BlockSpec((3, 128, chunk), lambda n: (0, 0, n))] * 8,
        out_shape=[out] * 8,
        scratch_shapes=[pltpu.VMEM((2, 1024, chunk), BF16)],
        compiler_params=params(),
        cost_estimate=pl.CostEstimate(flops=8 * 10**9, bytes_accessed=30 * 10**6, transcendentals=0),
    )(tables, gate_grad, up_grad, gate, gate, up, up)
    return outs[:4], outs[4:]


def combine_out(plane_of, tables, hidden, down):
    width, half = down.shape[1], down.shape[2] // 2
    chunk = chunk_of(half)
    steps = half // chunk
    out = jax.ShapeDtypeStruct((512, 3 * half), BF16)
    return pl.pallas_call(
        functools.partial(out_kernel, steps),
        grid=(3 * steps,),
        in_specs=[
            scalars(),
            whole(tables.shape),
            whole((1024, width)),
            pl.BlockSpec((2, width, chunk), lambda n: (0, 0, jnp.minimum(n, 2 * steps - 1))),
        ],
        out_specs=[pl.BlockSpec((512, chunk), lambda n: (0, n))] * 2,
        out_shape=[out] * 2,
        scratch_shapes=[pltpu.VMEM((2 * steps, 1024, chunk), BF16)],
        compiler_params=params(),
        cost_estimate=pl.CostEstimate(flops=6 * 10**9, bytes_accessed=30 * 10**6, transcendentals=0),
    )(plane_of, tables, hidden, down)


def weight_grads(rows, acts):
    width, half = acts[0].shape[1], rows.shape[2]
    chunk = chunk_of(half)
    steps = half // chunk
    terms = len(acts)
    return pl.pallas_call(
        functools.partial(weight_grads_kernel, terms),
        grid=(2, steps),
        in_specs=[pl.BlockSpec((1, 1024, chunk), lambda i, n: (i, 0, n))] + [whole((1024, width))] * terms,
        out_specs=[pl.BlockSpec((2, width, chunk), lambda i, n: (0, 0, i * steps + n))] * terms,
        out_shape=[jax.ShapeDtypeStruct((2, width, 2 * half), BF16)] * terms,
        compiler_params=params(),
        cost_estimate=pl.CostEstimate(flops=6 * 10**9, bytes_accessed=16 * 10**6, transcendentals=0),
    )(rows, *acts)


def context_kernel(picks, *refs):
    (own_l, own_r, own_t, sib_l, sib_r, sib_t), (left, right), (out, total) = refs[:6], refs[6:8], refs[8:]
    step = pl.program_id(0)

    @pl.when(step == 0)
    def _():
        total[...] = jnp.zeros_like(total)

    tail = jnp.concatenate([own_t[...], sib_t[...]], axis=0)
    for i, (own, sib, weight) in enumerate(((own_l, sib_l, left), (own_r, sib_r, right))):
        head = jnp.concatenate([own[...], sib[...]], axis=0)
        rows = dot(picks[0], head, 1, 0) + dot(picks[1 + i], tail, 1, 0)
        total[...] += dot(rows.astype(BF16), weight[...], 1, 1)

    @pl.when(step == pl.num_programs(0) - 1)
    def _():
        out[...] = total[...].astype(BF16)


def context_gradient(picks, own, sib, out_proj):
    features, half = out_proj.shape[0], out_proj.shape[1] // 2
    chunk = chunk_of(half)
    steps = half // chunk
    packed = [pl.BlockSpec((64, chunk), lambda n, p=p: (0, n + p * steps)) for p in range(3)]
    tokens = picks.shape[1]
    return pl.pallas_call(
        context_kernel,
        grid=(steps,),
        in_specs=[whole(picks.shape)]
        + packed * 2
        + [pl.BlockSpec((features, chunk), lambda n, p=p: (0, n + p * steps)) for p in range(2)],
        out_specs=whole((tokens, features)),
        out_shape=jax.ShapeDtypeStruct((tokens, features), BF16),
        scratch_shapes=[pltpu.VMEM((tokens, features), F32)],
        compiler_params=params(),
        cost_estimate=pl.CostEstimate(flops=10**9, bytes_accessed=6 * 10**6, transcendentals=0),
    )(picks, own, own, own, sib, sib, sib, out_proj, out_proj)


def on_device(
    context, out_proj, residual, norm_gain, gate_weight, up_weight, down_weight, expert_ids, gate_codes, cotangent
):
    width = residual.shape[1]
    half = width // 2
    x, zl, core = lax.axis_index("x"), lax.axis_index("zl"), lax.axis_index("core")
    tp = (x * 2 + zl) * 2 + core

    meta = jnp.concatenate(
        [
            jnp.pad(expert_ids.T.astype(BF16), ((0, 0), (0, 4))),
            jnp.pad(gate_codes.T.astype(BF16), ((0, 0), (0, 128 - 16 - TOK))),
        ],
        axis=1,
    )
    cot = pack(cotangent)
    cot_own = jnp.concatenate(around(jnp.concatenate(cot + [meta], axis=1), "z"), axis=0)

    order = np.arange(16)
    h, j, k = order // 8, (order // 2) % 4, order % 2
    sign = (1 - 2 * core) * jnp.asarray(1 - 2 * h)
    owner = (((x - j * sign) % 4) * 2 + (zl ^ jnp.asarray(k))) * 2 + (core ^ jnp.asarray(h))
    lane = np.arange(8)
    head_row = (owner[:, None] * TOK + lane[None, :]).reshape(128)
    tail_row = (owner[:, None] * TOK + 8 + (lane % 4)[None, :]).reshape(128)
    token = jnp.arange(16 * TOK)
    picked = (jnp.concatenate([head_row, tail_row])[:, None] == token[None, :]).astype(BF16)
    ordered = jnp.dot(picked, context, preferred_element_type=F32).astype(BF16)
    partial = jnp.dot(ordered, out_proj, preferred_element_type=F32).astype(BF16)
    cot_own = after(cot_own, partial)
    cot_own = lax.all_gather(cot_own, ("y", "x"), axis=0, tiled=True)
    first = jnp.asarray((np.arange(128) % 8 < 4)[:, None])
    tail = jnp.where(first, partial[128:, :half], partial[128:, half:])
    partial = jnp.concatenate([partial[:128], tail], axis=1).reshape(2, 8, 8, 3 * half)
    summed = (partial[0].astype(F32) + send(partial[1], SWAP).astype(F32)).astype(BF16)
    attended = summed[0].astype(F32)
    for j in range(4):
        for k in range(2):
            if j or k:
                attended = attended + send(summed[2 * j + k], tp_shifted(-j, k)).astype(F32)

    split = lambda v: [v[:, i * half : (i + 1) * half] for i in range(3)]
    stream = [r.astype(F32) + a for r, a in zip(pack(residual), split(attended))]
    inverse = [
        lax.rsqrt(s / width + EPSILON) for s in row_sums([s * s for s in stream])
    ]
    upper = jnp.asarray((np.arange(8) < 4)[:, None])
    gain = [
        norm_gain[None, :half],
        norm_gain[None, half:],
        jnp.where(upper, norm_gain[None, :half], norm_gain[None, half:]),
    ]
    inv = [inverse[0], inverse[0], inverse[1]]
    normed = [(s * i * g).astype(BF16) for s, i, g in zip(stream, inv, gain)]
    planes = [[gather_plane(part, order) for part, order in zip(normed, ORDERS)]]
    ring_step = lambda: planes.append([send(v, shifted(order[2], 1)) for v, order in zip(planes[-1], ORDERS)])
    ring_step()
    cot_own = after(cot_own, planes[1])
    ring_step()
    cot_planes = (cot_own, after(send(cot_own, SWAP), planes[2]))
    ring_step()

    y = lax.axis_index("y")
    block = np.arange(128) // 8
    turn = (1 - 2 * core) * jnp.asarray([[1], [-1]])
    steps_to = (block % 4) * 4 + ((x - block // 4) * turn) % 4
    info = jnp.concatenate([steps_to, jnp.full((6, 128), 2 * tp)], axis=0).astype(jnp.int32)
    plane_of = ((y - jnp.arange(4) * turn) % 4).reshape(8).astype(jnp.int32)
    tables, slot_gate = routing(plane_of, info, cot_planes, 3 * half)

    grad_rows, hidden_grad = dispatch_grads(plane_of, tables, cot_planes, down_weight)
    row_planes = []
    for p in range(3):
        own = [step[p] for step in planes]
        early = [after(v, cot_planes[1]) for v in own[:3]]
        row_planes.append((own, [send(v, SWAP) for v in early + own[3:]]))
    rows, hidden, gate_grad, up_grad = dispatch_rows(
        tables, row_planes, gate_weight, up_weight, hidden_grad, slot_gate
    )
    out_own, out_sib = combine_out(plane_of, tables, hidden, down_weight)
    back_own, back_sib = combine_back(tables, after(gate_grad, out_own), up_grad, gate_weight, up_weight)
    out_arrived = send(out_sib, SWAP)
    out_sum = add_float(out_own, out_arrived)
    weights = {}

    def down_beside(sums):
        weights["down"] = weight_grads(grad_rows, [after(hidden, sums)])
        return weights["down"]

    def up_beside(sums):
        weights["up"] = weight_grads(rows, [after(gate_grad, sums), up_grad])
        return weights["up"]

    beside = {1: lambda _: out_arrived, 2: lambda _: out_sum, 3: down_beside, 0: up_beside}
    back = scatter_parts(back_own, back_sib, beside)
    gate_out, up_out, down_out = *weights["up"], *weights["down"]
    mixture = scatter_whole(out_sum)

    scaled = [b * g for b, g in zip(back, gain)]
    inner = [s / width for s in row_sums([a * b for a, b in zip(scaled, stream)])]
    inner = [inner[0], inner[0], inner[1]]
    grad = [
        (c.astype(F32) + i * s - st * (i * i * i) * m).astype(BF16)
        for c, i, s, st, m in zip(cot, inv, scaled, stream, inner)
    ]
    residual_grad = unpack(grad)
    output = unpack([(s + m).astype(BF16) for s, m in zip(stream, mixture)])

    packed = jnp.concatenate(grad, axis=1)
    own = [packed if not (j or k) else send(packed, tp_shifted(j, k)) for j in range(4) for k in range(2)]
    own = jnp.concatenate(own, axis=0)
    is_head = token[:, None] == head_row[None, :]
    is_tail = token[:, None] == tail_row[None, :]
    upper_cols = jnp.asarray(np.arange(128) % 8 < 4)[None, :]
    picks = jnp.stack([is_head, is_tail & upper_cols, is_tail & ~upper_cols]).astype(BF16)
    context_grad = context_gradient(picks, own, send(own, SWAP), out_proj)
    return (output, residual_grad, context_grad, gate_out, up_out, down_out)


def solution(mesh):
    fine = Mesh(np.asarray(mesh.devices).reshape(2, 4, 4, 2, 2), AXES)
    ctx, tp = AXES[:2], AXES[2:]
    rows = P(AXES, None)
    experts = P(tp, ctx, None)
    return jax.shard_map(
        on_device,
        mesh=fine,
        in_specs=(P(ctx, tp), P(tp, None), rows, P(), experts, experts, experts, rows, rows, rows),
        out_specs=(rows, rows, P(ctx, tp), experts, experts, experts),
        check_vma=False,
    )
```

```python
import functools

import numpy as np
import jax
import jax.numpy as jnp
from jax import lax
from jax.experimental import pallas as pl
from jax.experimental.pallas import tpu as pltpu
from jax.sharding import Mesh, PartitionSpec as P

AXES = ("zh", "y", "x", "zl", "core")
CAP = 4
TOK = 12
EPSILON = 1e-06
BF16 = jnp.bfloat16
F32 = jnp.float32
VMEM_LIMIT = 28 * 1024 * 1024


def flat_index(z, y, x, core):
    return ((((z // 2) * 4 + y) * 4 + x) * 2 + z % 2) * 2 + core


def permutation(move):
    return [
        (flat_index(z, y, x, c), flat_index(*move(z, y, x, c)))
        for z in range(4)
        for y in range(4)
        for x in range(4)
        for c in range(2)
    ]


def shifted(axis, steps):
    def move(z, y, x, c):
        d = steps * (1 - 2 * c)
        if axis == "x":
            return z, y, (x + d) % 4, c
        if axis == "y":
            return z, (y + d) % 4, x, c
        return (z + d) % 4, y, x, c

    return permutation(move)


def tp_shifted(steps, flip):
    return permutation(lambda z, y, x, c: (z ^ flip, y, (x + steps * (1 - 2 * c)) % 4, c))


SWAP = permutation(lambda z, y, x, c: (z, y, x, 1 - c))
ORDERS = (("x", "y", "z"), ("y", "z", "x"), ("z", "x", "y"))


def send(v, pairs):
    return lax.ppermute(v, AXES, pairs)


def after(v, first):
    return lax.optimization_barrier((v, first))[0]


def around(v, axis):
    up = send(v, shifted(axis, 1))
    down = send(v, shifted(axis, -1))
    return [v, up, send(up, shifted(axis, 1)), down]


def around_sum(blocks, axis):
    chain = (blocks[3].astype(F32) + send(blocks[2], shifted(axis, 1)).astype(F32)).astype(BF16)
    direct = send(blocks[1], shifted(axis, -1)).astype(F32)
    return blocks[0].astype(F32) + direct + send(chain, shifted(axis, 1)).astype(F32)


def gather_plane(part, order):
    a, b, c = order
    width = part.shape[-1]
    one = jnp.stack(around(part, a))
    two = jnp.stack(around(one, b), axis=0 if a == "x" else 1)
    return two.reshape(128, width)


def scatter_parts(own, sib, beside):
    width = own[0].shape[-1]
    arrived = {j: send(sib[j], SWAP) for j in (1, 2, 3, 0)}
    t = [None] * 3
    for j in (1, 2, 3, 0):
        other = beside[j](t) if j in beside else None
        for p, order in enumerate(ORDERS):
            v = own[j][p].astype(F32) + arrived[j][p].astype(F32)
            if t[p] is not None:
                v = v + send(t[p], shifted(order[2], 1)).astype(F32)
            t[p] = v.astype(BF16)
        if other is not None:
            t = after(t, other)
    sums = []
    for v, (a, b, _) in zip(t, ORDERS):
        at = 0 if a == "x" else 1
        v = v.reshape(4, 4, 8, width)
        v = around_sum([lax.index_in_dim(v, d, at, False) for d in range(4)], b).astype(BF16)
        sums.append(around_sum([v[d] for d in range(4)], a))
    return sums


def add_float(a, b):
    return (a.astype(F32) + b.astype(F32)).astype(BF16)


def scatter_whole(t):
    t = lax.psum_scatter(t, ("y", "x"), scatter_dimension=0, tiled=True)
    t = around_sum([t[8 * d : 8 * d + 8] for d in range(4)], "z")
    width = t.shape[1] // 3
    return [t[:, i * width : (i + 1) * width] for i in range(3)]


def pack(rows):
    half = rows.shape[1] // 2
    tail = rows[8:]
    return [rows[:8, :half], rows[:8, half:], jnp.concatenate([tail[:, :half], tail[:, half:]], axis=0)]


def unpack(parts):
    left, right, tail = parts
    return jnp.concatenate(
        [
            jnp.concatenate([left, right], axis=1),
            jnp.concatenate([tail[:4], tail[4:]], axis=1),
        ],
        axis=0,
    )


def row_sums(products):
    head = jnp.sum(products[0], axis=1, keepdims=True) + jnp.sum(products[1], axis=1, keepdims=True)
    tail = jnp.sum(products[2], axis=1, keepdims=True)
    return head, tail + jnp.concatenate([tail[4:], tail[:4]], axis=0)


def dot(a, b, ca, cb):
    return lax.dot_general(a, b, (((ca,), (cb,)), ((), ())), preferred_element_type=F32)


def iota(axis):
    return lax.broadcasted_iota(jnp.int32, (128, 128), axis)


def one_if(condition, dtype=BF16):
    return jnp.where(condition, 1.0, 0.0).astype(dtype)


def routing_kernel(plane_of, info, *refs):
    planes, (tables, slot_gate) = refs[:2], refs[2:]
    slot, col = iota(0), iota(1)
    slot_block = (slot & 63) >> 2
    rank_of = (slot & 3).astype(F32)
    expert = ((slot >> 6) + info[2:3, :]).astype(F32)
    lane, sub = col, col & 7
    before = one_if(slot < col)
    is_token = lane < TOK
    spreads = [
        one_if(slot == sub),
        one_if((sub < 4) & (slot == sub + 8)),
        one_if((sub >= 4) & (slot == sub + 4)),
    ]
    block = col >> 3
    zx = one_if(block == slot_block, F32)
    xz = one_if((((block & 3) << 2) + (block >> 2)) == slot_block, F32)
    for group in range(8):
        half, g = divmod(group, 4)
        mine = info[half : half + 1, :] == slot_block
        meta = planes[half][plane_rows(plane_of, group), :]
        has = code = total = jnp.zeros((128, 128), F32)
        for k in range(8):
            value = dot(one_if(mine & (sub == k)), meta, 1, 0)
            codes = pltpu.roll(value, 128 - 16, 1)
            hit = one_if((value == expert) & is_token, F32)
            has = has + hit
            code = code + hit * codes
            total = total + codes
        rank = dot(has.astype(BF16), before, 1, 0)
        place = jnp.where(rank == rank_of, has, 0.0)
        number = jnp.sum(place * code, axis=1, keepdims=True)
        over = jnp.sum(place * total, axis=1, keepdims=True)
        gate = jnp.where(over > 0.0, number / jnp.maximum(over, 1.0), 0.0)
        slot_gate[pl.ds(group * 64, 64), :] = gate[:64]
        slot_gate[pl.ds(512 + group * 64, 64), :] = gate[64:]
        head, left, right = (dot(place.astype(BF16), s, 1, 0) for s in spreads)
        here = one_if(mine, F32)
        for i, (t, m) in enumerate(
            ((head, zx), (head, xz), (left, zx), (right, zx), (head, here), (left, here), (right, here))
        ):
            tables[i, group] = (t * m).astype(BF16)


def plane_rows(plane_of, group):
    return pl.ds(pl.multiple_of(plane_of[group] * 128, 128), 128)


def place_group(tables, group, heads, tail, out_ref, at):
    for lr in range(2):
        table = jnp.concatenate([tables[at[lr], group], tables[at[2 + lr], group]], axis=1)
        rows = dot(table, jnp.concatenate([heads[lr], tail], axis=0), 1, 0)
        rows = rows.astype(BF16)
        out_ref[lr, pl.ds(group * 64, 64), :] = rows[:64]
        out_ref[lr, pl.ds(512 + group * 64, 64), :] = rows[64:]


def grads_kernel(plane_of, tables, *refs):
    planes, down = refs[:6], refs[6:8]
    rows, hidden_grad, total = refs[8:]
    step = pl.program_id(0)

    @pl.when(step == 0)
    def _():
        total[...] = jnp.zeros_like(total)

    for group in range(8):
        at = plane_rows(plane_of, group)
        left, right, tail = (planes[2 * p + group // 4][at, :] for p in range(3))
        place_group(tables, group, (left, right), tail, rows, (4, 4, 5, 6))
    for e in range(2):
        at = pl.ds(e * 512, 512)
        total[at, :] += dot(rows[0, at, :], down[0][e], 1, 1) + dot(rows[1, at, :], down[1][e], 1, 1)

    @pl.when(step == pl.num_programs(0) - 1)
    def _():
        hidden_grad[...] = total[...]


def rows_kernel(*refs):
    tables, planes = refs[0], refs[1:25]
    gate, up = refs[25:27], refs[27:29]
    hidden_grad, slot_gate = refs[29:31]
    rows, hidden, gate_grad, up_grad, gate_total, up_total = refs[31:]
    step = pl.program_id(0)

    @pl.when(step == 0)
    def _():
        gate_total[...] = jnp.zeros_like(gate_total)
        up_total[...] = jnp.zeros_like(up_total)

    for group in range(8):
        half, g = divmod(group, 4)
        zs, xs, ys = (planes[p * 8 + half * 4 : p * 8 + half * 4 + 4] for p in range(3))
        pick = pl.ds(g * 32, 32)
        left = jnp.concatenate([ref[pick, :] for ref in zs], axis=0)
        right = jnp.concatenate([ref[pick, :] for ref in xs], axis=0)
        place_group(tables, group, (left, right), ys[g][...], rows, (0, 1, 2, 3))
    for e in range(2):
        at = pl.ds(e * 512, 512)
        left, right = rows[0, at, :], rows[1, at, :]
        gate_total[at, :] += dot(left, gate[0][e], 1, 1) + dot(right, gate[1][e], 1, 1)
        up_total[at, :] += dot(left, up[0][e], 1, 1) + dot(right, up[1][e], 1, 1)

    @pl.when(step == pl.num_programs(0) - 1)
    def _():
        for i in range(8):
            at = pl.ds(i * 128, 128)
            gate_act, up_act = gate_total[at, :], up_total[at, :]
            scale = slot_gate[at, :]
            back = hidden_grad[at, :] * scale
            s = 1.0 / (1.0 + jnp.exp(-gate_act))
            silu = gate_act * s
            hidden[at, :] = (silu * up_act * scale).astype(BF16)
            up_grad[at, :] = (back * silu).astype(BF16)
            gate_grad[at, :] = (back * up_act * s * (1.0 + gate_act * (1.0 - s))).astype(BF16)


def both_experts(slots, lr, group):
    return jnp.concatenate(
        [slots[lr, pl.ds(group * 64, 64), :], slots[lr, pl.ds(512 + group * 64, 64), :]], axis=0
    )


def back_kernel(tables, gate_grad, up_grad, *refs):
    gate, up, outs, slots = refs[:2], refs[2:4], refs[4:-1], refs[-1]
    for lr in range(2):
        for e in range(2):
            pick = pl.ds(e * 512, 512)
            value = dot(gate_grad[pick, :], gate[lr][e], 1, 0) + dot(up_grad[pick, :], up[lr][e], 1, 0)
            slots[lr, pick, :] = value.astype(BF16)
    for group in range(8):
        half, g = divmod(group, 4)
        out = outs[half * 4 : half * 4 + 4]
        left, right = (both_experts(slots, lr, group) for lr in range(2))
        head_left = dot(tables[0, group], left, 0, 0).astype(BF16)
        head_right = dot(tables[1, group], right, 0, 0).astype(BF16)
        tail = dot(tables[2, group], left, 0, 0) + dot(tables[3, group], right, 0, 0)
        for i in range(4):
            out[i][0, pl.ds(g * 32, 32), :] = head_left[i * 32 : (i + 1) * 32]
            out[i][1, pl.ds(g * 32, 32), :] = head_right[i * 32 : (i + 1) * 32]
        out[g][2] = tail.astype(BF16)


def out_kernel(steps, plane_of, tables, hidden, down, own, sib, slots):
    step = pl.program_id(0)
    outs = (own, sib)

    @pl.when(step < 2 * steps)
    def _():
        for e in range(2):
            pick = pl.ds(e * 512, 512)
            slots[step, pick, :] = dot(hidden[pick, :], down[e], 1, 0).astype(BF16)
        for group in range(8):
            value = dot(tables[4, group], both_experts(slots, step, group), 0, 0)
            outs[group // 4][plane_rows(plane_of, group), :] = value.astype(BF16)

    @pl.when(step >= 2 * steps)
    def _():
        for group in range(8):
            value = dot(tables[5, group], both_experts(slots, step - 2 * steps, group), 0, 0)
            value = value + dot(tables[6, group], both_experts(slots, step - steps, group), 0, 0)
            outs[group // 4][plane_rows(plane_of, group), :] = value.astype(BF16)


def weight_grads_kernel(terms, rows, *refs):
    for act, out in zip(refs[:terms], refs[terms:]):
        for e in range(2):
            at = pl.ds(e * 512, 512)
            out[e] = dot(act[at, :], rows[0, at, :], 0, 0).astype(BF16)


def whole(shape):
    return pl.BlockSpec(shape, lambda *_: (0,) * len(shape))


def params():
    return pltpu.CompilerParams(vmem_limit_bytes=VMEM_LIMIT)


def chunk_of(half, most=512):
    return min(most, half)


def flat_planes(planes):
    return [v for part in planes for half in part for v in half]


def weight_specs(weight, chunk, steps):
    shape = (weight.shape[0], weight.shape[1], chunk)
    return [
        pl.BlockSpec(shape, lambda n: (0, 0, n)),
        pl.BlockSpec(shape, lambda n, steps=steps: (0, 0, n + steps)),
    ]


def scalars():
    return pl.BlockSpec(memory_space=pltpu.SMEM)


def routing(plane_of, info, planes, width):
    return pl.pallas_call(
        routing_kernel,
        grid=(1,),
        in_specs=[scalars(), whole((8, 128))]
        + [pl.BlockSpec((512, 128), lambda n: (0, width // 128))] * 2,
        out_specs=[whole((7, 8, 128, 128)), whole((1024, 1))],
        out_shape=[
            jax.ShapeDtypeStruct((7, 8, 128, 128), BF16),
            jax.ShapeDtypeStruct((1024, 1), F32),
        ],
        compiler_params=params(),
        cost_estimate=pl.CostEstimate(flops=10**9, bytes_accessed=10**7, transcendentals=0),
    )(plane_of, info, *planes)


def dispatch_grads(plane_of, tables, planes, down):
    width, half = down.shape[1], down.shape[2] // 2
    chunk = chunk_of(half)
    steps = half // chunk
    specs = []
    for p in range(3):
        specs += [pl.BlockSpec((512, chunk), lambda n, p=p: (0, n + p * steps))] * 2
    return pl.pallas_call(
        grads_kernel,
        grid=(steps,),
        in_specs=[scalars(), whole(tables.shape)] + specs + weight_specs(down, chunk, steps),
        out_specs=[pl.BlockSpec((2, 1024, chunk), lambda n: (0, 0, n)), whole((1024, width))],
        out_shape=[
            jax.ShapeDtypeStruct((2, 1024, half), BF16),
            jax.ShapeDtypeStruct((1024, width), F32),
        ],
        scratch_shapes=[pltpu.VMEM((1024, width), F32)],
        compiler_params=params(),
        cost_estimate=pl.CostEstimate(flops=8 * 10**9, bytes_accessed=30 * 10**6, transcendentals=0),
    )(plane_of, tables, *(planes * 3), down, down)


def dispatch_rows(tables, planes, gate, up, hidden_grad, slot_gate):
    width, half = gate.shape[1], gate.shape[2] // 2
    chunk = chunk_of(half)
    steps = half // chunk
    small = jax.ShapeDtypeStruct((1024, width), BF16)
    return pl.pallas_call(
        rows_kernel,
        grid=(steps,),
        in_specs=[whole(tables.shape)]
        + [pl.BlockSpec((128, chunk), lambda n: (0, n))] * 24
        + weight_specs(gate, chunk, steps)
        + weight_specs(up, chunk, steps)
        + [whole((1024, width)), whole((1024, 1))],
        out_specs=[pl.BlockSpec((2, 1024, chunk), lambda n: (0, 0, n))] + [whole((1024, width))] * 3,
        out_shape=[jax.ShapeDtypeStruct((2, 1024, half), BF16), small, small, small],
        scratch_shapes=[pltpu.VMEM((1024, width), F32)] * 2,
        compiler_params=params(),
        cost_estimate=pl.CostEstimate(flops=10**10, bytes_accessed=30 * 10**6, transcendentals=0),
    )(tables, *flat_planes(planes), gate, gate, up, up, hidden_grad, slot_gate)


def combine_back(tables, gate_grad, up_grad, gate, up):
    width, half = gate.shape[1], gate.shape[2] // 2
    chunk = chunk_of(half)
    steps = half // chunk
    out = jax.ShapeDtypeStruct((3, 128, half), BF16)
    outs = pl.pallas_call(
        back_kernel,
        grid=(steps,),
        in_specs=[whole(tables.shape)]
        + [whole((1024, width))] * 2
        + weight_specs(gate, chunk, steps)
        + weight_specs(up, chunk, steps),
        out_specs=[pl.BlockSpec((3, 128, chunk), lambda n: (0, 0, n))] * 8,
        out_shape=[out] * 8,
        scratch_shapes=[pltpu.VMEM((2, 1024, chunk), BF16)],
        compiler_params=params(),
        cost_estimate=pl.CostEstimate(flops=8 * 10**9, bytes_accessed=30 * 10**6, transcendentals=0),
    )(tables, gate_grad, up_grad, gate, gate, up, up)
    return outs[:4], outs[4:]


def combine_out(plane_of, tables, hidden, down):
    width, half = down.shape[1], down.shape[2] // 2
    chunk = chunk_of(half, 1024)
    steps = half // chunk
    out = jax.ShapeDtypeStruct((512, 3 * half), BF16)
    return pl.pallas_call(
        functools.partial(out_kernel, steps),
        grid=(3 * steps,),
        in_specs=[
            scalars(),
            whole(tables.shape),
            whole((1024, width)),
            pl.BlockSpec((2, width, chunk), lambda n: (0, 0, jnp.minimum(n, 2 * steps - 1))),
        ],
        out_specs=[pl.BlockSpec((512, chunk), lambda n: (0, n))] * 2,
        out_shape=[out] * 2,
        scratch_shapes=[pltpu.VMEM((2 * steps, 1024, chunk), BF16)],
        compiler_params=params(),
        cost_estimate=pl.CostEstimate(flops=6 * 10**9, bytes_accessed=30 * 10**6, transcendentals=0),
    )(plane_of, tables, hidden, down)


def weight_grads(rows, acts):
    width, half = acts[0].shape[1], rows.shape[2]
    chunk = chunk_of(half, 1024)
    steps = half // chunk
    terms = len(acts)
    return pl.pallas_call(
        functools.partial(weight_grads_kernel, terms),
        grid=(2, steps),
        in_specs=[pl.BlockSpec((1, 1024, chunk), lambda i, n: (i, 0, n))] + [whole((1024, width))] * terms,
        out_specs=[pl.BlockSpec((2, width, chunk), lambda i, n: (0, 0, i * steps + n))] * terms,
        out_shape=[jax.ShapeDtypeStruct((2, width, 2 * half), BF16)] * terms,
        compiler_params=params(),
        cost_estimate=pl.CostEstimate(flops=6 * 10**9, bytes_accessed=16 * 10**6, transcendentals=0),
    )(rows, *acts)


def context_kernel(picks, *refs):
    (own_l, own_r, own_t, sib_l, sib_r, sib_t), (left, right), (out, total) = refs[:6], refs[6:8], refs[8:]
    step = pl.program_id(0)

    @pl.when(step == 0)
    def _():
        total[...] = jnp.zeros_like(total)

    tail = jnp.concatenate([own_t[...], sib_t[...]], axis=0)
    for i, (own, sib, weight) in enumerate(((own_l, sib_l, left), (own_r, sib_r, right))):
        head = jnp.concatenate([own[...], sib[...]], axis=0)
        rows = dot(picks[0], head, 1, 0) + dot(picks[1 + i], tail, 1, 0)
        total[...] += dot(rows.astype(BF16), weight[...], 1, 1)

    @pl.when(step == pl.num_programs(0) - 1)
    def _():
        out[...] = total[...].astype(BF16)


def context_gradient(picks, own, sib, out_proj):
    features, half = out_proj.shape[0], out_proj.shape[1] // 2
    chunk = chunk_of(half)
    steps = half // chunk
    packed = [pl.BlockSpec((64, chunk), lambda n, p=p: (0, n + p * steps)) for p in range(3)]
    tokens = picks.shape[1]
    return pl.pallas_call(
        context_kernel,
        grid=(steps,),
        in_specs=[whole(picks.shape)]
        + packed * 2
        + [pl.BlockSpec((features, chunk), lambda n, p=p: (0, n + p * steps)) for p in range(2)],
        out_specs=whole((tokens, features)),
        out_shape=jax.ShapeDtypeStruct((tokens, features), BF16),
        scratch_shapes=[pltpu.VMEM((tokens, features), F32)],
        compiler_params=params(),
        cost_estimate=pl.CostEstimate(flops=10**9, bytes_accessed=6 * 10**6, transcendentals=0),
    )(picks, own, own, own, sib, sib, sib, out_proj, out_proj)


def on_device(
    context, out_proj, residual, norm_gain, gate_weight, up_weight, down_weight, expert_ids, gate_codes, cotangent
):
    width = residual.shape[1]
    half = width // 2
    x, zl, core = lax.axis_index("x"), lax.axis_index("zl"), lax.axis_index("core")
    tp = (x * 2 + zl) * 2 + core

    meta = jnp.concatenate(
        [
            jnp.pad(expert_ids.T.astype(BF16), ((0, 0), (0, 4))),
            jnp.pad(gate_codes.T.astype(BF16), ((0, 0), (0, 128 - 16 - TOK))),
        ],
        axis=1,
    )
    cot = pack(cotangent)
    cot_own = jnp.concatenate(around(jnp.concatenate(cot + [meta], axis=1), "z"), axis=0)

    order = np.arange(16)
    h, j, k = order // 8, (order // 2) % 4, order % 2
    sign = (1 - 2 * core) * jnp.asarray(1 - 2 * h)
    owner = (((x - j * sign) % 4) * 2 + (zl ^ jnp.asarray(k))) * 2 + (core ^ jnp.asarray(h))
    lane = np.arange(8)
    head_row = (owner[:, None] * TOK + lane[None, :]).reshape(128)
    tail_row = (owner[:, None] * TOK + 8 + (lane % 4)[None, :]).reshape(128)
    token = jnp.arange(16 * TOK)
    picked = (jnp.concatenate([head_row, tail_row])[:, None] == token[None, :]).astype(BF16)
    ordered = jnp.dot(picked, context, preferred_element_type=F32).astype(BF16)
    partial = jnp.dot(ordered, out_proj, preferred_element_type=F32).astype(BF16)
    cot_own = after(cot_own, partial)
    cot_own = lax.all_gather(cot_own, ("y", "x"), axis=0, tiled=True)
    first = jnp.asarray((np.arange(128) % 8 < 4)[:, None])
    tail = jnp.where(first, partial[128:, :half], partial[128:, half:])
    partial = jnp.concatenate([partial[:128], tail], axis=1).reshape(2, 8, 8, 3 * half)
    summed = (partial[0].astype(F32) + send(partial[1], SWAP).astype(F32)).astype(BF16)
    attended = summed[0].astype(F32)
    for j in range(4):
        for k in range(2):
            if j or k:
                attended = attended + send(summed[2 * j + k], tp_shifted(-j, k)).astype(F32)

    split = lambda v: [v[:, i * half : (i + 1) * half] for i in range(3)]
    stream = [r.astype(F32) + a for r, a in zip(pack(residual), split(attended))]
    inverse = [
        lax.rsqrt(s / width + EPSILON) for s in row_sums([s * s for s in stream])
    ]
    upper = jnp.asarray((np.arange(8) < 4)[:, None])
    gain = [
        norm_gain[None, :half],
        norm_gain[None, half:],
        jnp.where(upper, norm_gain[None, :half], norm_gain[None, half:]),
    ]
    inv = [inverse[0], inverse[0], inverse[1]]
    normed = [(s * i * g).astype(BF16) for s, i, g in zip(stream, inv, gain)]
    planes = [[gather_plane(part, order) for part, order in zip(normed, ORDERS)]]
    ring_step = lambda: planes.append([send(v, shifted(order[2], 1)) for v, order in zip(planes[-1], ORDERS)])
    ring_step()
    cot_own = after(cot_own, planes[1])
    ring_step()
    cot_planes = (cot_own, after(send(cot_own, SWAP), planes[2]))
    ring_step()

    y = lax.axis_index("y")
    block = np.arange(128) // 8
    turn = (1 - 2 * core) * jnp.asarray([[1], [-1]])
    steps_to = (block % 4) * 4 + ((x - block // 4) * turn) % 4
    info = jnp.concatenate([steps_to, jnp.full((6, 128), 2 * tp)], axis=0).astype(jnp.int32)
    plane_of = ((y - jnp.arange(4) * turn) % 4).reshape(8).astype(jnp.int32)
    tables, slot_gate = routing(plane_of, info, cot_planes, 3 * half)

    grad_rows, hidden_grad = dispatch_grads(plane_of, tables, cot_planes, down_weight)
    row_planes = []
    for p in range(3):
        own = [step[p] for step in planes]
        early = [after(v, cot_planes[1]) for v in own[:3]]
        row_planes.append((own, [send(v, SWAP) for v in early + own[3:]]))
    rows, hidden, gate_grad, up_grad = dispatch_rows(
        tables, row_planes, gate_weight, up_weight, hidden_grad, slot_gate
    )
    out_own, out_sib = combine_out(plane_of, tables, hidden, down_weight)
    back_own, back_sib = combine_back(tables, after(gate_grad, out_own), up_grad, gate_weight, up_weight)
    out_arrived = send(out_sib, SWAP)
    out_sum = add_float(out_own, out_arrived)
    weights = {}

    def down_beside(sums):
        weights["down"] = weight_grads(grad_rows, [after(hidden, sums)])
        return weights["down"]

    def up_beside(sums):
        weights["up"] = weight_grads(rows, [after(gate_grad, sums), up_grad])
        return weights["up"]

    beside = {1: lambda _: out_arrived, 2: lambda _: out_sum, 3: down_beside, 0: up_beside}
    back = scatter_parts(back_own, back_sib, beside)
    gate_out, up_out, down_out = *weights["up"], *weights["down"]
    mixture = scatter_whole(out_sum)

    scaled = [b * g for b, g in zip(back, gain)]
    inner = [s / width for s in row_sums([a * b for a, b in zip(scaled, stream)])]
    inner = [inner[0], inner[0], inner[1]]
    grad = [
        (c.astype(F32) + i * s - st * (i * i * i) * m).astype(BF16)
        for c, i, s, st, m in zip(cot, inv, scaled, stream, inner)
    ]
    residual_grad = unpack(grad)
    output = unpack([(s + m).astype(BF16) for s, m in zip(stream, mixture)])

    packed = jnp.concatenate(grad, axis=1)
    own = [packed if not (j or k) else send(packed, tp_shifted(j, k)) for j in range(4) for k in range(2)]
    own = jnp.concatenate(own, axis=0)
    is_head = token[:, None] == head_row[None, :]
    is_tail = token[:, None] == tail_row[None, :]
    upper_cols = jnp.asarray(np.arange(128) % 8 < 4)[None, :]
    picks = jnp.stack([is_head, is_tail & upper_cols, is_tail & ~upper_cols]).astype(BF16)
    context_grad = context_gradient(picks, own, send(own, SWAP), out_proj)
    return (output, residual_grad, context_grad, gate_out, up_out, down_out)


def solution(mesh):
    fine = Mesh(np.asarray(mesh.devices).reshape(2, 4, 4, 2, 2), AXES)
    ctx, tp = AXES[:2], AXES[2:]
    rows = P(AXES, None)
    experts = P(tp, ctx, None)
    return jax.shard_map(
        on_device,
        mesh=fine,
        in_specs=(P(ctx, tp), P(tp, None), rows, P(), experts, experts, experts, rows, rows, rows),
        out_specs=(rows, rows, P(ctx, tp), experts, experts, experts),
        check_vma=False,
    )
```
